256 devices in a mesh: expert: 128 (over z, y, x), dp: 2 (over core).
Axes of the slice: x: 4, y: 4, z: 8, core: 2. Of those that a mesh axis runs over, the one named last changes fastest.
Arguments:
- tokens: bfloat16 [2, 16384, 2048], P('dp', 'expert'), may hold values from -6 to 6
- grad_out: bfloat16 [2, 16384, 2048], P('dp', 'expert'), may hold values from -3 to 3
- gates: bfloat16 [2, 128, 128, 3], P('dp', 'expert'), may hold values from 0.049804688 to 1
- slot_index: int32 [2, 128, 128, 3], P('dp', 'expert'), may hold values from 0 to 127, as said below
- slot_count: int32 [2, 128, 128], P('dp', 'expert'), may hold values from 1 to 3, as said below
- up_weight: bfloat16 [128, 2048, 768], P('expert', None, 'dp'), may hold values from -0.125 to 0.125
- down_weight: bfloat16 [128, 768, 2048], P('expert', 'dp'), may hold values from -0.21875 to 0.21875
Outputs:
- d_tokens: bfloat16 [2, 16384, 2048], P('dp', 'expert')
- d_gate: bfloat16 [2, 128, 128, 3], P('dp', 'expert')
- d_up: bfloat16 [128, 2048, 768], P('expert', None, 'dp')
- d_down: bfloat16 [128, 768, 2048], P('expert', 'dp')
The draws below stay inside these ranges and needn't reach their ends.
Inputs may be any that keep to these rules, and one draw needn't show every extreme that they name: `slot_index`: within each block the first slot_count entries are different rows; the other entries are rows too. `slot_count`: for each batch and expert the counts over all source devices sum to 256.
All inputs are finite; a program needn't handle non-finite values.
Results may differ from the reference program's by a relative error of at most 0.015.
Values may be sent and summed in bfloat16 or wider, within the bound.
A program may use at most 128 MiB of HBM per device.

```python
import jax
import jax.numpy as jnp
from jax import lax

D = 2048
FF_DEV = 768
TOK_DEV = 128
EXPERTS = 128
TOK_GROUP = 16384
SLOT = 3
N_DP = 2


def draw_slot_index(key, part):
    key = jax.random.fold_in(key, 11)
    scores = jax.random.randint(key, (N_DP, EXPERTS, EXPERTS, TOK_DEV), 0, 2 ** 20) * TOK_DEV + jnp.arange(TOK_DEV, dtype=jnp.int32)
    order = jnp.argsort(scores, axis=-1, stable=True)
    return order[..., :SLOT].astype(jnp.int32)


def draw_slot_count(key, part):
    key = jax.random.fold_in(key, 23)
    first_key, second_key = jax.random.split(key)
    scores = jax.random.randint(first_key, (N_DP, EXPERTS, EXPERTS), 0, 2 ** 20) * EXPERTS + jnp.arange(EXPERTS, dtype=jnp.int32)
    ranked = jnp.argsort(jnp.argsort(scores, axis=-1, stable=True), axis=-1, stable=True)
    third = SLOT // 3
    paired = jax.random.randint(second_key, (N_DP, EXPERTS, EXPERTS // 2), third, SLOT - third + 1)
    paired = paired.at[:, :, 0].set(SLOT)
    placed = jnp.stack([paired, 4 * third - paired], axis=-1).reshape(N_DP, EXPERTS, EXPERTS)
    counts = jnp.take_along_axis(placed, ranked, axis=-1)
    return jnp.transpose(counts, (0, 2, 1)).astype(jnp.int32)


def shard_levels(stream_key, extent, shards, smallest, largest):
    level = 1.0
    for axis_at, blocks in shards:
        heights = jax.random.uniform(jax.random.fold_in(jax.random.fold_in(stream_key, 6), axis_at), (blocks,), jnp.float32, smallest / len(shards), largest / len(shards))
        level = level * jnp.repeat(jnp.exp(heights), extent[axis_at] // blocks).reshape((-1,) + (1,) * (len(extent) - 1 - axis_at))
    return level


def scatter_about(stream_key, shape, width, bound, cuts=(), held_as=jnp.bfloat16):
    level = shard_levels(stream_key, shape, cuts, -0.22, 0.18) if cuts else 1.0
    values = jax.random.normal(stream_key, shape, jnp.float32) * width * level
    return jnp.minimum(jnp.maximum(values, -bound), bound).astype(held_as)


def setup_inputs(seed: int = 0) -> dict:
    key_of = jax.random.split(jax.random.key(seed), 8)
    tokens = scatter_about(key_of[0], (N_DP, TOK_GROUP, D), 1.0, 6.0, ((0, 2), (1, 128)))
    grad_out = scatter_about(key_of[1], (N_DP, TOK_GROUP, D), 0.5, 3.0, ((0, 2), (1, 128)))
    gates = jnp.clip(0.049804688 + 0.9501953 * jax.random.uniform(key_of[2], (N_DP, EXPERTS, EXPERTS, SLOT), jnp.float32) ** shard_levels(key_of[2], (N_DP, EXPERTS, EXPERTS, SLOT), ((0, 2), (1, 128)), -0.2, 0.2), 0.049804688, 1.0).astype(jnp.bfloat16)
    slot_index = draw_slot_index(jax.random.fold_in(key_of[7], 71), 0)
    slot_count = draw_slot_count(jax.random.fold_in(key_of[7], 71), 0)
    up_weight = scatter_about(key_of[5], (EXPERTS, D, FF_DEV), D ** -0.5, 0.125, ((0, 128), (2, 2)))
    down_weight = scatter_about(key_of[6], (EXPERTS, FF_DEV, D), FF_DEV ** -0.5, 0.21875, ((0, 128), (1, 2)))
    return {"tokens": tokens, "grad_out": grad_out, "gates": gates, "slot_index": slot_index, "slot_count": slot_count, "up_weight": up_weight, "down_weight": down_weight}


def expert_backward(rows_in, rows_grad, scale, live_mask, w_up, w_down):
    hidden = jnp.dot(rows_in, w_up, preferred_element_type=jnp.float32)
    sigmoid_h = jax.nn.sigmoid(hidden)
    activation = (hidden * sigmoid_h).astype(jnp.bfloat16)
    expert_out = jnp.dot(activation, w_down, preferred_element_type=jnp.float32)
    d_gate = live_mask * jnp.sum(rows_grad.astype(jnp.float32) * expert_out, axis=1)
    upstream = lax.dot_general(rows_grad, w_down, (((1,), (1,)), ((), ())), preferred_element_type=jnp.float32)
    d_hidden = (scale[:, None] * upstream * (sigmoid_h * (1.0 + hidden * (1.0 - sigmoid_h)))).astype(jnp.bfloat16)
    scaled = (scale[:, None] * activation.astype(jnp.float32)).astype(jnp.bfloat16)
    d_down = lax.dot_general(scaled, rows_grad, (((0,), (0,)), ((), ())), preferred_element_type=jnp.float32)
    d_up = lax.dot_general(rows_in, d_hidden, (((0,), (0,)), ((), ())), preferred_element_type=jnp.float32)
    d_rows = lax.dot_general(d_hidden, w_up, (((1,), (1,)), ((), ())), preferred_element_type=jnp.float32)
    return d_rows, d_gate, d_up, d_down


def reference(tokens, grad_out, gates, slot_index, slot_count, up_weight, down_weight):
    offsets = jnp.arange(EXPERTS, dtype=jnp.int32)[:, None] * TOK_DEV
    slot_ids = jnp.arange(SLOT, dtype=jnp.int32)

    def one_expert(carry, expert):
        picks = slot_index[:, :, expert, :] + offsets[None]
        live = (slot_ids[None, None, :] < slot_count[:, :, expert][..., None]).astype(jnp.float32)
        flat = picks.reshape(N_DP, -1)
        rows_in = jnp.concatenate([tokens[b][flat[b]] for b in range(N_DP)], axis=0)
        rows_grad = jnp.concatenate([grad_out[b][flat[b]] for b in range(N_DP)], axis=0)
        live_flat = live.reshape(-1)
        scale = gates[:, :, expert, :].astype(jnp.float32).reshape(-1) * live_flat
        d_rows, d_gate, d_up, d_down = expert_backward(rows_in, rows_grad, scale, live_flat, up_weight[expert], down_weight[expert])
        d_rows = d_rows.astype(jnp.bfloat16).astype(jnp.float32).reshape(N_DP, -1, D)
        for b in range(N_DP):
            carry = carry.at[b, flat[b]].add(d_rows[b])
        return carry, (d_gate.astype(jnp.bfloat16).reshape(N_DP, EXPERTS, SLOT), d_up.astype(jnp.bfloat16), d_down.astype(jnp.bfloat16))

    start = jnp.zeros((N_DP, TOK_GROUP, D), jnp.float32)
    summed, stacked = lax.scan(one_expert, start, jnp.arange(EXPERTS, dtype=jnp.int32))
    gate_grads, up_grads, down_grads = stacked
    return summed.astype(jnp.bfloat16), jnp.transpose(gate_grads, (1, 2, 0, 3)), up_grads, down_grads
```

```python
import jax
import jax.numpy as jnp
from jax import lax
from jax.experimental import pallas as pl
from jax.experimental.pallas import tpu as pltpu
from jax.sharding import PartitionSpec as P

MESH = pl.DeviceIdType.MESH
NX, NY, NZ = 4, 4, 8
N = NX * NY * NZ
LANES = 128
SUB = 16


def partner(me, step, sign):
    dz, dy, dx = step % NZ, (step // NZ) % NY, step // (NZ * NY)
    x, y, z = me % NX, (me // NX) % NY, me // (NX * NY)
    z = (z + sign * dz + NZ) % NZ
    y = (y + sign * dy + NY) % NY
    x = (x + sign * dx + NX) % NX
    return (z * NY + y) * NX + x


def enter(me):
    barrier = pltpu.get_barrier_semaphore()

    def greet(step, carry):
        pl.semaphore_signal(
            barrier,
            inc=1,
            device_id={"expert": lax.rem(me + step, N)},
            device_id_type=MESH,
        )
        return carry

    lax.fori_loop(1, N, greet, 0)
    pl.semaphore_wait(barrier, N - 1)


def forward_kernel(idx_ref, scale_ref, tok_ref, grad_ref, out_ref, send_ref, send_sem, recv_sem, own_sem):
    me = lax.axis_index("expert")
    enter(me)
    slots = send_ref.shape[1] // 2

    def fill(target):
        for k in range(slots):
            row = idx_ref[target * slots + k]
            send_ref[target, k] = tok_ref[row]
            scaled = grad_ref[row].astype(jnp.float32) * scale_ref[target * slots + k]
            send_ref[target, slots + k] = scaled.astype(jnp.bfloat16)

    fill(me)
    own = pltpu.make_async_copy(send_ref.at[me], out_ref.at[me], own_sem)
    own.start()

    def step(i, carry):
        target = partner(me, i, 1)
        fill(target)
        pltpu.make_async_remote_copy(
            src_ref=send_ref.at[target],
            dst_ref=out_ref.at[me],
            send_sem=send_sem,
            recv_sem=recv_sem,
            device_id={"expert": target},
            device_id_type=MESH,
        ).start()
        return carry

    lax.fori_loop(1, N, step, 0)
    rest = send_ref.at[pl.ds(0, N - 1)]
    pltpu.make_async_copy(rest, rest, recv_sem).wait()
    pltpu.make_async_copy(rest, rest, send_sem).wait()
    own.wait()


def return_kernel(rows_ref, gate_ref, out_ref, gout_ref, send_sem, recv_sem, gsend_sem, grecv_sem, own_sem):
    me = lax.axis_index("expert")
    enter(me)
    own = pltpu.make_async_copy(rows_ref.at[me], out_ref.at[me], own_sem.at[0])
    own.start()
    gown = pltpu.make_async_copy(gate_ref.at[me], gout_ref.at[me], own_sem.at[1])
    gown.start()

    def step(i, carry):
        target = partner(me, i, 1)
        pltpu.make_async_remote_copy(
            src_ref=rows_ref.at[target],
            dst_ref=out_ref.at[me],
            send_sem=send_sem,
            recv_sem=recv_sem,
            device_id={"expert": target},
            device_id_type=MESH,
        ).start()
        pltpu.make_async_remote_copy(
            src_ref=gate_ref.at[target],
            dst_ref=gout_ref.at[me],
            send_sem=gsend_sem,
            recv_sem=grecv_sem,
            device_id={"expert": target},
            device_id_type=MESH,
        ).start()
        return carry

    lax.fori_loop(1, N, step, 0)
    for ref, sems in ((rows_ref, (recv_sem, send_sem)), (gate_ref, (grecv_sem, gsend_sem))):
        rest = ref.at[pl.ds(0, N - 1)]
        for sem in sems:
            pltpu.make_async_copy(rest, rest, sem).wait()
    own.wait()
    gown.wait()


def per_device(tokens, grad_out, gates, slot_index, slot_count, up_weight, down_weight):
    experts, slots = slot_index.shape[2:]
    width = tokens.shape[2]
    total = experts * slots
    held = tokens.shape[1]
    flat = slot_index[0, 0].reshape(-1)
    live = lax.broadcasted_iota(jnp.int32, (experts, slots), 1) < slot_count[0, 0][:, None]
    live = live.astype(jnp.float32).reshape(total)
    scale = gates[0, 0].astype(jnp.float32).reshape(total) * live

    vmem = pl.BlockSpec(memory_space=pltpu.VMEM)
    smem = pl.BlockSpec(memory_space=pltpu.SMEM)
    block = (experts, 2 * slots, SUB, LANES)
    received = pl.pallas_call(
        forward_kernel,
        out_shape=jax.ShapeDtypeStruct(block, jnp.bfloat16),
        in_specs=[smem, smem, vmem, vmem],
        out_specs=vmem,
        scratch_shapes=[
            pltpu.VMEM(block, jnp.bfloat16),
            pltpu.SemaphoreType.DMA,
            pltpu.SemaphoreType.DMA,
            pltpu.SemaphoreType.DMA,
        ],
        compiler_params=pltpu.CompilerParams(
            collective_id=0, has_side_effects=True, vmem_limit_bytes=40 << 20
        ),
    )(
        flat,
        scale,
        tokens[0].reshape(held, SUB, LANES),
        grad_out[0].reshape(held, SUB, LANES),
    )
    rows_in = received[:, :slots].reshape(total, width)
    rows_grad = received[:, slots:].reshape(total, width)

    w_up = lax.all_gather(up_weight[0], "dp", axis=1, tiled=True)
    w_down = lax.all_gather(down_weight[0], "dp", axis=0, tiled=True)
    hidden = jnp.dot(rows_in, w_up, preferred_element_type=jnp.float32)
    gate_h = jax.nn.sigmoid(hidden)
    activation = (hidden * gate_h).astype(jnp.bfloat16)
    upstream = lax.dot_general(
        rows_grad, w_down, (((1,), (1,)), ((), ())), preferred_element_type=jnp.float32
    )
    d_hidden = (upstream * (gate_h * (1.0 + hidden * (1.0 - gate_h)))).astype(jnp.bfloat16)
    d_gate = jnp.sum(activation.astype(jnp.float32) * upstream, axis=1)
    d_rows = lax.dot_general(
        d_hidden, w_up, (((1,), (1,)), ((), ())), preferred_element_type=jnp.float32
    ).astype(jnp.bfloat16)
    d_down = lax.dot_general(
        activation, rows_grad, (((0,), (0,)), ((), ())), preferred_element_type=jnp.float32
    )
    d_up = lax.dot_general(
        rows_in, d_hidden, (((0,), (0,)), ((), ())), preferred_element_type=jnp.float32
    )
    d_up = lax.psum_scatter(d_up, "dp", scatter_dimension=1, tiled=True)
    d_down = lax.psum_scatter(d_down, "dp", scatter_dimension=0, tiled=True)

    gate_block = jnp.pad(d_gate.reshape(experts, 1, slots), ((0, 0), (0, 0), (0, LANES - slots)))
    back, gate_back = pl.pallas_call(
        return_kernel,
        out_shape=(
            jax.ShapeDtypeStruct((experts, slots, SUB, LANES), jnp.bfloat16),
            jax.ShapeDtypeStruct((experts, 1, LANES), jnp.float32),
        ),
        in_specs=[vmem, vmem],
        out_specs=(vmem, vmem),
        scratch_shapes=[pltpu.SemaphoreType.DMA] * 4 + [pltpu.SemaphoreType.DMA((2,))],
        compiler_params=pltpu.CompilerParams(
            collective_id=1, has_side_effects=True, vmem_limit_bytes=40 << 20
        ),
    )(d_rows.reshape(experts, slots, SUB, LANES), gate_block)

    spread = (flat[None, :] == jnp.arange(held, dtype=jnp.int32)[:, None]).astype(jnp.bfloat16)
    summed = jnp.dot(spread, back.reshape(total, width), preferred_element_type=jnp.float32)
    inverse = jnp.where(live > 0, 1.0 / jnp.where(live > 0, scale, 1.0), 0.0)
    d_gates = gate_back[:, 0, :slots] * inverse.reshape(experts, slots)
    return (
        summed.astype(jnp.bfloat16)[None],
        d_gates.astype(jnp.bfloat16)[None, None],
        d_up.astype(jnp.bfloat16)[None],
        d_down.astype(jnp.bfloat16)[None],
    )


def solution(mesh):
    in_specs = (
        P("dp", "expert", None),
        P("dp", "expert", None),
        P("dp", "expert", None, None),
        P("dp", "expert", None, None),
        P("dp", "expert", None),
        P("expert", None, "dp"),
        P("expert", "dp", None),
    )
    out_specs = (
        P("dp", "expert", None),
        P("dp", "expert", None, None),
        P("expert", None, "dp"),
        P("expert", "dp", None),
    )
    return jax.shard_map(
        per_device, mesh=mesh, in_specs=in_specs, out_specs=out_specs, check_vma=False
    )
```

```python
import jax
import jax.numpy as jnp
from jax import lax
from jax.experimental import pallas as pl
from jax.experimental.pallas import tpu as pltpu
from jax.sharding import PartitionSpec as P

MESH = pl.DeviceIdType.MESH
NX, NY, NZ = 4, 4, 8
N = NX * NY * NZ
CHUNKS = NX
PEERS = NY * NZ
LANES = 128
SUB = 16
WIDE = SUB * LANES


def place(me):
    return me % NX, (me // NX) % NY, me // (NX * NY)


def block_of(q, z, y):
    return q * PEERS + z * NY + y


def expert_of(q, z, y):
    return (z * NY + y) * NX + lax.rem(q - y + NX, NX)


def hop(i):
    return lax.rem(i, NZ), lax.div(i, NZ)


def bf16(v):
    return v.astype(jnp.bfloat16)


def dot(a, b, dims=((1,), (0,))):
    return lax.dot_general(a, b, (dims, ((), ())), preferred_element_type=jnp.float32)


def local_wait(ref, sem):
    pltpu.make_async_copy(ref, ref, sem).wait()


def kernel(
    idx_ref, scale_ref, pick_ref, tok_ref, grad_ref, up_ref, down_ref,
    dtok_ref, gback_ref, dup_ref, ddown_ref,
    send, recv, wu, wd, rows_x, rows_g, act, dhid, drow, dsend, back, gsend,
    up_out, up_in, down_out, down_in, total, perm,
    w_sem, f_send, f_recv, r_send, r_recv, g_send, g_recv, d_send, d_recv,
):
    me = lax.axis_index("expert")
    core = lax.axis_index("dp")
    x, y, z = place(me)
    q_me = lax.rem(x + y, NX)
    slots = send.shape[2]
    per_chunk = PEERS * slots
    half = up_ref.shape[1]
    mine = pl.ds(pl.multiple_of(core * half, LANES), half)
    theirs = pl.ds(pl.multiple_of((1 - core) * half, LANES), half)
    partner = {"dp": 1 - core}

    barrier = pltpu.get_barrier_semaphore()
    pl.semaphore_signal(barrier, inc=1, device_id=partner, device_id_type=MESH)

    def greet(step, carry):
        pl.semaphore_signal(
            barrier, inc=1, device_id={"expert": lax.rem(me + step, N)}, device_id_type=MESH
        )
        return carry

    lax.fori_loop(1, N, greet, 0)

    own_up = pltpu.make_async_copy(up_ref, wu.at[:, mine], w_sem.at[0])
    own_up.start()
    own_down = pltpu.make_async_copy(down_ref, wd.at[mine, :], w_sem.at[1])
    own_down.start()

    a = lax.broadcasted_iota(jnp.int32, (SUB * SUB, SUB * SUB), 0)
    b = lax.broadcasted_iota(jnp.int32, (SUB * SUB, SUB * SUB), 1)
    swap = (lax.rem(a, SUB) == lax.div(b, SUB)) & (lax.div(a, SUB) == lax.rem(b, SUB))
    perm[...] = jnp.where(swap, 1.0, 0.0).astype(jnp.bfloat16)

    def fill(target, carry):
        for k in range(slots):
            row = idx_ref[target * slots + k]
            send[target, 0, k] = tok_ref[row]
            scaled = grad_ref[row].astype(jnp.float32) * scale_ref[target * slots + k]
            send[target, 1, k] = bf16(scaled)
        return carry

    lax.fori_loop(0, N, fill, 0)
    pl.semaphore_wait(barrier, N)

    up_copy = pltpu.make_async_remote_copy(
        src_ref=up_ref, dst_ref=wu.at[:, mine], send_sem=w_sem.at[2], recv_sem=w_sem.at[3],
        device_id=partner, device_id_type=MESH,
    )
    up_copy.start()
    down_copy = pltpu.make_async_remote_copy(
        src_ref=down_ref, dst_ref=wd.at[mine, :], send_sem=w_sem.at[4], recv_sem=w_sem.at[5],
        device_id=partner, device_id_type=MESH,
    )
    down_copy.start()

    my_rows = pl.ds(block_of(q_me, z, y) * slots, slots)
    pltpu.make_async_copy(send.at[me], recv.at[:, my_rows], f_recv.at[0]).start()

    def push(n, carry):
        c = lax.div(n, PEERS)
        dz, dy = hop(lax.rem(n, PEERS))
        target = expert_of(lax.rem(q_me + c, NX), lax.rem(z + dz, NZ), lax.rem(y + dy, NY))
        pltpu.make_async_remote_copy(
            src_ref=send.at[target], dst_ref=recv.at[:, my_rows],
            send_sem=f_send, recv_sem=f_recv.at[c],
            device_id={"expert": target}, device_id_type=MESH,
        ).start()
        return carry

    lax.fori_loop(1, N, push, 0)

    own_up.wait()
    own_down.wait()
    up_copy.wait()
    down_copy.wait()

    groups = per_chunk // SUB
    grid_a = lax.broadcasted_iota(jnp.int32, (PEERS, per_chunk), 0)
    grid_b = lax.broadcasted_iota(jnp.int32, (PEERS, per_chunk), 1)
    to_peer = jnp.where(lax.div(grid_b, slots) == grid_a, 1.0, 0.0)
    row_id = lax.broadcasted_iota(jnp.int32, (per_chunk, LANES), 0)
    lane_id = lax.broadcasted_iota(jnp.int32, (per_chunk, LANES), 1)
    to_lane = jnp.where(lax.rem(row_id, slots) == lane_id, 1.0, 0.0)

    def chunk(c, carry):
        q = lax.rem(q_me - c + NX, NX)
        first = pl.multiple_of(q * per_chunk, SUB)
        local_wait(recv.at[:, pl.ds(0, per_chunk)], f_recv.at[c])

        def unpack(g, inner):
            r = pl.ds(pl.multiple_of(first + g * SUB, SUB), SUB)
            both = jnp.concatenate(
                [recv[0, r].reshape(SUB * SUB, LANES), recv[1, r].reshape(SUB * SUB, LANES)], axis=1
            )
            out = bf16(dot(perm[...], both))
            for f in range(SUB):
                part = out[f * SUB : (f + 1) * SUB]
                rows_x[r, f * LANES : (f + 1) * LANES] = part[:, :LANES]
                rows_g[r, f * LANES : (f + 1) * LANES] = part[:, LANES:]
            return inner

        lax.fori_loop(0, groups, unpack, 0)

        here = pl.ds(first, per_chunk)
        gate = jnp.zeros((per_chunk, 1), jnp.float32)
        for t in range(2 * half // 256):
            cols = slice(t * 256, (t + 1) * 256)
            hidden = dot(rows_x[here, :], wu[:, cols])
            upstream = dot(rows_g[here, :], wd[cols, :], ((1,), (1,)))
            s = jax.nn.sigmoid(hidden)
            activation = bf16(hidden * s)
            act[here, cols] = activation
            dhid[here, cols] = bf16(upstream * (s * (1.0 + hidden * (1.0 - s))))
            gate += jnp.sum(activation.astype(jnp.float32) * upstream, axis=1, keepdims=True)

        for t in range(WIDE // 512):
            cols = slice(t * 512, (t + 1) * 512)
            drow[:, cols] = bf16(dot(dhid[here, :], wu[cols, :], ((1,), (1,))))

        for g in range(0, groups, 2):
            pair = [
                jnp.concatenate(
                    [
                        drow[(g + h) * SUB : (g + h + 1) * SUB, f * LANES : (f + 1) * LANES]
                        for f in range(SUB)
                    ],
                    axis=0,
                )
                for h in range(2)
            ]
            out = bf16(dot(perm[...], jnp.concatenate(pair, axis=1)))
            for h in range(2):
                r = pl.ds(pl.multiple_of(first + (g + h) * SUB, SUB), SUB)
                dsend[r] = out[:, h * LANES : (h + 1) * LANES].reshape(SUB, SUB, LANES)

        @pl.when(c == 0)
        def _():
            pltpu.make_async_copy(dsend.at[my_rows], back.at[my_rows], r_recv.at[0]).start()

        def reply(i, inner):
            dz, dy = hop(i)
            zz, yy = lax.rem(z - dz + NZ, NZ), lax.rem(y - dy + NY, NY)
            source = pl.ds(block_of(q, zz, yy) * slots, slots)
            pltpu.make_async_remote_copy(
                src_ref=dsend.at[source], dst_ref=back.at[my_rows],
                send_sem=r_send, recv_sem=r_recv.at[c],
                device_id={"expert": expert_of(q, zz, yy)}, device_id_type=MESH,
            ).start()
            return inner

        lax.fori_loop(jnp.where(c == 0, 1, 0), PEERS, reply, 0)

        spread = lax.dot_general(
            to_peer, gate * to_lane, (((1,), (0,)), ((), ())),
            precision=lax.Precision.HIGHEST, preferred_element_type=jnp.float32,
        )
        gsend[pl.ds(q * PEERS, PEERS)] = spread.reshape(PEERS, 1, LANES)
        return carry

    lax.fori_loop(0, CHUNKS, chunk, 0)

    pltpu.make_async_copy(gsend.at[block_of(q_me, z, y)], gback_ref.at[me], g_recv).start()

    def reply_gate(n, carry):
        c = lax.div(n, PEERS)
        dz, dy = hop(lax.rem(n, PEERS))
        q, zz, yy = lax.rem(q_me - c + NX, NX), lax.rem(z - dz + NZ, NZ), lax.rem(y - dy + NY, NY)
        pltpu.make_async_remote_copy(
            src_ref=gsend.at[block_of(q, zz, yy)], dst_ref=gback_ref.at[me],
            send_sem=g_send, recv_sem=g_recv,
            device_id={"expert": expert_of(q, zz, yy)}, device_id_type=MESH,
        ).start()
        return carry

    lax.fori_loop(1, N, reply_gate, 0)

    tiles = WIDE // 512
    for t in range(tiles):
        cols = slice(t * 512, (t + 1) * 512)
        up_out[cols, :] = dot(rows_x[:, cols], dhid[:, theirs], ((0,), (0,)))
    up_swap = pltpu.make_async_remote_copy(
        src_ref=up_out, dst_ref=up_in, send_sem=d_send.at[0], recv_sem=d_recv.at[0],
        device_id=partner, device_id_type=MESH,
    )
    up_swap.start()
    for t in range(tiles):
        cols = slice(t * 512, (t + 1) * 512)
        down_out[:, cols] = dot(act[:, theirs], rows_g[:, cols], ((0,), (0,)))
    down_swap = pltpu.make_async_remote_copy(
        src_ref=down_out, dst_ref=down_in, send_sem=d_send.at[1], recv_sem=d_recv.at[1],
        device_id=partner, device_id_type=MESH,
    )
    down_swap.start()
    up_swap.wait()
    for t in range(tiles):
        cols = slice(t * 512, (t + 1) * 512)
        both = dot(rows_x[:, cols], dhid[:, mine], ((0,), (0,))) + up_in[cols, :]
        dup_ref[cols, :] = bf16(both)
    down_swap.wait()
    for t in range(tiles):
        cols = slice(t * 512, (t + 1) * 512)
        both = dot(act[:, mine], rows_g[:, cols], ((0,), (0,))) + down_in[:, cols]
        ddown_ref[:, cols] = bf16(both)

    total[...] = jnp.zeros_like(total)

    def combine(c, carry):
        q = lax.rem(q_me + c, NX)
        first = pl.multiple_of(q * per_chunk, SUB)
        local_wait(back.at[pl.ds(0, per_chunk)], r_recv.at[c])
        for g in range(0, groups, 2):
            pair = [
                back[pl.ds(pl.multiple_of(first + (g + h) * SUB, SUB), SUB)].reshape(SUB * SUB, LANES)
                for h in range(2)
            ]
            out = bf16(dot(perm[...], jnp.concatenate(pair, axis=1)))
            for h in range(2):
                for f in range(SUB):
                    drow[(g + h) * SUB : (g + h + 1) * SUB, f * LANES : (f + 1) * LANES] = out[
                        f * SUB : (f + 1) * SUB, h * LANES : (h + 1) * LANES
                    ]
        token = lax.broadcasted_iota(jnp.int32, (total.shape[0], per_chunk), 0)
        chosen = bf16(jnp.where(token == pick_ref[q], 1.0, 0.0))
        for t in range(tiles):
            cols = slice(t * 512, (t + 1) * 512)
            total[:, cols] += dot(chosen, drow[:, cols])
        return carry

    lax.fori_loop(0, CHUNKS, combine, 0)
    dtok_ref[...] = bf16(total[...])

    local_wait(gback_ref, g_recv)
    local_wait(gsend.at[pl.ds(0, N - 1)], g_send)
    local_wait(send.at[pl.ds(0, N - 1)], f_send)
    local_wait(dsend.at[pl.ds(0, (N - 1) * slots)], r_send)


def per_device(tokens, grad_out, gates, slot_index, slot_count, up_weight, down_weight):
    experts, slots = slot_index.shape[2:]
    held, width = tokens.shape[1:]
    half = up_weight.shape[2]
    total = experts * slots
    picks = slot_index[0, 0]
    live = lax.broadcasted_iota(jnp.int32, (experts, slots), 1) < slot_count[0, 0][:, None]
    scale = jnp.where(live, gates[0, 0].astype(jnp.float32), 0.0)
    cube = picks.reshape(NZ, NY, NX, slots)
    order = jnp.stack([jnp.roll(cube[:, j], j, axis=1) for j in range(NY)], axis=1)
    order = jnp.transpose(order, (2, 0, 1, 3)).reshape(CHUNKS, 1, PEERS * slots)

    vmem = pl.BlockSpec(memory_space=pltpu.VMEM)
    smem = pl.BlockSpec(memory_space=pltpu.SMEM)
    anywhere = pl.BlockSpec(memory_space=pl.ANY)
    low, full = jnp.bfloat16, jnp.float32
    dma = pltpu.SemaphoreType.DMA
    d_tokens, gate_back, d_up, d_down = pl.pallas_call(
        kernel,
        out_shape=(
            jax.ShapeDtypeStruct((held, width), low),
            jax.ShapeDtypeStruct((experts, 1, LANES), full),
            jax.ShapeDtypeStruct((width, half), low),
            jax.ShapeDtypeStruct((half, width), low),
        ),
        in_specs=[smem, smem, vmem, vmem, vmem, anywhere, anywhere],
        out_specs=(vmem, vmem, vmem, vmem),
        scratch_shapes=[
            pltpu.VMEM((experts, 2, slots, SUB, LANES), low),
            pltpu.VMEM((2, total, SUB, LANES), low),
            pltpu.VMEM((width, 2 * half), low),
            pltpu.VMEM((2 * half, width), low),
            pltpu.VMEM((total, width), low),
            pltpu.VMEM((total, width), low),
            pltpu.VMEM((total, 2 * half), low),
            pltpu.VMEM((total, 2 * half), low),
            pltpu.VMEM((PEERS * slots, width), low),
            pltpu.VMEM((total, SUB, LANES), low),
            pltpu.VMEM((total, SUB, LANES), low),
            pltpu.VMEM((experts, 1, LANES), full),
            pltpu.VMEM((width, half), full),
            pltpu.VMEM((width, half), full),
            pltpu.VMEM((half, width), full),
            pltpu.VMEM((half, width), full),
            pltpu.VMEM((held, width), full),
            pltpu.VMEM((SUB * SUB, SUB * SUB), low),
            dma((6,)),
            dma,
            dma((CHUNKS,)),
            dma,
            dma((CHUNKS,)),
            dma,
            dma,
            dma((2,)),
            dma((2,)),
        ],
        compiler_params=pltpu.CompilerParams(
            collective_id=0, has_side_effects=True, vmem_limit_bytes=56 << 20
        ),
    )(
        picks.reshape(total),
        scale.reshape(total),
        order,
        tokens[0].reshape(held, SUB, LANES),
        grad_out[0].reshape(held, SUB, LANES),
        up_weight[0],
        down_weight[0],
    )
    inverse = jnp.where(live, 1.0 / jnp.where(live, scale, 1.0), 0.0)
    d_gates = gate_back[:, 0, :slots] * inverse
    return (
        d_tokens[None],
        d_gates.astype(low)[None, None],
        d_up[None],
        d_down[None],
    )


def solution(mesh):
    in_specs = (
        P("dp", "expert", None),
        P("dp", "expert", None),
        P("dp", "expert", None, None),
        P("dp", "expert", None, None),
        P("dp", "expert", None),
        P("expert", None, "dp"),
        P("expert", "dp", None),
    )
    out_specs = (
        P("dp", "expert", None),
        P("dp", "expert", None, None),
        P("expert", None, "dp"),
        P("expert", "dp", None),
    )
    return jax.shard_map(
        per_device, mesh=mesh, in_specs=in_specs, out_specs=out_specs, check_vma=False
    )
```

```python
import jax
import jax.numpy as jnp
from jax import lax
from jax.experimental import pallas as pl
from jax.experimental.pallas import tpu as pltpu
from jax.sharding import PartitionSpec as P

MESH = pl.DeviceIdType.MESH
NX, NY, NZ = 4, 4, 8
N = NX * NY * NZ
CHUNKS = NX
PEERS = NY * NZ
LANES = 128
SUB = 16
WIDE = SUB * LANES


def place(me):
    return me % NX, (me // NX) % NY, me // (NX * NY)


def block_of(q, z, y):
    return q * PEERS + z * NY + y


def expert_of(q, z, y):
    return (z * NY + y) * NX + lax.rem(q - y + NX, NX)


def hop(i):
    return lax.rem(i, NZ), lax.div(i, NZ)


def bf16(v):
    return v.astype(jnp.bfloat16)


def dot(a, b, dims=((1,), (0,))):
    return lax.dot_general(a, b, (dims, ((), ())), preferred_element_type=jnp.float32)


def local_wait(ref, sem):
    pltpu.make_async_copy(ref, ref, sem).wait()


def kernel(
    idx_ref, pick_ref, gates_ref, count_ref, tok_ref, grad_ref, up_ref, down_ref,
    dtok_ref, dgate_ref, dup_ref, ddown_ref,
    tok, grad, scale_vec, scale, gback,
    send, recv, wu, wd, rows_x, rows_g, act, dhid, drow, dsend, back, gsend,
    up_out, up_in, down_out, down_in, total, perm,
    w_sem, s_sem, f_send, f_recv, r_send, r_recv, g_send, g_recv, d_send, d_recv,
):
    me = lax.axis_index("expert")
    core = lax.axis_index("dp")
    x, y, z = place(me)
    q_me = lax.rem(x + y, NX)
    slots = send.shape[2]
    per_chunk = PEERS * slots
    half = up_ref.shape[1]
    mine = pl.ds(pl.multiple_of(core * half, LANES), half)
    theirs = pl.ds(pl.multiple_of((1 - core) * half, LANES), half)
    partner = {"dp": 1 - core}

    barrier = pltpu.get_barrier_semaphore()
    pl.semaphore_signal(barrier, inc=1, device_id=partner, device_id_type=MESH)

    def greet(step, carry):
        pl.semaphore_signal(
            barrier, inc=1, device_id={"expert": lax.rem(me + step, N)}, device_id_type=MESH
        )
        return carry

    lax.fori_loop(1, N, greet, 0)

    own_up = pltpu.make_async_copy(up_ref, wu.at[:, mine], w_sem.at[0])
    own_up.start()
    own_down = pltpu.make_async_copy(down_ref, wd.at[mine, :], w_sem.at[1])
    own_down.start()

    a = lax.broadcasted_iota(jnp.int32, (SUB * SUB, SUB * SUB), 0)
    b = lax.broadcasted_iota(jnp.int32, (SUB * SUB, SUB * SUB), 1)
    swap = (lax.rem(a, SUB) == lax.div(b, SUB)) & (lax.div(a, SUB) == lax.rem(b, SUB))
    perm[...] = jnp.where(swap, 1.0, 0.0).astype(jnp.bfloat16)

    scale_vec[...] = jnp.zeros_like(scale_vec)
    for k in range(slots):
        live = jnp.where(count_ref[...] > k, 1.0, 0.0)
        scale_vec[k : k + 1, :] = live * gates_ref[k : k + 1, :].astype(jnp.float32)
    to_scalars = pltpu.make_async_copy(scale_vec, scale, s_sem)
    to_scalars.start()

    def by_row(g, carry):
        r = pl.ds(pl.multiple_of(g * SUB, SUB), SUB)
        both = jnp.concatenate(
            [
                jnp.concatenate(
                    [ref[r, f * LANES : (f + 1) * LANES] for f in range(SUB)], axis=0
                )
                for ref in (tok_ref, grad_ref)
            ],
            axis=1,
        )
        out = bf16(dot(perm[...], both))
        tok[r] = out[:, :LANES].reshape(SUB, SUB, LANES)
        grad[r] = out[:, LANES:].reshape(SUB, SUB, LANES)
        return carry

    lax.fori_loop(0, tok.shape[0] // SUB, by_row, 0)
    to_scalars.wait()

    def fill(target):
        for k in range(slots):
            row = idx_ref[k, 0, target]
            send[target, 0, k] = tok[row]
            send[target, 1, k] = bf16(grad[row].astype(jnp.float32) * scale[k, target])

    pl.semaphore_wait(barrier, N)

    up_copy = pltpu.make_async_remote_copy(
        src_ref=up_ref, dst_ref=wu.at[:, mine], send_sem=w_sem.at[2], recv_sem=w_sem.at[3],
        device_id=partner, device_id_type=MESH,
    )
    up_copy.start()
    down_copy = pltpu.make_async_remote_copy(
        src_ref=down_ref, dst_ref=wd.at[mine, :], send_sem=w_sem.at[4], recv_sem=w_sem.at[5],
        device_id=partner, device_id_type=MESH,
    )
    down_copy.start()

    my_rows = pl.ds(block_of(q_me, z, y) * slots, slots)

    def push(n, carry):
        c = lax.div(n, PEERS)
        dz, dy = hop(lax.rem(n, PEERS))
        target = expert_of(lax.rem(q_me + c, NX), lax.rem(z + dz, NZ), lax.rem(y + dy, NY))
        fill(target)
        pltpu.make_async_remote_copy(
            src_ref=send.at[target], dst_ref=recv.at[:, my_rows],
            send_sem=f_send, recv_sem=f_recv.at[c],
            device_id={"expert": target}, device_id_type=MESH,
        ).start()
        return carry

    lax.fori_loop(1, N, push, 0)
    fill(me)
    pltpu.make_async_copy(send.at[me], recv.at[:, my_rows], f_recv.at[0]).start()

    own_up.wait()
    own_down.wait()
    up_copy.wait()
    down_copy.wait()

    groups = per_chunk // SUB
    grid_a = lax.broadcasted_iota(jnp.int32, (PEERS, per_chunk), 0)
    grid_b = lax.broadcasted_iota(jnp.int32, (PEERS, per_chunk), 1)
    to_peer = jnp.where(lax.div(grid_b, slots) == grid_a, 1.0, 0.0)
    row_id = lax.broadcasted_iota(jnp.int32, (per_chunk, LANES), 0)
    lane_id = lax.broadcasted_iota(jnp.int32, (per_chunk, LANES), 1)
    to_lane = jnp.where(lax.rem(row_id, slots) == lane_id, 1.0, 0.0)

    def chunk(c, carry):
        q = lax.rem(q_me - c + NX, NX)
        first = pl.multiple_of(q * per_chunk, SUB)
        local_wait(recv.at[:, pl.ds(0, per_chunk)], f_recv.at[c])

        def unpack(g, inner):
            r = pl.ds(pl.multiple_of(first + g * SUB, SUB), SUB)
            both = jnp.concatenate(
                [recv[0, r].reshape(SUB * SUB, LANES), recv[1, r].reshape(SUB * SUB, LANES)], axis=1
            )
            out = bf16(dot(perm[...], both))
            for f in range(SUB):
                part = out[f * SUB : (f + 1) * SUB]
                rows_x[r, f * LANES : (f + 1) * LANES] = part[:, :LANES]
                rows_g[r, f * LANES : (f + 1) * LANES] = part[:, LANES:]
            return inner

        lax.fori_loop(0, groups, unpack, 0)

        here = pl.ds(first, per_chunk)
        gate = jnp.zeros((per_chunk, 1), jnp.float32)
        for t in range(2 * half // 256):
            cols = slice(t * 256, (t + 1) * 256)
            hidden = dot(rows_x[here, :], wu[:, cols])
            upstream = dot(rows_g[here, :], wd[cols, :], ((1,), (1,)))
            s = jax.nn.sigmoid(hidden)
            activation = bf16(hidden * s)
            act[here, cols] = activation
            dhid[here, cols] = bf16(upstream * (s * (1.0 + hidden * (1.0 - s))))
            gate += jnp.sum(activation.astype(jnp.float32) * upstream, axis=1, keepdims=True)

        for t in range(WIDE // 512):
            cols = slice(t * 512, (t + 1) * 512)
            drow[:, cols] = bf16(dot(dhid[here, :], wu[cols, :], ((1,), (1,))))

        for g in range(0, groups, 2):
            pair = [
                jnp.concatenate(
                    [
                        drow[(g + h) * SUB : (g + h + 1) * SUB, f * LANES : (f + 1) * LANES]
                        for f in range(SUB)
                    ],
                    axis=0,
                )
                for h in range(2)
            ]
            out = bf16(dot(perm[...], jnp.concatenate(pair, axis=1)))
            for h in range(2):
                r = pl.ds(pl.multiple_of(first + (g + h) * SUB, SUB), SUB)
                dsend[r] = out[:, h * LANES : (h + 1) * LANES].reshape(SUB, SUB, LANES)

        @pl.when(c == 0)
        def _():
            pltpu.make_async_copy(dsend.at[my_rows], back.at[my_rows], r_recv.at[0]).start()

        def reply(i, inner):
            dz, dy = hop(i)
            zz, yy = lax.rem(z - dz + NZ, NZ), lax.rem(y - dy + NY, NY)
            source = pl.ds(block_of(q, zz, yy) * slots, slots)
            pltpu.make_async_remote_copy(
                src_ref=dsend.at[source], dst_ref=back.at[my_rows],
                send_sem=r_send, recv_sem=r_recv.at[c],
                device_id={"expert": expert_of(q, zz, yy)}, device_id_type=MESH,
            ).start()
            return inner

        lax.fori_loop(jnp.where(c == 0, 1, 0), PEERS, reply, 0)

        spread = lax.dot_general(
            to_peer, gate * to_lane, (((1,), (0,)), ((), ())),
            precision=lax.Precision.HIGHEST, preferred_element_type=jnp.float32,
        )
        gsend[pl.ds(q * PEERS, PEERS)] = spread.reshape(PEERS, 1, LANES)
        return carry

    lax.fori_loop(0, CHUNKS, chunk, 0)

    pltpu.make_async_copy(gsend.at[block_of(q_me, z, y)], gback.at[me], g_recv).start()

    def reply_gate(n, carry):
        c = lax.div(n, PEERS)
        dz, dy = hop(lax.rem(n, PEERS))
        q, zz, yy = lax.rem(q_me - c + NX, NX), lax.rem(z - dz + NZ, NZ), lax.rem(y - dy + NY, NY)
        pltpu.make_async_remote_copy(
            src_ref=gsend.at[block_of(q, zz, yy)], dst_ref=gback.at[me],
            send_sem=g_send, recv_sem=g_recv,
            device_id={"expert": expert_of(q, zz, yy)}, device_id_type=MESH,
        ).start()
        return carry

    lax.fori_loop(1, N, reply_gate, 0)

    tiles = WIDE // 512
    for t in range(tiles):
        cols = slice(t * 512, (t + 1) * 512)
        up_out[cols, :] = dot(rows_x[:, cols], dhid[:, theirs], ((0,), (0,)))
    up_swap = pltpu.make_async_remote_copy(
        src_ref=up_out, dst_ref=up_in, send_sem=d_send.at[0], recv_sem=d_recv.at[0],
        device_id=partner, device_id_type=MESH,
    )
    up_swap.start()
    for t in range(tiles):
        cols = slice(t * 512, (t + 1) * 512)
        down_out[:, cols] = dot(act[:, theirs], rows_g[:, cols], ((0,), (0,)))
    down_swap = pltpu.make_async_remote_copy(
        src_ref=down_out, dst_ref=down_in, send_sem=d_send.at[1], recv_sem=d_recv.at[1],
        device_id=partner, device_id_type=MESH,
    )
    down_swap.start()
    up_swap.wait()
    for t in range(tiles):
        cols = slice(t * 512, (t + 1) * 512)
        both = dot(rows_x[:, cols], dhid[:, mine], ((0,), (0,))) + up_in[cols, :]
        dup_ref[cols, :] = bf16(both)
    down_swap.wait()
    for t in range(tiles):
        cols = slice(t * 512, (t + 1) * 512)
        both = dot(act[:, mine], rows_g[:, cols], ((0,), (0,))) + down_in[:, cols]
        ddown_ref[:, cols] = bf16(both)

    total[...] = jnp.zeros_like(total)

    def combine(c, carry):
        q = lax.rem(q_me + c, NX)
        first = pl.multiple_of(q * per_chunk, SUB)
        local_wait(back.at[pl.ds(0, per_chunk)], r_recv.at[c])
        for g in range(0, groups, 2):
            pair = [
                back[pl.ds(pl.multiple_of(first + (g + h) * SUB, SUB), SUB)].reshape(SUB * SUB, LANES)
                for h in range(2)
            ]
            out = bf16(dot(perm[...], jnp.concatenate(pair, axis=1)))
            for h in range(2):
                for f in range(SUB):
                    drow[(g + h) * SUB : (g + h + 1) * SUB, f * LANES : (f + 1) * LANES] = out[
                        f * SUB : (f + 1) * SUB, h * LANES : (h + 1) * LANES
                    ]
        expert = lax.broadcasted_iota(jnp.int32, (N, per_chunk), 0)
        peer = lax.div(lax.broadcasted_iota(jnp.int32, (N, per_chunk), 1), slots)
        owner = expert_of(q, lax.div(peer, NY), lax.rem(peer, NY))
        owned = jnp.where(expert == owner, 1.0, 0.0)
        slot = lax.rem(lax.broadcasted_iota(jnp.int32, (1, per_chunk), 1), slots)
        picked = jnp.zeros((1, per_chunk), jnp.float32)
        for k in range(slots):
            picked += jnp.where(slot == k, dot(pick_ref[k].astype(jnp.float32), owned), 0.0)
        token = lax.broadcasted_iota(jnp.int32, (total.shape[0], per_chunk), 0)
        chosen = bf16(jnp.where(token.astype(jnp.float32) == picked, 1.0, 0.0))
        for t in range(tiles):
            cols = slice(t * 512, (t + 1) * 512)
            total[:, cols] += dot(chosen, drow[:, cols])
        return carry

    lax.fori_loop(0, CHUNKS, combine, 0)
    dtok_ref[...] = bf16(total[...])

    local_wait(gback, g_recv)
    eye = jnp.where(
        lax.broadcasted_iota(jnp.int32, (8, LANES), 0)
        == lax.broadcasted_iota(jnp.int32, (8, LANES), 1),
        1.0,
        0.0,
    )
    by_slot = lax.dot_general(
        eye, gback[...].reshape(N, LANES), (((1,), (1,)), ((), ())),
        precision=lax.Precision.HIGHEST, preferred_element_type=jnp.float32,
    )
    for k in range(slots):
        c = scale_vec[k : k + 1, :]
        inverse = jnp.where(c > 0.0, 1.0 / jnp.where(c > 0.0, c, 1.0), 0.0)
        dgate_ref[k : k + 1, :] = bf16(by_slot[k : k + 1, :] * inverse)
    local_wait(gsend.at[pl.ds(0, N - 1)], g_send)
    local_wait(send.at[pl.ds(0, N - 1)], f_send)
    local_wait(dsend.at[pl.ds(0, (N - 1) * slots)], r_send)


def write_out(*refs):
    count = len(refs) // 2
    copies = [
        pltpu.make_async_copy(refs[i], refs[count + i], refs[-1].at[i]) for i in range(count)
    ]
    for copy in copies:
        copy.start()
    for copy in copies:
        copy.wait()


def per_device(tokens, grad_out, gates, slot_index, slot_count, up_weight, down_weight):
    experts, slots = slot_index.shape[2:]
    held, width = tokens.shape[1:]
    half = up_weight.shape[2]
    total = experts * slots
    picks = slot_index[0, 0].T.reshape(slots, 1, experts)

    vmem = pl.BlockSpec(memory_space=pltpu.VMEM)
    smem = pl.BlockSpec(memory_space=pltpu.SMEM)
    anywhere = pl.BlockSpec(memory_space=pl.ANY)
    low, full = jnp.bfloat16, jnp.float32
    dma = pltpu.SemaphoreType.DMA
    outs = (((held, width), low), ((slots, experts), low), ((width, half), low), ((half, width), low))
    results = pl.pallas_call(
        kernel,
        out_shape=tuple(pltpu.VMEM(shape, dtype) for shape, dtype in outs),
        in_specs=[smem, vmem, vmem, vmem, vmem, vmem, anywhere, anywhere],
        out_specs=(vmem, vmem, vmem, vmem),
        scratch_shapes=[
            pltpu.VMEM((held, SUB, LANES), low),
            pltpu.VMEM((held, SUB, LANES), low),
            pltpu.VMEM((8, experts), full),
            pltpu.SMEM((8, experts), full),
            pltpu.VMEM((experts, 1, LANES), full),
            pltpu.VMEM((experts, 2, slots, SUB, LANES), low),
            pltpu.VMEM((2, total, SUB, LANES), low),
            pltpu.VMEM((width, 2 * half), low),
            pltpu.VMEM((2 * half, width), low),
            pltpu.VMEM((total, width), low),
            pltpu.VMEM((total, width), low),
            pltpu.VMEM((total, 2 * half), low),
            pltpu.VMEM((total, 2 * half), low),
            pltpu.VMEM((PEERS * slots, width), low),
            pltpu.VMEM((total, SUB, LANES), low),
            pltpu.VMEM((total, SUB, LANES), low),
            pltpu.VMEM((experts, 1, LANES), full),
            pltpu.VMEM((width, half), full),
            pltpu.VMEM((width, half), full),
            pltpu.VMEM((half, width), full),
            pltpu.VMEM((half, width), full),
            pltpu.VMEM((held, width), full),
            pltpu.VMEM((SUB * SUB, SUB * SUB), low),
            dma((6,)),
            dma,
            dma,
            dma((CHUNKS,)),
            dma,
            dma((CHUNKS,)),
            dma,
            dma,
            dma((2,)),
            dma((2,)),
        ],
        compiler_params=pltpu.CompilerParams(
            collective_id=0, has_side_effects=True, vmem_limit_bytes=50 << 20
        ),
    )(
        picks,
        picks,
        gates[0, 0].T,
        slot_count[0],
        tokens[0],
        grad_out[0],
        up_weight[0],
        down_weight[0],
    )
    d_tokens, d_gate, d_up, d_down = pl.pallas_call(
        write_out,
        out_shape=tuple(jax.ShapeDtypeStruct(shape, dtype) for shape, dtype in outs),
        in_specs=[vmem] * 4,
        out_specs=(anywhere,) * 4,
        scratch_shapes=[dma((4,))],
    )(*results)
    return d_tokens[None], d_gate.T[None, None], d_up[None], d_down[None]


def solution(mesh):
    in_specs = (
        P("dp", "expert", None),
        P("dp", "expert", None),
        P("dp", "expert", None, None),
        P("dp", "expert", None, None),
        P("dp", "expert", None),
        P("expert", None, "dp"),
        P("expert", "dp", None),
    )
    out_specs = (
        P("dp", "expert", None),
        P("dp", "expert", None, None),
        P("expert", None, "dp"),
        P("expert", "dp", None),
    )
    return jax.shard_map(
        per_device, mesh=mesh, in_specs=in_specs, out_specs=out_specs, check_vma=False
    )
```

```python
import jax
import jax.numpy as jnp
from jax import lax
from jax.experimental import pallas as pl
from jax.experimental.pallas import tpu as pltpu
from jax.sharding import PartitionSpec as P

MESH = pl.DeviceIdType.MESH
NX, NY, NZ = 4, 4, 8
N = NX * NY * NZ
CHUNKS = NX
PEERS = NY * NZ
LANES = 128
SUB = 16
WIDE = SUB * LANES


def place(me):
    return me % NX, (me // NX) % NY, me // (NX * NY)


def block_of(q, z, y):
    return q * PEERS + z * NY + y


def expert_of(q, z, y):
    return (z * NY + y) * NX + lax.rem(q - y + NX, NX)


def hop(i):
    return lax.rem(i, NZ), lax.div(i, NZ)


def bf16(v):
    return v.astype(jnp.bfloat16)


def dot(a, b, dims=((1,), (0,))):
    return lax.dot_general(a, b, (dims, ((), ())), preferred_element_type=jnp.float32)


def local_wait(ref, sem):
    pltpu.make_async_copy(ref, ref, sem).wait()


def kernel(
    idx_ref, pick_hbm, gates_hbm, count_hbm, tok_ref, grad_ref, up_ref, down_ref,
    dtok_ref, dgate_ref, dup_ref, ddown_ref,
    pick_ref, gates_ref, count_ref, tok, grad, scale_vec, scale, gback,
    send, recv, wu, wd, rows_x, rows_g, act, dhid, drow, dsend, back, gsend,
    up_out, up_in, down_out, down_in, total, perm,
    w_sem, s_sem, small_sem, f_send, f_recv, r_send, r_recv, g_send, g_recv, d_send, d_recv,
):
    me = lax.axis_index("expert")
    core = lax.axis_index("dp")
    x, y, z = place(me)
    q_me = lax.rem(x + y, NX)
    slots = send.shape[2]
    per_chunk = PEERS * slots
    half = up_ref.shape[1]
    mine = pl.ds(pl.multiple_of(core * half, LANES), half)
    theirs = pl.ds(pl.multiple_of((1 - core) * half, LANES), half)
    partner = {"dp": 1 - core}

    barrier = pltpu.get_barrier_semaphore()
    pl.semaphore_signal(barrier, inc=1, device_id=partner, device_id_type=MESH)

    def greet(step, carry):
        pl.semaphore_signal(
            barrier, inc=1, device_id={"expert": lax.rem(me + step, N)}, device_id_type=MESH
        )
        return carry

    lax.fori_loop(1, N, greet, 0)

    own_up = pltpu.make_async_copy(up_ref, wu.at[:, mine], w_sem.at[0])
    own_up.start()
    own_down = pltpu.make_async_copy(down_ref, wd.at[mine, :], w_sem.at[1])
    own_down.start()

    small = [
        pltpu.make_async_copy(src, dst, small_sem.at[i])
        for i, (src, dst) in enumerate(
            ((gates_hbm, gates_ref), (count_hbm, count_ref), (pick_hbm, pick_ref))
        )
    ]
    for copy in small:
        copy.start()

    a = lax.broadcasted_iota(jnp.int32, (SUB * SUB, SUB * SUB), 0)
    b = lax.broadcasted_iota(jnp.int32, (SUB * SUB, SUB * SUB), 1)
    swap = (lax.rem(a, SUB) == lax.div(b, SUB)) & (lax.div(a, SUB) == lax.rem(b, SUB))
    perm[...] = jnp.where(swap, 1.0, 0.0).astype(jnp.bfloat16)

    for copy in small:
        copy.wait()
    scale_vec[...] = jnp.zeros_like(scale_vec)
    for k in range(slots):
        live = jnp.where(count_ref[...] > k, 1.0, 0.0)
        scale_vec[k : k + 1, :] = live * gates_ref[k : k + 1, :].astype(jnp.float32)
    to_scalars = pltpu.make_async_copy(scale_vec, scale, s_sem)
    to_scalars.start()

    def by_row(g, carry):
        r = pl.ds(pl.multiple_of(g * SUB, SUB), SUB)
        both = jnp.concatenate(
            [
                jnp.concatenate(
                    [ref[r, f * LANES : (f + 1) * LANES] for f in range(SUB)], axis=0
                )
                for ref in (tok_ref, grad_ref)
            ],
            axis=1,
        )
        out = bf16(dot(perm[...], both))
        tok[r] = out[:, :LANES].reshape(SUB, SUB, LANES)
        grad[r] = out[:, LANES:].reshape(SUB, SUB, LANES)
        return carry

    lax.fori_loop(0, tok.shape[0] // SUB, by_row, 0)
    to_scalars.wait()

    def fill(target):
        for k in range(slots):
            row = idx_ref[k, 0, target]
            send[target, 0, k] = tok[row]
            send[target, 1, k] = bf16(grad[row].astype(jnp.float32) * scale[k, target])

    pl.semaphore_wait(barrier, N)

    up_copy = pltpu.make_async_remote_copy(
        src_ref=up_ref, dst_ref=wu.at[:, mine], send_sem=w_sem.at[2], recv_sem=w_sem.at[3],
        device_id=partner, device_id_type=MESH,
    )
    up_copy.start()
    down_copy = pltpu.make_async_remote_copy(
        src_ref=down_ref, dst_ref=wd.at[mine, :], send_sem=w_sem.at[4], recv_sem=w_sem.at[5],
        device_id=partner, device_id_type=MESH,
    )
    down_copy.start()

    my_rows = pl.ds(block_of(q_me, z, y) * slots, slots)

    def push(n, carry):
        c = lax.div(n, PEERS)
        dz, dy = hop(lax.rem(n, PEERS))
        target = expert_of(lax.rem(q_me + c, NX), lax.rem(z + dz, NZ), lax.rem(y + dy, NY))
        fill(target)
        pltpu.make_async_remote_copy(
            src_ref=send.at[target], dst_ref=recv.at[:, my_rows],
            send_sem=f_send, recv_sem=f_recv.at[c],
            device_id={"expert": target}, device_id_type=MESH,
        ).start()
        return carry

    lax.fori_loop(1, N, push, 0)
    fill(me)
    pltpu.make_async_copy(send.at[me], recv.at[:, my_rows], f_recv.at[0]).start()

    own_up.wait()
    own_down.wait()
    up_copy.wait()
    down_copy.wait()

    groups = per_chunk // SUB
    grid_a = lax.broadcasted_iota(jnp.int32, (PEERS, per_chunk), 0)
    grid_b = lax.broadcasted_iota(jnp.int32, (PEERS, per_chunk), 1)
    to_peer = jnp.where(lax.div(grid_b, slots) == grid_a, 1.0, 0.0)
    row_id = lax.broadcasted_iota(jnp.int32, (per_chunk, LANES), 0)
    lane_id = lax.broadcasted_iota(jnp.int32, (per_chunk, LANES), 1)
    to_lane = jnp.where(lax.rem(row_id, slots) == lane_id, 1.0, 0.0)

    def chunk(c, carry):
        q = lax.rem(q_me - c + NX, NX)
        first = pl.multiple_of(q * per_chunk, SUB)
        local_wait(recv.at[:, pl.ds(0, per_chunk)], f_recv.at[c])

        def unpack(g, inner):
            r = pl.ds(pl.multiple_of(first + g * SUB, SUB), SUB)
            both = jnp.concatenate(
                [recv[0, r].reshape(SUB * SUB, LANES), recv[1, r].reshape(SUB * SUB, LANES)], axis=1
            )
            out = bf16(dot(perm[...], both))
            for f in range(SUB):
                part = out[f * SUB : (f + 1) * SUB]
                rows_x[r, f * LANES : (f + 1) * LANES] = part[:, :LANES]
                rows_g[r, f * LANES : (f + 1) * LANES] = part[:, LANES:]
            return inner

        lax.fori_loop(0, groups, unpack, 0)

        here = pl.ds(first, per_chunk)
        gate = jnp.zeros((per_chunk, 1), jnp.float32)
        for t in range(2 * half // 256):
            cols = slice(t * 256, (t + 1) * 256)
            hidden = dot(rows_x[here, :], wu[:, cols])
            upstream = dot(rows_g[here, :], wd[cols, :], ((1,), (1,)))
            s = jax.nn.sigmoid(hidden)
            activation = bf16(hidden * s)
            act[here, cols] = activation
            dhid[here, cols] = bf16(upstream * (s * (1.0 + hidden * (1.0 - s))))
            gate += jnp.sum(activation.astype(jnp.float32) * upstream, axis=1, keepdims=True)

        for t in range(WIDE // 512):
            cols = slice(t * 512, (t + 1) * 512)
            drow[:, cols] = bf16(dot(dhid[here, :], wu[cols, :], ((1,), (1,))))

        for g in range(0, groups, 2):
            pair = [
                jnp.concatenate(
                    [
                        drow[(g + h) * SUB : (g + h + 1) * SUB, f * LANES : (f + 1) * LANES]
                        for f in range(SUB)
                    ],
                    axis=0,
                )
                for h in range(2)
            ]
            out = bf16(dot(perm[...], jnp.concatenate(pair, axis=1)))
            for h in range(2):
                r = pl.ds(pl.multiple_of(first + (g + h) * SUB, SUB), SUB)
                dsend[r] = out[:, h * LANES : (h + 1) * LANES].reshape(SUB, SUB, LANES)

        @pl.when(c == 0)
        def _():
            pltpu.make_async_copy(dsend.at[my_rows], back.at[my_rows], r_recv.at[0]).start()

        def reply(i, inner):
            dz, dy = hop(i)
            zz, yy = lax.rem(z - dz + NZ, NZ), lax.rem(y - dy + NY, NY)
            source = pl.ds(block_of(q, zz, yy) * slots, slots)
            pltpu.make_async_remote_copy(
                src_ref=dsend.at[source], dst_ref=back.at[my_rows],
                send_sem=r_send, recv_sem=r_recv.at[c],
                device_id={"expert": expert_of(q, zz, yy)}, device_id_type=MESH,
            ).start()
            return inner

        lax.fori_loop(jnp.where(c == 0, 1, 0), PEERS, reply, 0)

        spread = lax.dot_general(
            to_peer, gate * to_lane, (((1,), (0,)), ((), ())),
            precision=lax.Precision.HIGHEST, preferred_element_type=jnp.float32,
        )
        gsend[pl.ds(q * PEERS, PEERS)] = spread.reshape(PEERS, 1, LANES)
        return carry

    lax.fori_loop(0, CHUNKS, chunk, 0)

    pltpu.make_async_copy(gsend.at[block_of(q_me, z, y)], gback.at[me], g_recv).start()

    def reply_gate(n, carry):
        c = lax.div(n, PEERS)
        dz, dy = hop(lax.rem(n, PEERS))
        q, zz, yy = lax.rem(q_me - c + NX, NX), lax.rem(z - dz + NZ, NZ), lax.rem(y - dy + NY, NY)
        pltpu.make_async_remote_copy(
            src_ref=gsend.at[block_of(q, zz, yy)], dst_ref=gback.at[me],
            send_sem=g_send, recv_sem=g_recv,
            device_id={"expert": expert_of(q, zz, yy)}, device_id_type=MESH,
        ).start()
        return carry

    lax.fori_loop(1, N, reply_gate, 0)

    tiles = WIDE // 512
    for t in range(tiles):
        cols = slice(t * 512, (t + 1) * 512)
        up_out[cols, :] = dot(rows_x[:, cols], dhid[:, theirs], ((0,), (0,)))
    up_swap = pltpu.make_async_remote_copy(
        src_ref=up_out, dst_ref=up_in, send_sem=d_send.at[0], recv_sem=d_recv.at[0],
        device_id=partner, device_id_type=MESH,
    )
    up_swap.start()
    for t in range(tiles):
        cols = slice(t * 512, (t + 1) * 512)
        down_out[:, cols] = dot(act[:, theirs], rows_g[:, cols], ((0,), (0,)))
    down_swap = pltpu.make_async_remote_copy(
        src_ref=down_out, dst_ref=down_in, send_sem=d_send.at[1], recv_sem=d_recv.at[1],
        device_id=partner, device_id_type=MESH,
    )
    down_swap.start()
    up_swap.wait()
    for t in range(tiles):
        cols = slice(t * 512, (t + 1) * 512)
        both = dot(rows_x[:, cols], dhid[:, mine], ((0,), (0,))) + up_in[cols, :]
        dup_ref[cols, :] = bf16(both)
    down_swap.wait()
    for t in range(tiles):
        cols = slice(t * 512, (t + 1) * 512)
        both = dot(act[:, mine], rows_g[:, cols], ((0,), (0,))) + down_in[:, cols]
        ddown_ref[:, cols] = bf16(both)

    total[...] = jnp.zeros_like(total)

    def combine(c, carry):
        q = lax.rem(q_me + c, NX)
        first = pl.multiple_of(q * per_chunk, SUB)
        local_wait(back.at[pl.ds(0, per_chunk)], r_recv.at[c])
        for g in range(0, groups, 2):
            pair = [
                back[pl.ds(pl.multiple_of(first + (g + h) * SUB, SUB), SUB)].reshape(SUB * SUB, LANES)
                for h in range(2)
            ]
            out = bf16(dot(perm[...], jnp.concatenate(pair, axis=1)))
            for h in range(2):
                for f in range(SUB):
                    drow[(g + h) * SUB : (g + h + 1) * SUB, f * LANES : (f + 1) * LANES] = out[
                        f * SUB : (f + 1) * SUB, h * LANES : (h + 1) * LANES
                    ]
        expert = lax.broadcasted_iota(jnp.int32, (N, per_chunk), 0)
        peer = lax.div(lax.broadcasted_iota(jnp.int32, (N, per_chunk), 1), slots)
        owner = expert_of(q, lax.div(peer, NY), lax.rem(peer, NY))
        owned = jnp.where(expert == owner, 1.0, 0.0)
        slot = lax.rem(lax.broadcasted_iota(jnp.int32, (1, per_chunk), 1), slots)
        picked = jnp.zeros((1, per_chunk), jnp.float32)
        for k in range(slots):
            picked += jnp.where(slot == k, dot(pick_ref[k].astype(jnp.float32), owned), 0.0)
        token = lax.broadcasted_iota(jnp.int32, (total.shape[0], per_chunk), 0)
        chosen = bf16(jnp.where(token.astype(jnp.float32) == picked, 1.0, 0.0))
        for t in range(tiles):
            cols = slice(t * 512, (t + 1) * 512)
            total[:, cols] += dot(chosen, drow[:, cols])
        return carry

    lax.fori_loop(0, CHUNKS, combine, 0)
    dtok_ref[...] = bf16(total[...])

    local_wait(gback, g_recv)
    eye = jnp.where(
        lax.broadcasted_iota(jnp.int32, (8, LANES), 0)
        == lax.broadcasted_iota(jnp.int32, (8, LANES), 1),
        1.0,
        0.0,
    )
    by_slot = lax.dot_general(
        eye, gback[...].reshape(N, LANES), (((1,), (1,)), ((), ())),
        precision=lax.Precision.HIGHEST, preferred_element_type=jnp.float32,
    )
    for k in range(slots):
        c = scale_vec[k : k + 1, :]
        inverse = jnp.where(c > 0.0, 1.0 / jnp.where(c > 0.0, c, 1.0), 0.0)
        dgate_ref[k : k + 1, :] = bf16(by_slot[k : k + 1, :] * inverse)
    local_wait(gsend.at[pl.ds(0, N - 1)], g_send)
    local_wait(send.at[pl.ds(0, N - 1)], f_send)
    local_wait(dsend.at[pl.ds(0, (N - 1) * slots)], r_send)


def write_out(*refs):
    count = len(refs) // 2
    copies = [
        pltpu.make_async_copy(refs[i], refs[count + i], refs[-1].at[i]) for i in range(count)
    ]
    for copy in copies:
        copy.start()
    for copy in copies:
        copy.wait()


def per_device(tokens, grad_out, gates, slot_index, slot_count, up_weight, down_weight):
    experts, slots = slot_index.shape[2:]
    held, width = tokens.shape[1:]
    half = up_weight.shape[2]
    total = experts * slots
    picks = jnp.transpose(slot_index[0], (2, 0, 1))

    vmem = pl.BlockSpec(memory_space=pltpu.VMEM)
    smem = pl.BlockSpec(memory_space=pltpu.SMEM)
    anywhere = pl.BlockSpec(memory_space=pl.ANY)
    hbm = pl.BlockSpec(memory_space=pltpu.HBM)
    low, full = jnp.bfloat16, jnp.float32

    def stay(array):
        return pltpu.with_memory_space_constraint(array, pltpu.HBM)

    dma = pltpu.SemaphoreType.DMA
    outs = (((held, width), low), ((slots, experts), low), ((width, half), low), ((half, width), low))
    results = pl.pallas_call(
        kernel,
        out_shape=tuple(pltpu.VMEM(shape, dtype) for shape, dtype in outs),
        in_specs=[smem, hbm, hbm, hbm, vmem, vmem, hbm, hbm],
        out_specs=(vmem, vmem, vmem, vmem),
        scratch_shapes=[
            pltpu.VMEM((slots, 1, experts), jnp.int32),
            pltpu.VMEM((slots, experts), low),
            pltpu.VMEM((1, experts), jnp.int32),
            pltpu.VMEM((held, SUB, LANES), low),
            pltpu.VMEM((held, SUB, LANES), low),
            pltpu.VMEM((8, experts), full),
            pltpu.SMEM((8, experts), full),
            pltpu.VMEM((experts, 1, LANES), full),
            pltpu.VMEM((experts, 2, slots, SUB, LANES), low),
            pltpu.VMEM((2, total, SUB, LANES), low),
            pltpu.VMEM((width, 2 * half), low),
            pltpu.VMEM((2 * half, width), low),
            pltpu.VMEM((total, width), low),
            pltpu.VMEM((total, width), low),
            pltpu.VMEM((total, 2 * half), low),
            pltpu.VMEM((total, 2 * half), low),
            pltpu.VMEM((PEERS * slots, width), low),
            pltpu.VMEM((total, SUB, LANES), low),
            pltpu.VMEM((total, SUB, LANES), low),
            pltpu.VMEM((experts, 1, LANES), full),
            pltpu.VMEM((width, half), full),
            pltpu.VMEM((width, half), full),
            pltpu.VMEM((half, width), full),
            pltpu.VMEM((half, width), full),
            pltpu.VMEM((held, width), full),
            pltpu.VMEM((SUB * SUB, SUB * SUB), low),
            dma((6,)),
            dma,
            dma((3,)),
            dma,
            dma((CHUNKS,)),
            dma,
            dma((CHUNKS,)),
            dma,
            dma,
            dma((2,)),
            dma((2,)),
        ],
        compiler_params=pltpu.CompilerParams(
            collective_id=0, has_side_effects=True, vmem_limit_bytes=50 << 20
        ),
    )(
        picks,
        stay(picks),
        stay(gates[0, 0].T),
        stay(slot_count[0]),
        tokens[0],
        grad_out[0],
        up_weight[0],
        down_weight[0],
    )
    d_tokens, d_gate, d_up, d_down = pl.pallas_call(
        write_out,
        out_shape=tuple(jax.ShapeDtypeStruct(shape, dtype) for shape, dtype in outs),
        in_specs=[vmem] * 4,
        out_specs=(anywhere,) * 4,
        scratch_shapes=[dma((4,))],
        compiler_params=pltpu.CompilerParams(vmem_limit_bytes=1 << 20),
    )(*(pltpu.with_memory_space_constraint(r, pltpu.VMEM) for r in results))
    return d_tokens[None], d_gate.T[None, None], d_up[None], d_down[None]


def solution(mesh):
    in_specs = (
        P("dp", "expert", None),
        P("dp", "expert", None),
        P("dp", "expert", None, None),
        P("dp", "expert", None, None),
        P("dp", "expert", None),
        P("expert", None, "dp"),
        P("expert", "dp", None),
    )
    out_specs = (
        P("dp", "expert", None),
        P("dp", "expert", None, None),
        P("expert", None, "dp"),
        P("expert", "dp", None),
    )
    return jax.shard_map(
        per_device, mesh=mesh, in_specs=in_specs, out_specs=out_specs, check_vma=False
    )
```

```python
import jax
import jax.numpy as jnp
from jax import lax
from jax.experimental import pallas as pl
from jax.experimental.pallas import tpu as pltpu
from jax.sharding import PartitionSpec as P

MESH = pl.DeviceIdType.MESH
NX, NY, NZ = 4, 4, 8
N = NX * NY * NZ
CHUNKS = NX
PEERS = NY * NZ
LANES = 128
SUB = 16
WIDE = SUB * LANES
PLANE = NX * NY
PAIRS = PLANE * PLANE
CAP = 96
FEW = 64
PARTS = 2


def place(me):
    return me % NX, (me // NX) % NY, me // (NX * NY)


def block_of(q, z, y):
    return q * PEERS + z * NY + y


def expert_of(q, z, y):
    return (z * NY + y) * NX + lax.rem(q - y + NX, NX)


def hop(i):
    return lax.rem(i, NZ), lax.div(i, NZ)


def bf16(v):
    return v.astype(jnp.bfloat16)


def dot(a, b, dims=((1,), (0,))):
    return lax.dot_general(a, b, (dims, ((), ())), preferred_element_type=jnp.float32)


def local_wait(ref, sem):
    pltpu.make_async_copy(ref, ref, sem).wait()


def padded_kernel(
    idx_ref, pick_hbm, gates_hbm, count_hbm, tok_ref, grad_ref, up_ref, down_ref,
    dtok_ref, dgate_ref, dup_ref, ddown_ref,
    pick_ref, gates_ref, count_ref, tok, grad, scale_vec, scale, gback,
    send, recv, wu, wd, rows_x, rows_g, act, dhid, drow, dsend, back, gsend,
    up_out, up_in, down_out, down_in, total, perm,
    w_sem, s_sem, small_sem, f_send, f_recv, r_send, r_recv, g_send, g_recv, d_send, d_recv,
):
    me = lax.axis_index("expert")
    core = lax.axis_index("dp")
    x, y, z = place(me)
    q_me = lax.rem(x + y, NX)
    slots = send.shape[2]
    per_chunk = PEERS * slots
    half = up_ref.shape[1]
    mine = pl.ds(pl.multiple_of(core * half, LANES), half)
    theirs = pl.ds(pl.multiple_of((1 - core) * half, LANES), half)
    partner = {"dp": 1 - core}

    barrier = pltpu.get_barrier_semaphore()
    pl.semaphore_signal(barrier, inc=1, device_id=partner, device_id_type=MESH)

    def greet(step, carry):
        pl.semaphore_signal(
            barrier, inc=1, device_id={"expert": lax.rem(me + step, N)}, device_id_type=MESH
        )
        return carry

    lax.fori_loop(1, N, greet, 0)

    own_up = pltpu.make_async_copy(up_ref, wu.at[:, mine], w_sem.at[0])
    own_up.start()
    own_down = pltpu.make_async_copy(down_ref, wd.at[mine, :], w_sem.at[1])
    own_down.start()

    small = [
        pltpu.make_async_copy(src, dst, small_sem.at[i])
        for i, (src, dst) in enumerate(
            ((gates_hbm, gates_ref), (count_hbm, count_ref), (pick_hbm, pick_ref))
        )
    ]
    for copy in small:
        copy.start()

    a = lax.broadcasted_iota(jnp.int32, (SUB * SUB, SUB * SUB), 0)
    b = lax.broadcasted_iota(jnp.int32, (SUB * SUB, SUB * SUB), 1)
    swap = (lax.rem(a, SUB) == lax.div(b, SUB)) & (lax.div(a, SUB) == lax.rem(b, SUB))
    perm[...] = jnp.where(swap, 1.0, 0.0).astype(jnp.bfloat16)

    for copy in small:
        copy.wait()
    scale_vec[...] = jnp.zeros_like(scale_vec)
    for k in range(slots):
        live = jnp.where(count_ref[...] > k, 1.0, 0.0)
        scale_vec[k : k + 1, :] = live * gates_ref[k : k + 1, :].astype(jnp.float32)
    to_scalars = pltpu.make_async_copy(scale_vec, scale, s_sem)
    to_scalars.start()

    def by_row(g, carry):
        r = pl.ds(pl.multiple_of(g * SUB, SUB), SUB)
        both = jnp.concatenate(
            [
                jnp.concatenate(
                    [ref[r, f * LANES : (f + 1) * LANES] for f in range(SUB)], axis=0
                )
                for ref in (tok_ref, grad_ref)
            ],
            axis=1,
        )
        out = bf16(dot(perm[...], both))
        tok[r] = out[:, :LANES].reshape(SUB, SUB, LANES)
        grad[r] = out[:, LANES:].reshape(SUB, SUB, LANES)
        return carry

    lax.fori_loop(0, tok.shape[0] // SUB, by_row, 0)
    to_scalars.wait()

    def fill(target):
        for k in range(slots):
            row = idx_ref[k, 0, target]
            send[target, 0, k] = tok[row]
            send[target, 1, k] = bf16(grad[row].astype(jnp.float32) * scale[k, target])

    pl.semaphore_wait(barrier, N)

    up_copy = pltpu.make_async_remote_copy(
        src_ref=up_ref, dst_ref=wu.at[:, mine], send_sem=w_sem.at[2], recv_sem=w_sem.at[3],
        device_id=partner, device_id_type=MESH,
    )
    up_copy.start()
    down_copy = pltpu.make_async_remote_copy(
        src_ref=down_ref, dst_ref=wd.at[mine, :], send_sem=w_sem.at[4], recv_sem=w_sem.at[5],
        device_id=partner, device_id_type=MESH,
    )
    down_copy.start()

    my_rows = pl.ds(block_of(q_me, z, y) * slots, slots)

    def push(n, carry):
        c = lax.div(n, PEERS)
        dz, dy = hop(lax.rem(n, PEERS))
        target = expert_of(lax.rem(q_me + c, NX), lax.rem(z + dz, NZ), lax.rem(y + dy, NY))
        fill(target)
        pltpu.make_async_remote_copy(
            src_ref=send.at[target], dst_ref=recv.at[:, my_rows],
            send_sem=f_send, recv_sem=f_recv.at[c],
            device_id={"expert": target}, device_id_type=MESH,
        ).start()
        return carry

    lax.fori_loop(1, N, push, 0)
    fill(me)
    pltpu.make_async_copy(send.at[me], recv.at[:, my_rows], f_recv.at[0]).start()

    own_up.wait()
    own_down.wait()
    up_copy.wait()
    down_copy.wait()

    groups = per_chunk // SUB
    grid_a = lax.broadcasted_iota(jnp.int32, (PEERS, per_chunk), 0)
    grid_b = lax.broadcasted_iota(jnp.int32, (PEERS, per_chunk), 1)
    to_peer = jnp.where(lax.div(grid_b, slots) == grid_a, 1.0, 0.0)
    row_id = lax.broadcasted_iota(jnp.int32, (per_chunk, LANES), 0)
    lane_id = lax.broadcasted_iota(jnp.int32, (per_chunk, LANES), 1)
    to_lane = jnp.where(lax.rem(row_id, slots) == lane_id, 1.0, 0.0)

    def chunk(c, carry):
        q = lax.rem(q_me - c + NX, NX)
        first = pl.multiple_of(q * per_chunk, SUB)
        local_wait(recv.at[:, pl.ds(0, per_chunk)], f_recv.at[c])

        def unpack(g, inner):
            r = pl.ds(pl.multiple_of(first + g * SUB, SUB), SUB)
            both = jnp.concatenate(
                [recv[0, r].reshape(SUB * SUB, LANES), recv[1, r].reshape(SUB * SUB, LANES)], axis=1
            )
            out = bf16(dot(perm[...], both))
            for f in range(SUB):
                part = out[f * SUB : (f + 1) * SUB]
                rows_x[r, f * LANES : (f + 1) * LANES] = part[:, :LANES]
                rows_g[r, f * LANES : (f + 1) * LANES] = part[:, LANES:]
            return inner

        lax.fori_loop(0, groups, unpack, 0)

        here = pl.ds(first, per_chunk)
        gate = jnp.zeros((per_chunk, 1), jnp.float32)
        for t in range(2 * half // 256):
            cols = slice(t * 256, (t + 1) * 256)
            hidden = dot(rows_x[here, :], wu[:, cols])
            upstream = dot(rows_g[here, :], wd[cols, :], ((1,), (1,)))
            s = jax.nn.sigmoid(hidden)
            activation = bf16(hidden * s)
            act[here, cols] = activation
            dhid[here, cols] = bf16(upstream * (s * (1.0 + hidden * (1.0 - s))))
            gate += jnp.sum(activation.astype(jnp.float32) * upstream, axis=1, keepdims=True)

        for t in range(WIDE // 512):
            cols = slice(t * 512, (t + 1) * 512)
            drow[:, cols] = bf16(dot(dhid[here, :], wu[cols, :], ((1,), (1,))))

        for g in range(0, groups, 2):
            pair = [
                jnp.concatenate(
                    [
                        drow[(g + h) * SUB : (g + h + 1) * SUB, f * LANES : (f + 1) * LANES]
                        for f in range(SUB)
                    ],
                    axis=0,
                )
                for h in range(2)
            ]
            out = bf16(dot(perm[...], jnp.concatenate(pair, axis=1)))
            for h in range(2):
                r = pl.ds(pl.multiple_of(first + (g + h) * SUB, SUB), SUB)
                dsend[r] = out[:, h * LANES : (h + 1) * LANES].reshape(SUB, SUB, LANES)

        @pl.when(c == 0)
        def _():
            pltpu.make_async_copy(dsend.at[my_rows], back.at[my_rows], r_recv.at[0]).start()

        def reply(i, inner):
            dz, dy = hop(i)
            zz, yy = lax.rem(z - dz + NZ, NZ), lax.rem(y - dy + NY, NY)
            source = pl.ds(block_of(q, zz, yy) * slots, slots)
            pltpu.make_async_remote_copy(
                src_ref=dsend.at[source], dst_ref=back.at[my_rows],
                send_sem=r_send, recv_sem=r_recv.at[c],
                device_id={"expert": expert_of(q, zz, yy)}, device_id_type=MESH,
            ).start()
            return inner

        lax.fori_loop(jnp.where(c == 0, 1, 0), PEERS, reply, 0)

        spread = lax.dot_general(
            to_peer, gate * to_lane, (((1,), (0,)), ((), ())),
            precision=lax.Precision.HIGHEST, preferred_element_type=jnp.float32,
        )
        gsend[pl.ds(q * PEERS, PEERS)] = spread.reshape(PEERS, 1, LANES)
        return carry

    lax.fori_loop(0, CHUNKS, chunk, 0)

    pltpu.make_async_copy(gsend.at[block_of(q_me, z, y)], gback.at[me], g_recv).start()

    def reply_gate(n, carry):
        c = lax.div(n, PEERS)
        dz, dy = hop(lax.rem(n, PEERS))
        q, zz, yy = lax.rem(q_me - c + NX, NX), lax.rem(z - dz + NZ, NZ), lax.rem(y - dy + NY, NY)
        pltpu.make_async_remote_copy(
            src_ref=gsend.at[block_of(q, zz, yy)], dst_ref=gback.at[me],
            send_sem=g_send, recv_sem=g_recv,
            device_id={"expert": expert_of(q, zz, yy)}, device_id_type=MESH,
        ).start()
        return carry

    lax.fori_loop(1, N, reply_gate, 0)

    tiles = WIDE // 512
    for t in range(tiles):
        cols = slice(t * 512, (t + 1) * 512)
        up_out[cols, :] = dot(rows_x[:, cols], dhid[:, theirs], ((0,), (0,)))
    up_swap = pltpu.make_async_remote_copy(
        src_ref=up_out, dst_ref=up_in, send_sem=d_send.at[0], recv_sem=d_recv.at[0],
        device_id=partner, device_id_type=MESH,
    )
    up_swap.start()
    for t in range(tiles):
        cols = slice(t * 512, (t + 1) * 512)
        down_out[:, cols] = dot(act[:, theirs], rows_g[:, cols], ((0,), (0,)))
    down_swap = pltpu.make_async_remote_copy(
        src_ref=down_out, dst_ref=down_in, send_sem=d_send.at[1], recv_sem=d_recv.at[1],
        device_id=partner, device_id_type=MESH,
    )
    down_swap.start()
    up_swap.wait()
    for t in range(tiles):
        cols = slice(t * 512, (t + 1) * 512)
        both = dot(rows_x[:, cols], dhid[:, mine], ((0,), (0,))) + up_in[cols, :]
        dup_ref[cols, :] = bf16(both)
    down_swap.wait()
    for t in range(tiles):
        cols = slice(t * 512, (t + 1) * 512)
        both = dot(act[:, mine], rows_g[:, cols], ((0,), (0,))) + down_in[:, cols]
        ddown_ref[:, cols] = bf16(both)

    total[...] = jnp.zeros_like(total)

    def combine(c, carry):
        q = lax.rem(q_me + c, NX)
        first = pl.multiple_of(q * per_chunk, SUB)
        local_wait(back.at[pl.ds(0, per_chunk)], r_recv.at[c])
        for g in range(0, groups, 2):
            pair = [
                back[pl.ds(pl.multiple_of(first + (g + h) * SUB, SUB), SUB)].reshape(SUB * SUB, LANES)
                for h in range(2)
            ]
            out = bf16(dot(perm[...], jnp.concatenate(pair, axis=1)))
            for h in range(2):
                for f in range(SUB):
                    drow[(g + h) * SUB : (g + h + 1) * SUB, f * LANES : (f + 1) * LANES] = out[
                        f * SUB : (f + 1) * SUB, h * LANES : (h + 1) * LANES
                    ]
        expert = lax.broadcasted_iota(jnp.int32, (N, per_chunk), 0)
        peer = lax.div(lax.broadcasted_iota(jnp.int32, (N, per_chunk), 1), slots)
        owner = expert_of(q, lax.div(peer, NY), lax.rem(peer, NY))
        owned = jnp.where(expert == owner, 1.0, 0.0)
        slot = lax.rem(lax.broadcasted_iota(jnp.int32, (1, per_chunk), 1), slots)
        picked = jnp.zeros((1, per_chunk), jnp.float32)
        for k in range(slots):
            picked += jnp.where(slot == k, dot(pick_ref[k].astype(jnp.float32), owned), 0.0)
        token = lax.broadcasted_iota(jnp.int32, (total.shape[0], per_chunk), 0)
        chosen = bf16(jnp.where(token.astype(jnp.float32) == picked, 1.0, 0.0))
        for t in range(tiles):
            cols = slice(t * 512, (t + 1) * 512)
            total[:, cols] += dot(chosen, drow[:, cols])
        return carry

    lax.fori_loop(0, CHUNKS, combine, 0)
    dtok_ref[...] = bf16(total[...])

    local_wait(gback, g_recv)
    eye = jnp.where(
        lax.broadcasted_iota(jnp.int32, (8, LANES), 0)
        == lax.broadcasted_iota(jnp.int32, (8, LANES), 1),
        1.0,
        0.0,
    )
    by_slot = lax.dot_general(
        eye, gback[...].reshape(N, LANES), (((1,), (1,)), ((), ())),
        precision=lax.Precision.HIGHEST, preferred_element_type=jnp.float32,
    )
    for k in range(slots):
        c = scale_vec[k : k + 1, :]
        inverse = jnp.where(c > 0.0, 1.0 / jnp.where(c > 0.0, c, 1.0), 0.0)
        dgate_ref[k : k + 1, :] = bf16(by_slot[k : k + 1, :] * inverse)
    local_wait(gsend.at[pl.ds(0, N - 1)], g_send)
    local_wait(send.at[pl.ds(0, N - 1)], f_send)
    local_wait(dsend.at[pl.ds(0, (N - 1) * slots)], r_send)


def lean_kernel(
    idx_ref, pick_hbm, gates_hbm, count_hbm, tok_ref, grad_ref, up_ref, down_ref,
    dtok_ref, dgate_ref, dup_ref, ddown_ref, flag_ref,
    pick_ref, gates_ref, count_ref, tok, grad, scale_vec, scale, gback,
    send, recv, wu, wd, rows_x, rows_g, act, dhid, drow, dsend, back, gsend,
    up_out, up_in, up_own, down_out, down_in, down_own, total, perm, above,
    third, r1_in, r1, meta1, live3, o2, r2, meta2, got2, o3, o3_out, r3,
    d3, rr1_in, rr1, ro2, rr2, ro3, ro3_out, d3back, pack_out, pack_in, pack_src, pack_dst, own_pick, flag_in,
    w_sem, s_sem, small_sem, f_send, f_recv, r_send, r_recv, g_send, g_recv, d_send, d_recv,
    t_send, t_recv, m_send, m_recv,
):
    me = lax.axis_index("expert")
    core = lax.axis_index("dp")
    x, y, z = place(me)
    p = lax.rem(me, PLANE)
    q_me = lax.rem(x + y, NX)
    slots = pick_ref.shape[0]
    direct = send.shape[2]
    quarter = PEERS * direct
    per_chunk = recv.shape[1] // PARTS
    half = up_ref.shape[1]
    mine = pl.ds(pl.multiple_of(core * half, LANES), half)
    partner = {"dp": 1 - core}
    my_lanes = pl.ds(pl.multiple_of(p * LANES, LANES), LANES)

    barrier = pltpu.get_barrier_semaphore()
    pl.semaphore_signal(barrier, inc=1, device_id=partner, device_id_type=MESH)

    def greet(step, carry):
        pl.semaphore_signal(
            barrier, inc=1, device_id={"expert": lax.rem(me + step, N)}, device_id_type=MESH
        )
        return carry

    lax.fori_loop(1, N, greet, 0)

    small = [
        pltpu.make_async_copy(src, dst, small_sem.at[i])
        for i, (src, dst) in enumerate(
            ((gates_hbm, gates_ref), (count_hbm, count_ref), (pick_hbm, pick_ref))
        )
    ]
    for copy in small:
        copy.start()
    own_up = pltpu.make_async_copy(up_ref, wu.at[:, mine], w_sem.at[0])
    own_up.start()
    own_down = pltpu.make_async_copy(down_ref, wd.at[mine, :], w_sem.at[1])
    own_down.start()

    a = lax.broadcasted_iota(jnp.int32, (PAIRS, PAIRS), 0)
    b = lax.broadcasted_iota(jnp.int32, (PAIRS, PAIRS), 1)
    swap = (lax.rem(a, SUB) == lax.div(b, SUB)) & (lax.div(a, SUB) == lax.rem(b, SUB))
    perm[...] = bf16(jnp.where(swap, 1.0, 0.0))
    above[...] = bf16(jnp.where(a < b, 1.0, 0.0))

    for copy in small:
        copy.wait()
    scale_vec[...] = jnp.zeros_like(scale_vec)
    for k in range(slots):
        live = jnp.where(count_ref[...] > k, 1.0, 0.0)
        scale_vec[k : k + 1, :] = live * gates_ref[k : k + 1, :].astype(jnp.float32)
        live3[0] = live
    to_scalars = pltpu.make_async_copy(scale_vec, scale, s_sem)
    to_scalars.start()

    few = lax.broadcasted_iota(jnp.int32, (FEW, N), 0).astype(jnp.float32)

    def squeeze(live):
        position = dot(bf16(live), above[:N, :N])
        return bf16(jnp.where((few == position) & (live > 0.5), 1.0, 0.0))

    token = lax.broadcasted_iota(jnp.int32, (tok.shape[0], N), 0)
    last_pick = jnp.where(token == pick_ref[slots - 1], 1.0, 0.0)
    last_scaled = bf16(last_pick * scale_vec[slots - 1 : slots, :])
    squeezed = squeeze(live3[0])
    last_pick = bf16(dot(bf16(last_pick), squeezed, ((1,), (1,))))
    last_scaled = bf16(dot(last_scaled, squeezed, ((1,), (1,))))
    own_pick[...] = last_pick
    for m in range(PLANE):
        lanes = slice(m * LANES, (m + 1) * LANES)
        third[m, :, :LANES] = bf16(dot(last_pick, tok_ref[:, lanes], ((0,), (0,))))
        third[m, :, LANES:] = bf16(dot(last_scaled, grad_ref[:, lanes], ((0,), (0,))))

    def by_row(g, carry):
        r = pl.ds(pl.multiple_of(g * SUB, SUB), SUB)
        both = jnp.concatenate(
            [
                jnp.concatenate([ref[r, f * LANES : (f + 1) * LANES] for f in range(SUB)], axis=0)
                for ref in (tok_ref, grad_ref)
            ],
            axis=1,
        )
        out = bf16(dot(perm[...], both))
        tok[r] = out[:, :LANES].reshape(SUB, SUB, LANES)
        grad[r] = out[:, LANES:].reshape(SUB, SUB, LANES)
        return carry

    lax.fori_loop(0, tok.shape[0] // SUB, by_row, 0)
    to_scalars.wait()

    def ship(src, dst, target, send_sem, recv_sem):
        pltpu.make_async_remote_copy(
            src_ref=src, dst_ref=dst, send_sem=send_sem, recv_sem=recv_sem,
            device_id={"expert": target}, device_id_type=MESH,
        ).start()

    def in_plane(src_of, dst, sem):
        def one(k, carry):
            peer = lax.rem(p + k, PLANE)
            ship(src_of(peer), dst, z * PLANE + peer, t_send.at[sem], t_recv.at[sem])
            return carry

        pltpu.make_async_copy(src_of(p), dst, t_recv.at[sem]).start()
        lax.fori_loop(1, PLANE, one, 0)

    def along_z(src, dst, sems):
        def one(k, carry):
            zz = lax.rem(z + k, NZ)
            ship(src.at[zz], dst.at[z], zz * PLANE + p, sems[0], sems[1])
            return carry

        pltpu.make_async_copy(src.at[z], dst.at[z], sems[1]).start()
        lax.fori_loop(1, NZ, one, 0)

    pl.semaphore_wait(barrier, N)

    in_plane(lambda m: third.at[m], r1_in.at[p], 0)

    def tell(k, carry):
        ship(live3.at[0], meta1.at[p], z * PLANE + lax.rem(p + k, PLANE), m_send.at[0], m_recv.at[0])
        return carry

    pltpu.make_async_copy(live3.at[0], meta1.at[p], m_recv.at[0]).start()
    lax.fori_loop(1, PLANE, tell, 0)

    up_copy = pltpu.make_async_remote_copy(
        src_ref=up_ref, dst_ref=wu.at[:, mine], send_sem=w_sem.at[2], recv_sem=w_sem.at[3],
        device_id=partner, device_id_type=MESH,
    )
    up_copy.start()
    down_copy = pltpu.make_async_remote_copy(
        src_ref=down_ref, dst_ref=wd.at[mine, :], send_sem=w_sem.at[4], recv_sem=w_sem.at[5],
        device_id=partner, device_id_type=MESH,
    )
    down_copy.start()

    my_peer = (z * NY + y) * direct

    def rows_at(c):
        return pl.ds(c * quarter + my_peer, direct)

    def fill(target):
        for k in range(direct):
            row = idx_ref[k, 0, target]
            send[target, 0, k] = tok[row]
            send[target, 1, k] = bf16(grad[row].astype(jnp.float32) * scale[k, target])

    def push(n, carry):
        c = lax.div(n, PEERS)
        dz, dy = hop(lax.rem(n, PEERS))
        target = expert_of(lax.rem(q_me + c, NX), lax.rem(z + dz, NZ), lax.rem(y + dy, NY))
        fill(target)
        ship(send.at[target], recv.at[:, rows_at(c)], target, f_send, f_recv.at[c * PARTS // NX])
        return carry

    def push_part(c):
        lax.fori_loop(max(1, c * PEERS), (c + 1) * PEERS, push, 0)
        if c == 0:
            fill(me)
            pltpu.make_async_copy(send.at[me], recv.at[:, rows_at(0)], f_recv.at[0]).start()

    row_a = lax.broadcasted_iota(jnp.int32, (N, PAIRS), 0)
    col_a = lax.broadcasted_iota(jnp.int32, (N, PAIRS), 1)
    col_p = lax.broadcasted_iota(jnp.int32, (PLANE, PAIRS), 1)
    row_p = lax.broadcasted_iota(jnp.int32, (PLANE, PAIRS), 0)
    rank = lax.broadcasted_iota(jnp.int32, (CAP, PAIRS), 0).astype(jnp.float32)

    def pack(zz, over):
        pick_plane = jnp.where(row_a == zz * PLANE + lax.rem(col_a, PLANE), 1.0, 0.0)
        spread = dot(meta1[...].reshape(PLANE, LANES), pick_plane)
        own = jnp.where(lax.div(col_p, PLANE) == row_p, spread, 0.0)
        live = jnp.sum(own, axis=0, keepdims=True)
        position = dot(bf16(live), above[...])
        chosen = bf16(jnp.where((rank == position) & (live > 0.5), 1.0, 0.0))
        pack_out[zz] = chosen
        meta2[zz, :, :PAIRS] = live
        source = jnp.concatenate(
            [r1[j, pl.ds(pl.multiple_of(zz * PLANE, PLANE), PLANE)] for j in range(PLANE)], axis=0
        )
        o2[zz] = bf16(dot(chosen, source))
        return jnp.maximum(over, jnp.sum(live, axis=1, keepdims=True))

    def send_thirds():
        local_wait(meta1, m_recv.at[0])
        local_wait(r1_in, t_recv.at[0])

        def widen(j, crowd):
            live = meta1[j]
            chosen = squeeze(live)
            pack_src[j] = chosen
            r1[j] = bf16(dot(chosen, r1_in[j], ((0,), (0,))))
            return jnp.maximum(crowd, jnp.sum(live, axis=1, keepdims=True))

        crowd = lax.fori_loop(0, PLANE, widen, jnp.zeros((1, 1), jnp.float32))
        most = lax.fori_loop(0, NZ, pack, jnp.zeros((1, 1), jnp.float32))
        over = jnp.broadcast_to(jnp.where((most > CAP) | (crowd > FEW), 1.0, 0.0), (1, LANES))
        for j in range(NZ):
            meta2[j, :, PAIRS:] = over
        along_z(meta2, got2, (m_send.at[1], m_recv.at[1]))
        along_z(o2, r2, (t_send.at[1], t_recv.at[1]))

    def compute(first, rows):
        here = pl.ds(first, rows)
        gate = jnp.zeros((rows, 1), jnp.float32)
        for t in range(2 * half // 256):
            cols = slice(t * 256, (t + 1) * 256)
            hidden = dot(rows_x[here, :], wu[:, cols])
            upstream = dot(rows_g[here, :], wd[cols, :], ((1,), (1,)))
            s = jax.nn.sigmoid(hidden)
            activation = bf16(hidden * s)
            act[here, cols] = activation
            dhid[here, cols] = bf16(upstream * (s * (1.0 + hidden * (1.0 - s))))
            gate += jnp.sum(activation.astype(jnp.float32) * upstream, axis=1, keepdims=True)
        return gate

    def row_grads(first, rows, out):
        for t in range(WIDE // 512):
            cols = slice(t * 512, (t + 1) * 512)
            out[:rows, cols] = bf16(dot(dhid[pl.ds(first, rows), :], wu[cols, :], ((1,), (1,))))

    def peer_ids(c, sign, shape, axis):
        row = lax.broadcasted_iota(jnp.int32, shape, axis) + c * per_chunk
        turn = lax.div(row, quarter)
        peer = lax.div(lax.rem(row, quarter), direct)
        q = lax.rem(q_me + sign * turn + NX, NX)
        return expert_of(q, lax.div(peer, NY), lax.rem(peer, NY)), lax.rem(row, direct)

    groups = per_chunk // SUB
    gsend[...] = jnp.zeros_like(gsend)

    def chunk(c):
        first = c * per_chunk
        local_wait(recv.at[:, pl.ds(0, per_chunk)], f_recv.at[c])

        def unpack(g, inner):
            r = pl.ds(pl.multiple_of(first + g * SUB, SUB), SUB)
            both = jnp.concatenate(
                [recv[0, r].reshape(PAIRS, LANES), recv[1, r].reshape(PAIRS, LANES)], axis=1
            )
            out = bf16(dot(perm[...], both))
            for f in range(SUB):
                part = out[f * SUB : (f + 1) * SUB]
                rows_x[r, f * LANES : (f + 1) * LANES] = part[:, :LANES]
                rows_g[r, f * LANES : (f + 1) * LANES] = part[:, LANES:]
            return inner

        lax.fori_loop(0, groups, unpack, 0)
        gate = compute(first, per_chunk)
        row_grads(first, per_chunk, drow)

        for g in range(0, groups, 2):
            pair = [
                jnp.concatenate(
                    [
                        drow[(g + h) * SUB : (g + h + 1) * SUB, f * LANES : (f + 1) * LANES]
                        for f in range(SUB)
                    ],
                    axis=0,
                )
                for h in range(2)
            ]
            out = bf16(dot(perm[...], jnp.concatenate(pair, axis=1)))
            for h in range(2):
                r = pl.ds(first + (g + h) * SUB, SUB)
                dsend[r] = out[:, h * LANES : (h + 1) * LANES].reshape(SUB, SUB, LANES)

        if c == 0:
            pltpu.make_async_copy(dsend.at[rows_at(0)], back.at[rows_at(0)], r_recv.at[0]).start()

        def reply(n, inner):
            turn = lax.div(n, PEERS)
            dz, dy = hop(lax.rem(n, PEERS))
            q = lax.rem(q_me - turn + NX, NX)
            zz, yy = lax.rem(z - dz + NZ, NZ), lax.rem(y - dy + NY, NY)
            source = pl.ds(turn * quarter + (zz * NY + yy) * direct, direct)
            ship(
                dsend.at[source], back.at[rows_at(turn)], expert_of(q, zz, yy),
                r_send, r_recv.at[c],
            )
            return inner

        span = N // PARTS
        lax.fori_loop(max(1, c * span), (c + 1) * span, reply, 0)

        owner, slot = peer_ids(c, -1, (1, per_chunk), 1)
        to_source = jnp.where(
            lax.broadcasted_iota(jnp.int32, (N, per_chunk), 0) == owner, 1.0, 0.0
        )
        _, slot = peer_ids(c, -1, (per_chunk, LANES), 0)
        to_lane = lax.broadcasted_iota(jnp.int32, (per_chunk, LANES), 1) == slot
        spread = lax.dot_general(
            to_source, jnp.where(to_lane, gate, 0.0), (((1,), (0,)), ((), ())),
            precision=lax.Precision.HIGHEST, preferred_element_type=jnp.float32,
        )
        gsend[...] += spread.reshape(N, 1, LANES)

    def open_thirds():
        local_wait(got2, m_recv.at[1])
        local_wait(r2, t_recv.at[1])
        flag = jnp.zeros((1, LANES), jnp.float32)
        for j in range(NZ):
            flag = jnp.maximum(flag, got2[j, :, PAIRS:])
        flag_ref[...] = jnp.broadcast_to(flag, flag_ref.shape)

        def one(zz, carry):
            live = got2[zz][:, :PAIRS]
            position = dot(bf16(live), above[...])
            live = dot(bf16(live), perm[...])
            position = dot(bf16(position), perm[...])
            chosen = bf16(jnp.where((rank == position) & (live > 0.5), 1.0, 0.0))
            pack_in[zz] = chosen
            out = bf16(dot(chosen, r2[zz], ((0,), (0,))))
            for j in range(PLANE):
                o3[j, pl.ds(pl.multiple_of(zz * PLANE, PLANE), PLANE)] = out[j * SUB : (j + 1) * SUB]
            return carry

        lax.fori_loop(0, NZ, one, 0)
        flags = got2[...].reshape(NZ, PAIRS + LANES)[:, :PAIRS]
        row_s = lax.broadcasted_iota(jnp.int32, (PAIRS, N), 0)
        col_s = lax.broadcasted_iota(jnp.int32, (PAIRS, N), 1)
        row_z = lax.broadcasted_iota(jnp.int32, (NZ, N), 0)
        col_z = lax.broadcasted_iota(jnp.int32, (NZ, N), 1)

        def narrow(j, carry):
            here = (lax.rem(row_s, PLANE) == j) & (lax.div(row_s, PLANE) == lax.rem(col_s, PLANE))
            spread = dot(flags, jnp.where(here, 1.0, 0.0))
            live = jnp.where(lax.div(col_z, PLANE) == row_z, spread, 0.0)
            chosen = squeeze(jnp.sum(live, axis=0, keepdims=True))
            pack_dst[j] = chosen
            o3_out[j] = bf16(dot(chosen, o3[j]))
            return carry

        lax.fori_loop(0, PLANE, narrow, 0)
        in_plane(lambda m: o3_out.at[m], r3.at[p], 2)

    def run_thirds():
        local_wait(r3, t_recv.at[2])
        first = recv.shape[1]
        for m in range(PLANE):
            lanes = slice(m * LANES, (m + 1) * LANES)
            rows_x[first:, lanes] = r3[m, :, :LANES]
            rows_g[first:, lanes] = r3[m, :, LANES:]
        gate = compute(first, FEW)
        row_grads(first, FEW, d3)
        in_plane(
            lambda m: d3.at[:, pl.ds(pl.multiple_of(m * LANES, LANES), LANES)], rr1_in.at[p], 3
        )
        lane = lax.broadcasted_iota(jnp.int32, (FEW, LANES), 1)
        spread = lax.dot_general(
            pack_dst[p].astype(jnp.float32), jnp.where(lane == slots - 1, gate, 0.0),
            (((0,), (0,)), ((), ())),
            precision=lax.Precision.HIGHEST, preferred_element_type=jnp.float32,
        )
        gsend[...] += spread.reshape(N, 1, LANES)

    def pack_back():
        local_wait(rr1_in, t_recv.at[3])

        def widen(j, carry):
            rr1[j] = bf16(dot(pack_dst[j], rr1_in[j], ((0,), (0,))))
            return carry

        lax.fori_loop(0, PLANE, widen, 0)

        def one(zz, carry):
            source = jnp.concatenate(
                [rr1[j, pl.ds(pl.multiple_of(zz * PLANE, PLANE), PLANE)] for j in range(PLANE)], axis=0
            )
            ro2[zz] = bf16(dot(pack_in[zz], source))
            return carry

        lax.fori_loop(0, NZ, one, 0)
        along_z(ro2, rr2, (t_send.at[4], t_recv.at[4]))

    def open_back():
        local_wait(rr2, t_recv.at[4])

        def one(zz, carry):
            out = bf16(dot(pack_out[zz], rr2[zz], ((0,), (0,))))
            for j in range(PLANE):
                ro3[j, pl.ds(pl.multiple_of(zz * PLANE, PLANE), PLANE)] = out[j * SUB : (j + 1) * SUB]
            return carry

        lax.fori_loop(0, NZ, one, 0)

        def narrow(j, carry):
            ro3_out[j] = bf16(dot(pack_src[j], ro3[j]))
            return carry

        lax.fori_loop(0, PLANE, narrow, 0)
        in_plane(lambda m: ro3_out.at[m], d3back.at[:, my_lanes], 5)

    def weights_here():
        own_up.wait()
        own_down.wait()
        up_copy.wait()
        down_copy.wait()

    tiles = WIDE // 512

    def weight_grads():
        pltpu.make_async_copy(gsend.at[me], gback.at[me], g_recv).start()

        def reply_gate(n, carry):
            target = lax.rem(me + n, N)
            ship(gsend.at[target], gback.at[me], target, g_send, g_recv)
            return carry

        lax.fori_loop(1, N, reply_gate, 0)

        flag_swap = pltpu.make_async_remote_copy(
            src_ref=flag_ref, dst_ref=flag_in, send_sem=d_send.at[2], recv_sem=d_recv.at[2],
            device_id=partner, device_id_type=MESH,
        )
        flag_swap.start()

        first_core = core == 0
        for t in range(tiles):
            cols = slice(t * 512, (t + 1) * 512)
            whole = dot(rows_x[:, cols], dhid[...], ((0,), (0,)))
            left, right = whole[:, :half], whole[:, half:]
            up_out[cols, :] = bf16(jnp.where(first_core, right, left))
            up_own[cols, :] = jnp.where(first_core, left, right)
        up_swap = pltpu.make_async_remote_copy(
            src_ref=up_out, dst_ref=up_in, send_sem=d_send.at[0], recv_sem=d_recv.at[0],
            device_id=partner, device_id_type=MESH,
        )
        up_swap.start()
        for t in range(tiles):
            cols = slice(t * 512, (t + 1) * 512)
            whole = dot(act[...], rows_g[:, cols], ((0,), (0,)))
            left, right = whole[:half], whole[half:]
            down_out[:, cols] = bf16(jnp.where(first_core, right, left))
            down_own[:, cols] = jnp.where(first_core, left, right)
        down_swap = pltpu.make_async_remote_copy(
            src_ref=down_out, dst_ref=down_in, send_sem=d_send.at[1], recv_sem=d_recv.at[1],
            device_id=partner, device_id_type=MESH,
        )
        down_swap.start()
        up_swap.wait()
        for t in range(tiles):
            cols = slice(t * 512, (t + 1) * 512)
            dup_ref[cols, :] = bf16(up_own[cols, :] + up_in[cols, :].astype(jnp.float32))
        down_swap.wait()
        for t in range(tiles):
            cols = slice(t * 512, (t + 1) * 512)
            ddown_ref[:, cols] = bf16(down_own[:, cols] + down_in[:, cols].astype(jnp.float32))
        flag_swap.wait()
        flag_ref[...] = jnp.maximum(flag_ref[...], flag_in[...])

    def finish_rows():
        total[...] = jnp.zeros_like(total)

        def combine(c, carry):
            first = pl.multiple_of(c * per_chunk, SUB)
            local_wait(back.at[pl.ds(0, per_chunk)], r_recv.at[c])
            for g in range(0, groups, 2):
                pair = [
                    back[pl.ds(pl.multiple_of(first + (g + h) * SUB, SUB), SUB)].reshape(PAIRS, LANES)
                    for h in range(2)
                ]
                out = bf16(dot(perm[...], jnp.concatenate(pair, axis=1)))
                for h in range(2):
                    for f in range(SUB):
                        drow[(g + h) * SUB : (g + h + 1) * SUB, f * LANES : (f + 1) * LANES] = out[
                            f * SUB : (f + 1) * SUB, h * LANES : (h + 1) * LANES
                        ]
            owner, slot = peer_ids(c, 1, (1, per_chunk), 1)
            owned = jnp.where(
                lax.broadcasted_iota(jnp.int32, (N, per_chunk), 0) == owner, 1.0, 0.0
            )
            picked = jnp.zeros((1, per_chunk), jnp.float32)
            for k in range(direct):
                picked += jnp.where(slot == k, dot(pick_ref[k].astype(jnp.float32), owned), 0.0)
            rows = lax.broadcasted_iota(jnp.int32, (total.shape[0], per_chunk), 0)
            chosen = bf16(jnp.where(rows.astype(jnp.float32) == picked, 1.0, 0.0))
            for t in range(tiles):
                cols = slice(t * 512, (t + 1) * 512)
                total[:, cols] += dot(chosen, drow[:, cols])
            return carry

        lax.fori_loop(0, PARTS, combine, 0)
        local_wait(d3back, t_recv.at[5])
        for t in range(tiles):
            cols = slice(t * 512, (t + 1) * 512)
            dtok_ref[:, cols] = bf16(total[:, cols] + dot(own_pick[...], d3back[:, cols]))

    push_part(0)
    push_part(1)
    send_thirds()
    push_part(2)
    push_part(3)
    weights_here()
    chunk(0)
    open_thirds()
    run_thirds()
    chunk(1)
    pack_back()
    weight_grads()
    open_back()
    finish_rows()

    local_wait(gback, g_recv)
    eye = jnp.where(
        lax.broadcasted_iota(jnp.int32, (8, LANES), 0)
        == lax.broadcasted_iota(jnp.int32, (8, LANES), 1),
        1.0,
        0.0,
    )
    by_slot = lax.dot_general(
        eye, gback[...].reshape(N, LANES), (((1,), (1,)), ((), ())),
        precision=lax.Precision.HIGHEST, preferred_element_type=jnp.float32,
    )
    for k in range(slots):
        c = scale_vec[k : k + 1, :]
        inverse = jnp.where(c > 0.0, 1.0 / jnp.where(c > 0.0, c, 1.0), 0.0)
        dgate_ref[k : k + 1, :] = bf16(by_slot[k : k + 1, :] * inverse)

    local_wait(gsend.at[pl.ds(0, N - 1)], g_send)
    local_wait(send.at[pl.ds(0, N - 1)], f_send)
    local_wait(dsend.at[pl.ds(0, (N - 1) * direct)], r_send)
    local_wait(meta1.at[pl.ds(0, PLANE - 1)], m_send.at[0])
    local_wait(meta2.at[pl.ds(0, NZ - 1)], m_send.at[1])
    for i, ref in enumerate((third, o2, o3_out, rr1_in, ro2, ro3_out)):
        local_wait(ref.at[pl.ds(0, ref.shape[0] - 1)], t_send.at[i])


def write_out(*refs):
    count = len(refs) // 2
    copies = [
        pltpu.make_async_copy(refs[i], refs[count + i], refs[-1].at[i]) for i in range(count)
    ]
    for copy in copies:
        copy.start()
    for copy in copies:
        copy.wait()


def per_device(tokens, grad_out, gates, slot_index, slot_count, up_weight, down_weight):
    experts, slots = slot_index.shape[2:]
    held, width = tokens.shape[1:]
    half = up_weight.shape[2]
    total = experts * slots
    picks = jnp.transpose(slot_index[0], (2, 0, 1))

    vmem = pl.BlockSpec(memory_space=pltpu.VMEM)
    smem = pl.BlockSpec(memory_space=pltpu.SMEM)
    anywhere = pl.BlockSpec(memory_space=pl.ANY)
    hbm = pl.BlockSpec(memory_space=pltpu.HBM)
    low, full = jnp.bfloat16, jnp.float32

    def stay(array):
        return pltpu.with_memory_space_constraint(array, pltpu.HBM)

    dma = pltpu.SemaphoreType.DMA
    outs = (((held, width), low), ((slots, experts), low), ((width, half), low), ((half, width), low))
    operands = (
        picks,
        stay(picks),
        stay(gates[0, 0].T),
        stay(slot_count[0]),
        tokens[0],
        grad_out[0],
        up_weight[0],
        down_weight[0],
    )
    small = [
        pltpu.VMEM((slots, 1, experts), jnp.int32),
        pltpu.VMEM((slots, experts), low),
        pltpu.VMEM((1, experts), jnp.int32),
        pltpu.VMEM((held, SUB, LANES), low),
        pltpu.VMEM((held, SUB, LANES), low),
        pltpu.VMEM((8, experts), full),
        pltpu.SMEM((8, experts), full),
        pltpu.VMEM((experts, 1, LANES), full),
    ]

    def shared(sent, rows, parts, swapped):
        return [
            pltpu.VMEM((experts, 2, sent, SUB, LANES), low),
            pltpu.VMEM((2, sent * experts, SUB, LANES), low),
            pltpu.VMEM((width, 2 * half), low),
            pltpu.VMEM((2 * half, width), low),
            pltpu.VMEM((rows, width), low),
            pltpu.VMEM((rows, width), low),
            pltpu.VMEM((rows, 2 * half), low),
            pltpu.VMEM((rows, 2 * half), low),
            pltpu.VMEM((sent * experts // parts, width), low),
            pltpu.VMEM((sent * experts, SUB, LANES), low),
            pltpu.VMEM((sent * experts, SUB, LANES), low),
            pltpu.VMEM((experts, 1, LANES), full),
            *swapped,
            pltpu.VMEM((held, width), full),
            pltpu.VMEM((PAIRS, PAIRS), low),
        ]

    thirds = [
        pltpu.VMEM((PAIRS, PAIRS), low),
        pltpu.VMEM((PLANE, FEW, 2 * LANES), low),
        pltpu.VMEM((PLANE, FEW, 2 * LANES), low),
        pltpu.VMEM((PLANE, experts, 2 * LANES), low),
        pltpu.VMEM((PLANE, 1, LANES), full),
        pltpu.VMEM((1, 1, LANES), full),
        pltpu.VMEM((NZ, CAP, 2 * LANES), low),
        pltpu.VMEM((NZ, CAP, 2 * LANES), low),
        pltpu.VMEM((NZ, 1, PAIRS + LANES), full),
        pltpu.VMEM((NZ, 1, PAIRS + LANES), full),
        pltpu.VMEM((PLANE, experts, 2 * LANES), low),
        pltpu.VMEM((PLANE, FEW, 2 * LANES), low),
        pltpu.VMEM((PLANE, FEW, 2 * LANES), low),
        pltpu.VMEM((FEW, width), low),
        pltpu.VMEM((PLANE, FEW, LANES), low),
        pltpu.VMEM((PLANE, experts, LANES), low),
        pltpu.VMEM((NZ, CAP, LANES), low),
        pltpu.VMEM((NZ, CAP, LANES), low),
        pltpu.VMEM((PLANE, experts, LANES), low),
        pltpu.VMEM((PLANE, FEW, LANES), low),
        pltpu.VMEM((FEW, width), low),
        pltpu.VMEM((NZ, CAP, PAIRS), low),
        pltpu.VMEM((NZ, CAP, PAIRS), low),
        pltpu.VMEM((PLANE, FEW, experts), low),
        pltpu.VMEM((PLANE, FEW, experts), low),
        pltpu.VMEM((held, FEW), low),
        pltpu.VMEM((8, LANES), full),
    ]

    def sems(chunks, swaps):
        return [
            dma((6,)), dma, dma((3,)), dma, dma((chunks,)), dma, dma((chunks,)),
            dma, dma, dma((swaps,)), dma((swaps,)),
        ]

    def call(body, results, scratch, number):
        return pl.pallas_call(
            body,
            out_shape=tuple(pltpu.VMEM(shape, dtype) for shape, dtype in results),
            in_specs=[smem, hbm, hbm, hbm, vmem, vmem, hbm, hbm],
            out_specs=(vmem,) * len(results),
            scratch_shapes=scratch,
            compiler_params=pltpu.CompilerParams(
                collective_id=number, has_side_effects=True, vmem_limit_bytes=50 << 20
            ),
        )(*operands)

    def store(*results):
        return pl.pallas_call(
            write_out,
            out_shape=tuple(jax.ShapeDtypeStruct(shape, dtype) for shape, dtype in outs),
            in_specs=[vmem] * 4,
            out_specs=(anywhere,) * 4,
            scratch_shapes=[dma((4,))],
            compiler_params=pltpu.CompilerParams(vmem_limit_bytes=1 << 20),
        )(*(pltpu.with_memory_space_constraint(r, pltpu.VMEM) for r in results))

    *results, flag = call(
        lean_kernel,
        outs + (((8, LANES), full),),
        small + shared(slots - 1, (slots - 1) * experts + FEW, PARTS, [pltpu.VMEM(shape, kind) for shape in ((width, half), (half, width)) for kind in (low, low, full)]) + thirds + sems(PARTS, 3) + [dma((6,)), dma((6,)), dma((2,)), dma((2,))],
        0,
    )

    def padded(*unused):
        return store(*call(padded_kernel, outs, small + shared(slots, total, CHUNKS, [pltpu.VMEM(shape, full) for shape in ((width, half), (half, width)) for _ in range(2)]) + sems(CHUNKS, 2), 1))

    d_tokens, d_gate, d_up, d_down = lax.cond(flag[0, 0] > 0.5, padded, store, *results)
    return d_tokens[None], d_gate.T[None, None], d_up[None], d_down[None]


def solution(mesh):
    in_specs = (
        P("dp", "expert", None),
        P("dp", "expert", None),
        P("dp", "expert", None, None),
        P("dp", "expert", None, None),
        P("dp", "expert", None),
        P("expert", None, "dp"),
        P("expert", "dp", None),
    )
    out_specs = (
        P("dp", "expert", None),
        P("dp", "expert", None, None),
        P("expert", None, "dp"),
        P("expert", "dp", None),
    )
    return jax.shard_map(
        per_device, mesh=mesh, in_specs=in_specs, out_specs=out_specs, check_vma=False
    )
```

```python
import jax
import jax.numpy as jnp
from jax import lax
from jax.experimental import pallas as pl
from jax.experimental.pallas import tpu as pltpu
from jax.sharding import PartitionSpec as P

MESH = pl.DeviceIdType.MESH
NX, NY, NZ = 4, 4, 8
N = NX * NY * NZ
CHUNKS = NX
PEERS = NY * NZ
LANES = 128
SUB = 16
WIDE = SUB * LANES
PLANE = NX * NY
PAIRS = PLANE * PLANE
CAP = 96
FEW = 64
PARTS = 2


def place(me):
    return me % NX, (me // NX) % NY, me // (NX * NY)


def block_of(q, z, y):
    return q * PEERS + z * NY + y


def expert_of(q, z, y):
    return (z * NY + y) * NX + lax.rem(q - y + NX, NX)


def hop(i):
    return lax.rem(i, NZ), lax.div(i, NZ)


def bf16(v):
    return v.astype(jnp.bfloat16)


def dot(a, b, dims=((1,), (0,))):
    return lax.dot_general(a, b, (dims, ((), ())), preferred_element_type=jnp.float32)


def local_wait(ref, sem):
    pltpu.make_async_copy(ref, ref, sem).wait()


def padded_kernel(
    idx_ref, pick_hbm, gates_hbm, count_hbm, tok_ref, grad_ref, up_ref, down_ref,
    dtok_ref, dgate_ref, dup_ref, ddown_ref,
    pick_ref, gates_ref, count_ref, tok, grad, scale_vec, scale, gback,
    send, recv, wu, wd, rows_x, rows_g, act, dhid, drow, dsend, back, gsend,
    up_out, up_in, down_out, down_in, total, perm,
    w_sem, s_sem, small_sem, f_send, f_recv, r_send, r_recv, g_send, g_recv, d_send, d_recv,
):
    me = lax.axis_index("expert")
    core = lax.axis_index("dp")
    x, y, z = place(me)
    q_me = lax.rem(x + y, NX)
    slots = send.shape[2]
    per_chunk = PEERS * slots
    half = up_ref.shape[1]
    mine = pl.ds(pl.multiple_of(core * half, LANES), half)
    theirs = pl.ds(pl.multiple_of((1 - core) * half, LANES), half)
    partner = {"dp": 1 - core}

    barrier = pltpu.get_barrier_semaphore()
    pl.semaphore_signal(barrier, inc=1, device_id=partner, device_id_type=MESH)

    def greet(step, carry):
        pl.semaphore_signal(
            barrier, inc=1, device_id={"expert": lax.rem(me + step, N)}, device_id_type=MESH
        )
        return carry

    lax.fori_loop(1, N, greet, 0)

    own_up = pltpu.make_async_copy(up_ref, wu.at[:, mine], w_sem.at[0])
    own_up.start()
    own_down = pltpu.make_async_copy(down_ref, wd.at[mine, :], w_sem.at[1])
    own_down.start()

    small = [
        pltpu.make_async_copy(src, dst, small_sem.at[i])
        for i, (src, dst) in enumerate(
            ((gates_hbm, gates_ref), (count_hbm, count_ref), (pick_hbm, pick_ref))
        )
    ]
    for copy in small:
        copy.start()

    a = lax.broadcasted_iota(jnp.int32, (SUB * SUB, SUB * SUB), 0)
    b = lax.broadcasted_iota(jnp.int32, (SUB * SUB, SUB * SUB), 1)
    swap = (lax.rem(a, SUB) == lax.div(b, SUB)) & (lax.div(a, SUB) == lax.rem(b, SUB))
    perm[...] = jnp.where(swap, 1.0, 0.0).astype(jnp.bfloat16)

    for copy in small:
        copy.wait()
    scale_vec[...] = jnp.zeros_like(scale_vec)
    for k in range(slots):
        live = jnp.where(count_ref[...] > k, 1.0, 0.0)
        scale_vec[k : k + 1, :] = live * gates_ref[k : k + 1, :].astype(jnp.float32)
    to_scalars = pltpu.make_async_copy(scale_vec, scale, s_sem)
    to_scalars.start()

    def by_row(g, carry):
        r = pl.ds(pl.multiple_of(g * SUB, SUB), SUB)
        both = jnp.concatenate(
            [
                jnp.concatenate(
                    [ref[r, f * LANES : (f + 1) * LANES] for f in range(SUB)], axis=0
                )
                for ref in (tok_ref, grad_ref)
            ],
            axis=1,
        )
        out = bf16(dot(perm[...], both))
        tok[r] = out[:, :LANES].reshape(SUB, SUB, LANES)
        grad[r] = out[:, LANES:].reshape(SUB, SUB, LANES)
        return carry

    lax.fori_loop(0, tok.shape[0] // SUB, by_row, 0)
    to_scalars.wait()

    def fill(target):
        for k in range(slots):
            row = idx_ref[k, 0, target]
            send[target, 0, k] = tok[row]
            send[target, 1, k] = bf16(grad[row].astype(jnp.float32) * scale[k, target])

    pl.semaphore_wait(barrier, N)

    up_copy = pltpu.make_async_remote_copy(
        src_ref=up_ref, dst_ref=wu.at[:, mine], send_sem=w_sem.at[2], recv_sem=w_sem.at[3],
        device_id=partner, device_id_type=MESH,
    )
    up_copy.start()
    down_copy = pltpu.make_async_remote_copy(
        src_ref=down_ref, dst_ref=wd.at[mine, :], send_sem=w_sem.at[4], recv_sem=w_sem.at[5],
        device_id=partner, device_id_type=MESH,
    )
    down_copy.start()

    my_rows = pl.ds(block_of(q_me, z, y) * slots, slots)

    def push(n, carry):
        c = lax.div(n, PEERS)
        dz, dy = hop(lax.rem(n, PEERS))
        target = expert_of(lax.rem(q_me + c, NX), lax.rem(z + dz, NZ), lax.rem(y + dy, NY))
        fill(target)
        pltpu.make_async_remote_copy(
            src_ref=send.at[target], dst_ref=recv.at[:, my_rows],
            send_sem=f_send, recv_sem=f_recv.at[c],
            device_id={"expert": target}, device_id_type=MESH,
        ).start()
        return carry

    lax.fori_loop(1, N, push, 0)
    fill(me)
    pltpu.make_async_copy(send.at[me], recv.at[:, my_rows], f_recv.at[0]).start()

    own_up.wait()
    own_down.wait()
    up_copy.wait()
    down_copy.wait()

    groups = per_chunk // SUB
    grid_a = lax.broadcasted_iota(jnp.int32, (PEERS, per_chunk), 0)
    grid_b = lax.broadcasted_iota(jnp.int32, (PEERS, per_chunk), 1)
    to_peer = jnp.where(lax.div(grid_b, slots) == grid_a, 1.0, 0.0)
    row_id = lax.broadcasted_iota(jnp.int32, (per_chunk, LANES), 0)
    lane_id = lax.broadcasted_iota(jnp.int32, (per_chunk, LANES), 1)
    to_lane = jnp.where(lax.rem(row_id, slots) == lane_id, 1.0, 0.0)

    def chunk(c, carry):
        q = lax.rem(q_me - c + NX, NX)
        first = pl.multiple_of(q * per_chunk, SUB)
        local_wait(recv.at[:, pl.ds(0, per_chunk)], f_recv.at[c])

        def unpack(g, inner):
            r = pl.ds(pl.multiple_of(first + g * SUB, SUB), SUB)
            both = jnp.concatenate(
                [recv[0, r].reshape(SUB * SUB, LANES), recv[1, r].reshape(SUB * SUB, LANES)], axis=1
            )
            out = bf16(dot(perm[...], both))
            for f in range(SUB):
                part = out[f * SUB : (f + 1) * SUB]
                rows_x[r, f * LANES : (f + 1) * LANES] = part[:, :LANES]
                rows_g[r, f * LANES : (f + 1) * LANES] = part[:, LANES:]
            return inner

        lax.fori_loop(0, groups, unpack, 0)

        here = pl.ds(first, per_chunk)
        gate = jnp.zeros((per_chunk, 1), jnp.float32)
        for t in range(2 * half // 256):
            cols = slice(t * 256, (t + 1) * 256)
            hidden = dot(rows_x[here, :], wu[:, cols])
            upstream = dot(rows_g[here, :], wd[cols, :], ((1,), (1,)))
            s = jax.nn.sigmoid(hidden)
            activation = bf16(hidden * s)
            act[here, cols] = activation
            dhid[here, cols] = bf16(upstream * (s * (1.0 + hidden * (1.0 - s))))
            gate += jnp.sum(activation.astype(jnp.float32) * upstream, axis=1, keepdims=True)

        for t in range(WIDE // 512):
            cols = slice(t * 512, (t + 1) * 512)
            drow[:, cols] = bf16(dot(dhid[here, :], wu[cols, :], ((1,), (1,))))

        for g in range(0, groups, 2):
            pair = [
                jnp.concatenate(
                    [
                        drow[(g + h) * SUB : (g + h + 1) * SUB, f * LANES : (f + 1) * LANES]
                        for f in range(SUB)
                    ],
                    axis=0,
                )
                for h in range(2)
            ]
            out = bf16(dot(perm[...], jnp.concatenate(pair, axis=1)))
            for h in range(2):
                r = pl.ds(pl.multiple_of(first + (g + h) * SUB, SUB), SUB)
                dsend[r] = out[:, h * LANES : (h + 1) * LANES].reshape(SUB, SUB, LANES)

        @pl.when(c == 0)
        def _():
            pltpu.make_async_copy(dsend.at[my_rows], back.at[my_rows], r_recv.at[0]).start()

        def reply(i, inner):
            dz, dy = hop(i)
            zz, yy = lax.rem(z - dz + NZ, NZ), lax.rem(y - dy + NY, NY)
            source = pl.ds(block_of(q, zz, yy) * slots, slots)
            pltpu.make_async_remote_copy(
                src_ref=dsend.at[source], dst_ref=back.at[my_rows],
                send_sem=r_send, recv_sem=r_recv.at[c],
                device_id={"expert": expert_of(q, zz, yy)}, device_id_type=MESH,
            ).start()
            return inner

        lax.fori_loop(jnp.where(c == 0, 1, 0), PEERS, reply, 0)

        spread = lax.dot_general(
            to_peer, gate * to_lane, (((1,), (0,)), ((), ())),
            precision=lax.Precision.HIGHEST, preferred_element_type=jnp.float32,
        )
        gsend[pl.ds(q * PEERS, PEERS)] = spread.reshape(PEERS, 1, LANES)
        return carry

    lax.fori_loop(0, CHUNKS, chunk, 0)

    pltpu.make_async_copy(gsend.at[block_of(q_me, z, y)], gback.at[me], g_recv).start()

    def reply_gate(n, carry):
        c = lax.div(n, PEERS)
        dz, dy = hop(lax.rem(n, PEERS))
        q, zz, yy = lax.rem(q_me - c + NX, NX), lax.rem(z - dz + NZ, NZ), lax.rem(y - dy + NY, NY)
        pltpu.make_async_remote_copy(
            src_ref=gsend.at[block_of(q, zz, yy)], dst_ref=gback.at[me],
            send_sem=g_send, recv_sem=g_recv,
            device_id={"expert": expert_of(q, zz, yy)}, device_id_type=MESH,
        ).start()
        return carry

    lax.fori_loop(1, N, reply_gate, 0)

    tiles = WIDE // 512
    for t in range(tiles):
        cols = slice(t * 512, (t + 1) * 512)
        up_out[cols, :] = dot(rows_x[:, cols], dhid[:, theirs], ((0,), (0,)))
    up_swap = pltpu.make_async_remote_copy(
        src_ref=up_out, dst_ref=up_in, send_sem=d_send.at[0], recv_sem=d_recv.at[0],
        device_id=partner, device_id_type=MESH,
    )
    up_swap.start()
    for t in range(tiles):
        cols = slice(t * 512, (t + 1) * 512)
        down_out[:, cols] = dot(act[:, theirs], rows_g[:, cols], ((0,), (0,)))
    down_swap = pltpu.make_async_remote_copy(
        src_ref=down_out, dst_ref=down_in, send_sem=d_send.at[1], recv_sem=d_recv.at[1],
        device_id=partner, device_id_type=MESH,
    )
    down_swap.start()
    up_swap.wait()
    for t in range(tiles):
        cols = slice(t * 512, (t + 1) * 512)
        both = dot(rows_x[:, cols], dhid[:, mine], ((0,), (0,))) + up_in[cols, :]
        dup_ref[cols, :] = bf16(both)
    down_swap.wait()
    for t in range(tiles):
        cols = slice(t * 512, (t + 1) * 512)
        both = dot(act[:, mine], rows_g[:, cols], ((0,), (0,))) + down_in[:, cols]
        ddown_ref[:, cols] = bf16(both)

    total[...] = jnp.zeros_like(total)

    def combine(c, carry):
        q = lax.rem(q_me + c, NX)
        first = pl.multiple_of(q * per_chunk, SUB)
        local_wait(back.at[pl.ds(0, per_chunk)], r_recv.at[c])
        for g in range(0, groups, 2):
            pair = [
                back[pl.ds(pl.multiple_of(first + (g + h) * SUB, SUB), SUB)].reshape(SUB * SUB, LANES)
                for h in range(2)
            ]
            out = bf16(dot(perm[...], jnp.concatenate(pair, axis=1)))
            for h in range(2):
                for f in range(SUB):
                    drow[(g + h) * SUB : (g + h + 1) * SUB, f * LANES : (f + 1) * LANES] = out[
                        f * SUB : (f + 1) * SUB, h * LANES : (h + 1) * LANES
                    ]
        expert = lax.broadcasted_iota(jnp.int32, (N, per_chunk), 0)
        peer = lax.div(lax.broadcasted_iota(jnp.int32, (N, per_chunk), 1), slots)
        owner = expert_of(q, lax.div(peer, NY), lax.rem(peer, NY))
        owned = jnp.where(expert == owner, 1.0, 0.0)
        slot = lax.rem(lax.broadcasted_iota(jnp.int32, (1, per_chunk), 1), slots)
        picked = jnp.zeros((1, per_chunk), jnp.float32)
        for k in range(slots):
            picked += jnp.where(slot == k, dot(pick_ref[k].astype(jnp.float32), owned), 0.0)
        token = lax.broadcasted_iota(jnp.int32, (total.shape[0], per_chunk), 0)
        chosen = bf16(jnp.where(token.astype(jnp.float32) == picked, 1.0, 0.0))
        for t in range(tiles):
            cols = slice(t * 512, (t + 1) * 512)
            total[:, cols] += dot(chosen, drow[:, cols])
        return carry

    lax.fori_loop(0, CHUNKS, combine, 0)
    dtok_ref[...] = bf16(total[...])

    local_wait(gback, g_recv)
    eye = jnp.where(
        lax.broadcasted_iota(jnp.int32, (8, LANES), 0)
        == lax.broadcasted_iota(jnp.int32, (8, LANES), 1),
        1.0,
        0.0,
    )
    by_slot = lax.dot_general(
        eye, gback[...].reshape(N, LANES), (((1,), (1,)), ((), ())),
        precision=lax.Precision.HIGHEST, preferred_element_type=jnp.float32,
    )
    for k in range(slots):
        c = scale_vec[k : k + 1, :]
        inverse = jnp.where(c > 0.0, 1.0 / jnp.where(c > 0.0, c, 1.0), 0.0)
        dgate_ref[k : k + 1, :] = bf16(by_slot[k : k + 1, :] * inverse)
    local_wait(gsend.at[pl.ds(0, N - 1)], g_send)
    local_wait(send.at[pl.ds(0, N - 1)], f_send)
    local_wait(dsend.at[pl.ds(0, (N - 1) * slots)], r_send)


def lean_kernel(
    idx_ref, pick_hbm, gates_hbm, count_hbm, tok_ref, grad_ref, up_ref, down_ref,
    dtok_ref, dgate_ref, dup_ref, ddown_ref, flag_ref,
    pick_ref, gates_ref, count_ref, tok, grad, scale_vec, scale, gback,
    send, recv, wu, wd, rows_x, rows_g, act, dhid, drow, dsend, back, gsend,
    up_out, up_in, up_own, down_out, down_in, down_own, total, perm, above,
    third, r1_in, r1, meta1, live3, o2, r2, meta2, got2, o3, o3_out, r3,
    d3, rr1_in, rr1, ro2, rr2, ro3, ro3_out, d3back, pack_out, pack_in, pack_src, pack_dst, own_pick, flag_in,
    w_sem, s_sem, small_sem, f_send, f_recv, r_send, r_recv, g_send, g_recv, d_send, d_recv,
    t_send, t_recv, m_send, m_recv,
):
    me = lax.axis_index("expert")
    core = lax.axis_index("dp")
    x, y, z = place(me)
    p = lax.rem(me, PLANE)
    q_me = lax.rem(x + y, NX)
    slots = pick_ref.shape[0]
    direct = send.shape[2]
    quarter = PEERS * direct
    per_chunk = recv.shape[1] // PARTS
    half = up_ref.shape[1]
    mine = pl.ds(pl.multiple_of(core * half, LANES), half)
    partner = {"dp": 1 - core}
    my_lanes = pl.ds(pl.multiple_of(p * LANES, LANES), LANES)

    barrier = pltpu.get_barrier_semaphore()
    pl.semaphore_signal(barrier, inc=1, device_id=partner, device_id_type=MESH)

    def greet(step, carry):
        pl.semaphore_signal(
            barrier, inc=1, device_id={"expert": lax.rem(me + step, N)}, device_id_type=MESH
        )
        return carry

    lax.fori_loop(1, N, greet, 0)

    small = [
        pltpu.make_async_copy(src, dst, small_sem.at[i])
        for i, (src, dst) in enumerate(
            ((gates_hbm, gates_ref), (count_hbm, count_ref), (pick_hbm, pick_ref))
        )
    ]
    for copy in small:
        copy.start()
    own_up = pltpu.make_async_copy(up_ref, wu.at[:, mine], w_sem.at[0])
    own_up.start()
    own_down = pltpu.make_async_copy(down_ref, wd.at[mine, :], w_sem.at[1])
    own_down.start()

    a = lax.broadcasted_iota(jnp.int32, (PAIRS, PAIRS), 0)
    b = lax.broadcasted_iota(jnp.int32, (PAIRS, PAIRS), 1)
    above[...] = bf16(jnp.where(a < b, 1.0, 0.0))

    for copy in small:
        copy.wait()
    scale_vec[...] = jnp.zeros_like(scale_vec)
    for k in range(slots):
        live = jnp.where(count_ref[...] > k, 1.0, 0.0)
        scale_vec[k : k + 1, :] = live * gates_ref[k : k + 1, :].astype(jnp.float32)
        live3[0] = live
    to_scalars = pltpu.make_async_copy(scale_vec, scale, s_sem)
    to_scalars.start()

    few = lax.broadcasted_iota(jnp.int32, (FEW, N), 0).astype(jnp.float32)

    def squeeze(live):
        position = dot(bf16(live), above[:N, :N])
        return bf16(jnp.where((few == position) & (live > 0.5), 1.0, 0.0))

    token = lax.broadcasted_iota(jnp.int32, (tok.shape[0], N), 0)
    last_pick = jnp.where(token == pick_ref[slots - 1], 1.0, 0.0)
    last_scaled = bf16(last_pick * scale_vec[slots - 1 : slots, :])
    squeezed = squeeze(live3[0])
    own_pick[...] = bf16(dot(bf16(last_pick), squeezed, ((1,), (1,))))
    chosen_rows = bf16(dot(squeezed, bf16(last_pick), ((1,), (1,))))
    scaled_rows = bf16(dot(squeezed, last_scaled, ((1,), (1,))))
    for t in range(WIDE // 512):
        cols = slice(t * 512, (t + 1) * 512)
        row_part = bf16(dot(chosen_rows, tok_ref[:, cols]))
        grad_part = bf16(dot(scaled_rows, grad_ref[:, cols]))
        for m in range(512 // LANES):
            lanes = slice(m * LANES, (m + 1) * LANES)
            third[t * 512 // LANES + m, :, :LANES] = row_part[:, lanes]
            third[t * 512 // LANES + m, :, LANES:] = grad_part[:, lanes]

    def ship(src, dst, target, send_sem, recv_sem):
        pltpu.make_async_remote_copy(
            src_ref=src, dst_ref=dst, send_sem=send_sem, recv_sem=recv_sem,
            device_id={"expert": target}, device_id_type=MESH,
        ).start()

    def in_plane(src_of, dst, sem):
        def one(k, carry):
            peer = lax.rem(p + k, PLANE)
            ship(src_of(peer), dst, z * PLANE + peer, t_send.at[sem], t_recv.at[sem])
            return carry

        pltpu.make_async_copy(src_of(p), dst, t_recv.at[sem]).start()
        lax.fori_loop(1, PLANE, one, 0)

    def along_z(src, dst, sems):
        def one(k, carry):
            zz = lax.rem(z + k, NZ)
            ship(src.at[zz], dst.at[z], zz * PLANE + p, sems[0], sems[1])
            return carry

        pltpu.make_async_copy(src.at[z], dst.at[z], sems[1]).start()
        lax.fori_loop(1, NZ, one, 0)

    pl.semaphore_wait(barrier, N)

    in_plane(lambda m: third.at[m], r1_in.at[p], 0)

    def tell(k, carry):
        ship(live3.at[0], meta1.at[p], z * PLANE + lax.rem(p + k, PLANE), m_send.at[0], m_recv.at[0])
        return carry

    pltpu.make_async_copy(live3.at[0], meta1.at[p], m_recv.at[0]).start()
    lax.fori_loop(1, PLANE, tell, 0)

    up_copy = pltpu.make_async_remote_copy(
        src_ref=up_ref, dst_ref=wu.at[:, mine], send_sem=w_sem.at[2], recv_sem=w_sem.at[3],
        device_id=partner, device_id_type=MESH,
    )
    up_copy.start()
    down_copy = pltpu.make_async_remote_copy(
        src_ref=down_ref, dst_ref=wd.at[mine, :], send_sem=w_sem.at[4], recv_sem=w_sem.at[5],
        device_id=partner, device_id_type=MESH,
    )
    down_copy.start()

    swap = (lax.rem(a, SUB) == lax.div(b, SUB)) & (lax.div(a, SUB) == lax.rem(b, SUB))
    perm[...] = bf16(jnp.where(swap, 1.0, 0.0))

    def by_row(g, carry):
        r = pl.ds(pl.multiple_of(g * SUB, SUB), SUB)
        both = jnp.concatenate(
            [
                jnp.concatenate([ref[r, f * LANES : (f + 1) * LANES] for f in range(SUB)], axis=0)
                for ref in (tok_ref, grad_ref)
            ],
            axis=1,
        )
        out = bf16(dot(perm[...], both))
        tok[r] = out[:, :LANES].reshape(SUB, SUB, LANES)
        grad[r] = out[:, LANES:].reshape(SUB, SUB, LANES)
        return carry

    lax.fori_loop(0, tok.shape[0] // SUB, by_row, 0)
    to_scalars.wait()

    my_peer = (z * NY + y) * direct

    def rows_at(c):
        return pl.ds(c * quarter + my_peer, direct)

    def fill(target):
        for k in range(direct):
            row = idx_ref[k, 0, target]
            send[target, 0, k] = tok[row]
            send[target, 1, k] = bf16(grad[row].astype(jnp.float32) * scale[k, target])

    def push(n, carry):
        c = lax.div(n, PEERS)
        dz, dy = hop(lax.rem(n, PEERS))
        target = expert_of(lax.rem(q_me + c, NX), lax.rem(z + dz, NZ), lax.rem(y + dy, NY))
        fill(target)
        ship(send.at[target], recv.at[:, rows_at(c)], target, f_send, f_recv.at[c * PARTS // NX])
        return carry

    def push_part(c):
        lax.fori_loop(max(1, c * PEERS), (c + 1) * PEERS, push, 0)
        if c == 0:
            fill(me)
            pltpu.make_async_copy(send.at[me], recv.at[:, rows_at(0)], f_recv.at[0]).start()

    row_a = lax.broadcasted_iota(jnp.int32, (N, PAIRS), 0)
    col_a = lax.broadcasted_iota(jnp.int32, (N, PAIRS), 1)
    col_p = lax.broadcasted_iota(jnp.int32, (PLANE, PAIRS), 1)
    row_p = lax.broadcasted_iota(jnp.int32, (PLANE, PAIRS), 0)
    rank = lax.broadcasted_iota(jnp.int32, (CAP, PAIRS), 0).astype(jnp.float32)

    def pack(zz, over):
        pick_plane = jnp.where(row_a == zz * PLANE + lax.rem(col_a, PLANE), 1.0, 0.0)
        spread = dot(meta1[...].reshape(PLANE, LANES), pick_plane)
        own = jnp.where(lax.div(col_p, PLANE) == row_p, spread, 0.0)
        live = jnp.sum(own, axis=0, keepdims=True)
        position = dot(bf16(live), above[...])
        chosen = bf16(jnp.where((rank == position) & (live > 0.5), 1.0, 0.0))
        pack_out[zz] = chosen
        meta2[zz, :, :PAIRS] = live
        source = jnp.concatenate(
            [r1[j, pl.ds(pl.multiple_of(zz * PLANE, PLANE), PLANE)] for j in range(PLANE)], axis=0
        )
        o2[zz] = bf16(dot(chosen, source))
        return jnp.maximum(over, jnp.sum(live, axis=1, keepdims=True))

    def send_thirds():
        local_wait(meta1, m_recv.at[0])
        local_wait(r1_in, t_recv.at[0])

        def widen(j, crowd):
            live = meta1[j]
            chosen = squeeze(live)
            pack_src[j] = chosen
            r1[j] = bf16(dot(chosen, r1_in[j], ((0,), (0,))))
            return jnp.maximum(crowd, jnp.sum(live, axis=1, keepdims=True))

        crowd = lax.fori_loop(0, PLANE, widen, jnp.zeros((1, 1), jnp.float32))
        most = lax.fori_loop(0, NZ, pack, jnp.zeros((1, 1), jnp.float32))
        over = jnp.broadcast_to(jnp.where((most > CAP) | (crowd > FEW), 1.0, 0.0), (1, LANES))
        for j in range(NZ):
            meta2[j, :, PAIRS:] = over
        along_z(meta2, got2, (m_send.at[1], m_recv.at[1]))
        along_z(o2, r2, (t_send.at[1], t_recv.at[1]))

    def compute(first, rows):
        here = pl.ds(first, rows)
        gate = jnp.zeros((rows, 1), jnp.float32)
        for t in range(2 * half // 256):
            cols = slice(t * 256, (t + 1) * 256)
            hidden = dot(rows_x[here, :], wu[:, cols])
            upstream = dot(rows_g[here, :], wd[cols, :], ((1,), (1,)))
            s = jax.nn.sigmoid(hidden)
            activation = bf16(hidden * s)
            act[here, cols] = activation
            dhid[here, cols] = bf16(upstream * (s * (1.0 + hidden * (1.0 - s))))
            gate += jnp.sum(activation.astype(jnp.float32) * upstream, axis=1, keepdims=True)
        return gate

    def row_grads(first, rows, out):
        for t in range(WIDE // 512):
            cols = slice(t * 512, (t + 1) * 512)
            out[:rows, cols] = bf16(dot(dhid[pl.ds(first, rows), :], wu[cols, :], ((1,), (1,))))

    def peer_ids(c, sign, shape, axis):
        row = lax.broadcasted_iota(jnp.int32, shape, axis) + c * per_chunk
        turn = lax.div(row, quarter)
        peer = lax.div(lax.rem(row, quarter), direct)
        q = lax.rem(q_me + sign * turn + NX, NX)
        return expert_of(q, lax.div(peer, NY), lax.rem(peer, NY)), lax.rem(row, direct)

    groups = per_chunk // SUB
    gsend[...] = jnp.zeros_like(gsend)

    def chunk(c):
        first = c * per_chunk
        local_wait(recv.at[:, pl.ds(0, per_chunk)], f_recv.at[c])

        def unpack(g, inner):
            r = pl.ds(pl.multiple_of(first + g * SUB, SUB), SUB)
            both = jnp.concatenate(
                [recv[0, r].reshape(PAIRS, LANES), recv[1, r].reshape(PAIRS, LANES)], axis=1
            )
            out = bf16(dot(perm[...], both))
            for f in range(SUB):
                part = out[f * SUB : (f + 1) * SUB]
                rows_x[r, f * LANES : (f + 1) * LANES] = part[:, :LANES]
                rows_g[r, f * LANES : (f + 1) * LANES] = part[:, LANES:]
            return inner

        lax.fori_loop(0, groups, unpack, 0)
        gate = compute(first, per_chunk)
        row_grads(first, per_chunk, drow)

        for g in range(0, groups, 2):
            pair = [
                jnp.concatenate(
                    [
                        drow[(g + h) * SUB : (g + h + 1) * SUB, f * LANES : (f + 1) * LANES]
                        for f in range(SUB)
                    ],
                    axis=0,
                )
                for h in range(2)
            ]
            out = bf16(dot(perm[...], jnp.concatenate(pair, axis=1)))
            for h in range(2):
                r = pl.ds(first + (g + h) * SUB, SUB)
                dsend[r] = out[:, h * LANES : (h + 1) * LANES].reshape(SUB, SUB, LANES)

        if c == 0:
            pltpu.make_async_copy(dsend.at[rows_at(0)], back.at[rows_at(0)], r_recv.at[0]).start()

        def reply(n, inner):
            turn = lax.div(n, PEERS)
            dz, dy = hop(lax.rem(n, PEERS))
            q = lax.rem(q_me - turn + NX, NX)
            zz, yy = lax.rem(z - dz + NZ, NZ), lax.rem(y - dy + NY, NY)
            source = pl.ds(turn * quarter + (zz * NY + yy) * direct, direct)
            ship(
                dsend.at[source], back.at[rows_at(turn)], expert_of(q, zz, yy),
                r_send, r_recv.at[c],
            )
            return inner

        span = N // PARTS
        lax.fori_loop(max(1, c * span), (c + 1) * span, reply, 0)

        owner, slot = peer_ids(c, -1, (1, per_chunk), 1)
        to_source = jnp.where(
            lax.broadcasted_iota(jnp.int32, (N, per_chunk), 0) == owner, 1.0, 0.0
        )
        _, slot = peer_ids(c, -1, (per_chunk, LANES), 0)
        to_lane = lax.broadcasted_iota(jnp.int32, (per_chunk, LANES), 1) == slot
        spread = lax.dot_general(
            to_source, jnp.where(to_lane, gate, 0.0), (((1,), (0,)), ((), ())),
            precision=lax.Precision.HIGHEST, preferred_element_type=jnp.float32,
        )
        gsend[...] += spread.reshape(N, 1, LANES)

    def open_thirds():
        local_wait(got2, m_recv.at[1])
        local_wait(r2, t_recv.at[1])
        flag = jnp.zeros((1, LANES), jnp.float32)
        for j in range(NZ):
            flag = jnp.maximum(flag, got2[j, :, PAIRS:])
        flag_ref[...] = jnp.broadcast_to(flag, flag_ref.shape)

        def one(zz, carry):
            live = got2[zz][:, :PAIRS]
            position = dot(bf16(live), above[...])
            live = dot(bf16(live), perm[...])
            position = dot(bf16(position), perm[...])
            chosen = bf16(jnp.where((rank == position) & (live > 0.5), 1.0, 0.0))
            pack_in[zz] = chosen
            out = bf16(dot(chosen, r2[zz], ((0,), (0,))))
            for j in range(PLANE):
                o3[j, pl.ds(pl.multiple_of(zz * PLANE, PLANE), PLANE)] = out[j * SUB : (j + 1) * SUB]
            return carry

        lax.fori_loop(0, NZ, one, 0)
        flags = got2[...].reshape(NZ, PAIRS + LANES)[:, :PAIRS]
        row_s = lax.broadcasted_iota(jnp.int32, (PAIRS, N), 0)
        col_s = lax.broadcasted_iota(jnp.int32, (PAIRS, N), 1)
        row_z = lax.broadcasted_iota(jnp.int32, (NZ, N), 0)
        col_z = lax.broadcasted_iota(jnp.int32, (NZ, N), 1)

        def narrow(j, carry):
            here = (lax.rem(row_s, PLANE) == j) & (lax.div(row_s, PLANE) == lax.rem(col_s, PLANE))
            spread = dot(flags, jnp.where(here, 1.0, 0.0))
            live = jnp.where(lax.div(col_z, PLANE) == row_z, spread, 0.0)
            chosen = squeeze(jnp.sum(live, axis=0, keepdims=True))
            pack_dst[j] = chosen
            o3_out[j] = bf16(dot(chosen, o3[j]))
            return carry

        lax.fori_loop(0, PLANE, narrow, 0)
        in_plane(lambda m: o3_out.at[m], r3.at[p], 2)

    def run_thirds():
        local_wait(r3, t_recv.at[2])
        first = recv.shape[1]
        for m in range(PLANE):
            lanes = slice(m * LANES, (m + 1) * LANES)
            rows_x[first:, lanes] = r3[m, :, :LANES]
            rows_g[first:, lanes] = r3[m, :, LANES:]
        gate = compute(first, FEW)
        row_grads(first, FEW, d3)
        in_plane(
            lambda m: d3.at[:, pl.ds(pl.multiple_of(m * LANES, LANES), LANES)], rr1_in.at[p], 3
        )
        lane = lax.broadcasted_iota(jnp.int32, (FEW, LANES), 1)
        spread = lax.dot_general(
            pack_dst[p].astype(jnp.float32), jnp.where(lane == slots - 1, gate, 0.0),
            (((0,), (0,)), ((), ())),
            precision=lax.Precision.HIGHEST, preferred_element_type=jnp.float32,
        )
        gsend[...] += spread.reshape(N, 1, LANES)

    def pack_back():
        local_wait(rr1_in, t_recv.at[3])

        def widen(j, carry):
            rr1[j] = bf16(dot(pack_dst[j], rr1_in[j], ((0,), (0,))))
            return carry

        lax.fori_loop(0, PLANE, widen, 0)

        def one(zz, carry):
            source = jnp.concatenate(
                [rr1[j, pl.ds(pl.multiple_of(zz * PLANE, PLANE), PLANE)] for j in range(PLANE)], axis=0
            )
            ro2[zz] = bf16(dot(pack_in[zz], source))
            return carry

        lax.fori_loop(0, NZ, one, 0)
        along_z(ro2, rr2, (t_send.at[4], t_recv.at[4]))

    def open_back():
        local_wait(rr2, t_recv.at[4])

        def one(zz, carry):
            out = bf16(dot(pack_out[zz], rr2[zz], ((0,), (0,))))
            for j in range(PLANE):
                ro3[j, pl.ds(pl.multiple_of(zz * PLANE, PLANE), PLANE)] = out[j * SUB : (j + 1) * SUB]
            return carry

        lax.fori_loop(0, NZ, one, 0)

        def narrow(j, carry):
            ro3_out[j] = bf16(dot(pack_src[j], ro3[j]))
            return carry

        lax.fori_loop(0, PLANE, narrow, 0)
        in_plane(lambda m: ro3_out.at[m], d3back.at[:, my_lanes], 5)

    def weights_here():
        own_up.wait()
        own_down.wait()
        up_copy.wait()
        down_copy.wait()

    tiles = WIDE // 512

    def weight_grads():
        pltpu.make_async_copy(gsend.at[me], gback.at[me], g_recv).start()

        def reply_gate(n, carry):
            target = lax.rem(me + n, N)
            ship(gsend.at[target], gback.at[me], target, g_send, g_recv)
            return carry

        lax.fori_loop(1, N, reply_gate, 0)

        flag_swap = pltpu.make_async_remote_copy(
            src_ref=flag_ref, dst_ref=flag_in, send_sem=d_send.at[2], recv_sem=d_recv.at[2],
            device_id=partner, device_id_type=MESH,
        )
        flag_swap.start()

        first_core = core == 0
        for t in range(tiles):
            cols = slice(t * 512, (t + 1) * 512)
            whole = dot(rows_x[:, cols], dhid[...], ((0,), (0,)))
            left, right = whole[:, :half], whole[:, half:]
            up_out[cols, :] = bf16(jnp.where(first_core, right, left))
            up_own[cols, :] = jnp.where(first_core, left, right)
        up_swap = pltpu.make_async_remote_copy(
            src_ref=up_out, dst_ref=up_in, send_sem=d_send.at[0], recv_sem=d_recv.at[0],
            device_id=partner, device_id_type=MESH,
        )
        up_swap.start()
        for t in range(tiles):
            cols = slice(t * 512, (t + 1) * 512)
            whole = dot(act[...], rows_g[:, cols], ((0,), (0,)))
            left, right = whole[:half], whole[half:]
            down_out[:, cols] = bf16(jnp.where(first_core, right, left))
            down_own[:, cols] = jnp.where(first_core, left, right)
        down_swap = pltpu.make_async_remote_copy(
            src_ref=down_out, dst_ref=down_in, send_sem=d_send.at[1], recv_sem=d_recv.at[1],
            device_id=partner, device_id_type=MESH,
        )
        down_swap.start()
        up_swap.wait()
        for t in range(tiles):
            cols = slice(t * 512, (t + 1) * 512)
            dup_ref[cols, :] = bf16(up_own[cols, :] + up_in[cols, :].astype(jnp.float32))
        down_swap.wait()
        for t in range(tiles):
            cols = slice(t * 512, (t + 1) * 512)
            ddown_ref[:, cols] = bf16(down_own[:, cols] + down_in[:, cols].astype(jnp.float32))
        flag_swap.wait()
        flag_ref[...] = jnp.maximum(flag_ref[...], flag_in[...])

    def finish_rows():
        total[...] = jnp.zeros_like(total)

        def combine(c, carry):
            first = pl.multiple_of(c * per_chunk, SUB)
            local_wait(back.at[pl.ds(0, per_chunk)], r_recv.at[c])
            for g in range(0, groups, 2):
                pair = [
                    back[pl.ds(pl.multiple_of(first + (g + h) * SUB, SUB), SUB)].reshape(PAIRS, LANES)
                    for h in range(2)
                ]
                out = bf16(dot(perm[...], jnp.concatenate(pair, axis=1)))
                for h in range(2):
                    for f in range(SUB):
                        drow[(g + h) * SUB : (g + h + 1) * SUB, f * LANES : (f + 1) * LANES] = out[
                            f * SUB : (f + 1) * SUB, h * LANES : (h + 1) * LANES
                        ]
            owner, slot = peer_ids(c, 1, (1, per_chunk), 1)
            owned = jnp.where(
                lax.broadcasted_iota(jnp.int32, (N, per_chunk), 0) == owner, 1.0, 0.0
            )
            picked = jnp.zeros((1, per_chunk), jnp.float32)
            for k in range(direct):
                picked += jnp.where(slot == k, dot(pick_ref[k].astype(jnp.float32), owned), 0.0)
            rows = lax.broadcasted_iota(jnp.int32, (total.shape[0], per_chunk), 0)
            chosen = bf16(jnp.where(rows.astype(jnp.float32) == picked, 1.0, 0.0))
            for t in range(tiles):
                cols = slice(t * 512, (t + 1) * 512)
                total[:, cols] += dot(chosen, drow[:, cols])
            return carry

        lax.fori_loop(0, PARTS, combine, 0)
        local_wait(d3back, t_recv.at[5])
        for t in range(tiles):
            cols = slice(t * 512, (t + 1) * 512)
            dtok_ref[:, cols] = bf16(total[:, cols] + dot(own_pick[...], d3back[:, cols]))

    push_part(0)
    push_part(1)
    send_thirds()
    push_part(2)
    push_part(3)
    weights_here()
    chunk(0)
    open_thirds()
    run_thirds()
    chunk(1)
    pack_back()
    weight_grads()
    open_back()
    finish_rows()

    local_wait(gback, g_recv)
    eye = jnp.where(
        lax.broadcasted_iota(jnp.int32, (8, LANES), 0)
        == lax.broadcasted_iota(jnp.int32, (8, LANES), 1),
        1.0,
        0.0,
    )
    by_slot = lax.dot_general(
        eye, gback[...].reshape(N, LANES), (((1,), (1,)), ((), ())),
        precision=lax.Precision.HIGHEST, preferred_element_type=jnp.float32,
    )
    for k in range(slots):
        c = scale_vec[k : k + 1, :]
        inverse = jnp.where(c > 0.0, 1.0 / jnp.where(c > 0.0, c, 1.0), 0.0)
        dgate_ref[k : k + 1, :] = bf16(by_slot[k : k + 1, :] * inverse)

    local_wait(gsend.at[pl.ds(0, N - 1)], g_send)
    local_wait(send.at[pl.ds(0, N - 1)], f_send)
    local_wait(dsend.at[pl.ds(0, (N - 1) * direct)], r_send)
    local_wait(meta1.at[pl.ds(0, PLANE - 1)], m_send.at[0])
    local_wait(meta2.at[pl.ds(0, NZ - 1)], m_send.at[1])
    for i, ref in enumerate((third, o2, o3_out, rr1_in, ro2, ro3_out)):
        local_wait(ref.at[pl.ds(0, ref.shape[0] - 1)], t_send.at[i])


def write_out(*refs):
    count = len(refs) // 2
    copies = [
        pltpu.make_async_copy(refs[i], refs[count + i], refs[-1].at[i]) for i in range(count)
    ]
    for copy in copies:
        copy.start()
    for copy in copies:
        copy.wait()


def per_device(tokens, grad_out, gates, slot_index, slot_count, up_weight, down_weight):
    experts, slots = slot_index.shape[2:]
    held, width = tokens.shape[1:]
    half = up_weight.shape[2]
    total = experts * slots
    picks = jnp.transpose(slot_index[0], (2, 0, 1))

    vmem = pl.BlockSpec(memory_space=pltpu.VMEM)
    smem = pl.BlockSpec(memory_space=pltpu.SMEM)
    anywhere = pl.BlockSpec(memory_space=pl.ANY)
    hbm = pl.BlockSpec(memory_space=pltpu.HBM)
    low, full = jnp.bfloat16, jnp.float32

    def stay(array):
        return pltpu.with_memory_space_constraint(array, pltpu.HBM)

    dma = pltpu.SemaphoreType.DMA
    outs = (((held, width), low), ((slots, experts), low), ((width, half), low), ((half, width), low))
    operands = (
        picks,
        stay(picks),
        stay(gates[0, 0].T),
        stay(slot_count[0]),
        tokens[0],
        grad_out[0],
        up_weight[0],
        down_weight[0],
    )
    small = [
        pltpu.VMEM((slots, 1, experts), jnp.int32),
        pltpu.VMEM((slots, experts), low),
        pltpu.VMEM((1, experts), jnp.int32),
        pltpu.VMEM((held, SUB, LANES), low),
        pltpu.VMEM((held, SUB, LANES), low),
        pltpu.VMEM((8, experts), full),
        pltpu.SMEM((8, experts), full),
        pltpu.VMEM((experts, 1, LANES), full),
    ]

    def shared(sent, rows, parts, swapped):
        return [
            pltpu.VMEM((experts, 2, sent, SUB, LANES), low),
            pltpu.VMEM((2, sent * experts, SUB, LANES), low),
            pltpu.VMEM((width, 2 * half), low),
            pltpu.VMEM((2 * half, width), low),
            pltpu.VMEM((rows, width), low),
            pltpu.VMEM((rows, width), low),
            pltpu.VMEM((rows, 2 * half), low),
            pltpu.VMEM((rows, 2 * half), low),
            pltpu.VMEM((sent * experts // parts, width), low),
            pltpu.VMEM((sent * experts, SUB, LANES), low),
            pltpu.VMEM((sent * experts, SUB, LANES), low),
            pltpu.VMEM((experts, 1, LANES), full),
            *swapped,
            pltpu.VMEM((held, width), full),
            pltpu.VMEM((PAIRS, PAIRS), low),
        ]

    thirds = [
        pltpu.VMEM((PAIRS, PAIRS), low),
        pltpu.VMEM((PLANE, FEW, 2 * LANES), low),
        pltpu.VMEM((PLANE, FEW, 2 * LANES), low),
        pltpu.VMEM((PLANE, experts, 2 * LANES), low),
        pltpu.VMEM((PLANE, 1, LANES), full),
        pltpu.VMEM((1, 1, LANES), full),
        pltpu.VMEM((NZ, CAP, 2 * LANES), low),
        pltpu.VMEM((NZ, CAP, 2 * LANES), low),
        pltpu.VMEM((NZ, 1, PAIRS + LANES), full),
        pltpu.VMEM((NZ, 1, PAIRS + LANES), full),
        pltpu.VMEM((PLANE, experts, 2 * LANES), low),
        pltpu.VMEM((PLANE, FEW, 2 * LANES), low),
        pltpu.VMEM((PLANE, FEW, 2 * LANES), low),
        pltpu.VMEM((FEW, width), low),
        pltpu.VMEM((PLANE, FEW, LANES), low),
        pltpu.VMEM((PLANE, experts, LANES), low),
        pltpu.VMEM((NZ, CAP, LANES), low),
        pltpu.VMEM((NZ, CAP, LANES), low),
        pltpu.VMEM((PLANE, experts, LANES), low),
        pltpu.VMEM((PLANE, FEW, LANES), low),
        pltpu.VMEM((FEW, width), low),
        pltpu.VMEM((NZ, CAP, PAIRS), low),
        pltpu.VMEM((NZ, CAP, PAIRS), low),
        pltpu.VMEM((PLANE, FEW, experts), low),
        pltpu.VMEM((PLANE, FEW, experts), low),
        pltpu.VMEM((held, FEW), low),
        pltpu.VMEM((8, LANES), full),
    ]

    def sems(chunks, swaps):
        return [
            dma((6,)), dma, dma((3,)), dma, dma((chunks,)), dma, dma((chunks,)),
            dma, dma, dma((swaps,)), dma((swaps,)),
        ]

    def call(body, results, scratch, number):
        return pl.pallas_call(
            body,
            out_shape=tuple(pltpu.VMEM(shape, dtype) for shape, dtype in results),
            in_specs=[smem, hbm, hbm, hbm, vmem, vmem, hbm, hbm],
            out_specs=(vmem,) * len(results),
            scratch_shapes=scratch,
            compiler_params=pltpu.CompilerParams(
                collective_id=number, has_side_effects=True, vmem_limit_bytes=50 << 20
            ),
        )(*operands)

    def store(*results):
        return pl.pallas_call(
            write_out,
            out_shape=tuple(jax.ShapeDtypeStruct(shape, dtype) for shape, dtype in outs),
            in_specs=[vmem] * 4,
            out_specs=(anywhere,) * 4,
            scratch_shapes=[dma((4,))],
            compiler_params=pltpu.CompilerParams(vmem_limit_bytes=1 << 20),
        )(*(pltpu.with_memory_space_constraint(r, pltpu.VMEM) for r in results))

    *results, flag = call(
        lean_kernel,
        outs + (((8, LANES), full),),
        small + shared(slots - 1, (slots - 1) * experts + FEW, PARTS, [pltpu.VMEM(shape, kind) for shape in ((width, half), (half, width)) for kind in (low, low, full)]) + thirds + sems(PARTS, 3) + [dma((6,)), dma((6,)), dma((2,)), dma((2,))],
        0,
    )

    def padded(*unused):
        return store(*call(padded_kernel, outs, small + shared(slots, total, CHUNKS, [pltpu.VMEM(shape, full) for shape in ((width, half), (half, width)) for _ in range(2)]) + sems(CHUNKS, 2), 1))

    d_tokens, d_gate, d_up, d_down = lax.cond(flag[0, 0] > 0.5, padded, store, *results)
    return d_tokens[None], d_gate.T[None, None], d_up[None], d_down[None]


def solution(mesh):
    in_specs = (
        P("dp", "expert", None),
        P("dp", "expert", None),
        P("dp", "expert", None, None),
        P("dp", "expert", None, None),
        P("dp", "expert", None),
        P("expert", None, "dp"),
        P("expert", "dp", None),
    )
    out_specs = (
        P("dp", "expert", None),
        P("dp", "expert", None, None),
        P("expert", None, "dp"),
        P("expert", "dp", None),
    )
    return jax.shard_map(
        per_device, mesh=mesh, in_specs=in_specs, out_specs=out_specs, check_vma=False
    )
```

```python
import jax
import jax.numpy as jnp
from jax import lax
from jax.experimental import pallas as pl
from jax.experimental.pallas import tpu as pltpu
from jax.sharding import PartitionSpec as P

MESH = pl.DeviceIdType.MESH
NX, NY, NZ = 4, 4, 8
N = NX * NY * NZ
CHUNKS = NX
PEERS = NY * NZ
LANES = 128
SUB = 16
WIDE = SUB * LANES
PLANE = NX * NY
PAIRS = PLANE * PLANE
CAP = 96
FEW = 64
PARTS = 2


def place(me):
    return me % NX, (me // NX) % NY, me // (NX * NY)


def block_of(q, z, y):
    return q * PEERS + z * NY + y


def expert_of(q, z, y):
    return (z * NY + y) * NX + lax.rem(q - y + NX, NX)


def hop(i):
    return lax.rem(i, NZ), lax.div(i, NZ)


def bf16(v):
    return v.astype(jnp.bfloat16)


def dot(a, b, dims=((1,), (0,))):
    return lax.dot_general(a, b, (dims, ((), ())), preferred_element_type=jnp.float32)


def local_wait(ref, sem):
    pltpu.make_async_copy(ref, ref, sem).wait()


def padded_kernel(
    idx_ref, pick_hbm, gates_hbm, count_hbm, tok_ref, grad_ref, up_ref, down_ref,
    dtok_ref, dgate_ref, dup_ref, ddown_ref,
    pick_ref, gates_ref, count_ref, tok, grad, scale_vec, scale, gback,
    send, recv, wu, wd, rows_x, rows_g, act, dhid, drow, dsend, back, gsend,
    up_out, up_in, down_out, down_in, total, perm,
    w_sem, s_sem, small_sem, f_send, f_recv, r_send, r_recv, g_send, g_recv, d_send, d_recv,
):
    me = lax.axis_index("expert")
    core = lax.axis_index("dp")
    x, y, z = place(me)
    q_me = lax.rem(x + y, NX)
    slots = send.shape[2]
    per_chunk = PEERS * slots
    half = up_ref.shape[1]
    mine = pl.ds(pl.multiple_of(core * half, LANES), half)
    theirs = pl.ds(pl.multiple_of((1 - core) * half, LANES), half)
    partner = {"dp": 1 - core}

    barrier = pltpu.get_barrier_semaphore()
    pl.semaphore_signal(barrier, inc=1, device_id=partner, device_id_type=MESH)

    def greet(step, carry):
        pl.semaphore_signal(
            barrier, inc=1, device_id={"expert": lax.rem(me + step, N)}, device_id_type=MESH
        )
        return carry

    lax.fori_loop(1, N, greet, 0)

    own_up = pltpu.make_async_copy(up_ref, wu.at[:, mine], w_sem.at[0])
    own_up.start()
    own_down = pltpu.make_async_copy(down_ref, wd.at[mine, :], w_sem.at[1])
    own_down.start()

    small = [
        pltpu.make_async_copy(src, dst, small_sem.at[i])
        for i, (src, dst) in enumerate(
            ((gates_hbm, gates_ref), (count_hbm, count_ref), (pick_hbm, pick_ref))
        )
    ]
    for copy in small:
        copy.start()

    a = lax.broadcasted_iota(jnp.int32, (SUB * SUB, SUB * SUB), 0)
    b = lax.broadcasted_iota(jnp.int32, (SUB * SUB, SUB * SUB), 1)
    swap = (lax.rem(a, SUB) == lax.div(b, SUB)) & (lax.div(a, SUB) == lax.rem(b, SUB))
    perm[...] = jnp.where(swap, 1.0, 0.0).astype(jnp.bfloat16)

    for copy in small:
        copy.wait()
    scale_vec[...] = jnp.zeros_like(scale_vec)
    for k in range(slots):
        live = jnp.where(count_ref[...] > k, 1.0, 0.0)
        scale_vec[k : k + 1, :] = live * gates_ref[k : k + 1, :].astype(jnp.float32)
    to_scalars = pltpu.make_async_copy(scale_vec, scale, s_sem)
    to_scalars.start()

    def by_row(g, carry):
        r = pl.ds(pl.multiple_of(g * SUB, SUB), SUB)
        both = jnp.concatenate(
            [
                jnp.concatenate(
                    [ref[r, f * LANES : (f + 1) * LANES] for f in range(SUB)], axis=0
                )
                for ref in (tok_ref, grad_ref)
            ],
            axis=1,
        )
        out = bf16(dot(perm[...], both))
        tok[r] = out[:, :LANES].reshape(SUB, SUB, LANES)
        grad[r] = out[:, LANES:].reshape(SUB, SUB, LANES)
        return carry

    lax.fori_loop(0, tok.shape[0] // SUB, by_row, 0)
    to_scalars.wait()

    def fill(target):
        for k in range(slots):
            row = idx_ref[k, 0, target]
            send[target, 0, k] = tok[row]
            send[target, 1, k] = bf16(grad[row].astype(jnp.float32) * scale[k, target])

    pl.semaphore_wait(barrier, N)

    up_copy = pltpu.make_async_remote_copy(
        src_ref=up_ref, dst_ref=wu.at[:, mine], send_sem=w_sem.at[2], recv_sem=w_sem.at[3],
        device_id=partner, device_id_type=MESH,
    )
    up_copy.start()
    down_copy = pltpu.make_async_remote_copy(
        src_ref=down_ref, dst_ref=wd.at[mine, :], send_sem=w_sem.at[4], recv_sem=w_sem.at[5],
        device_id=partner, device_id_type=MESH,
    )
    down_copy.start()

    my_rows = pl.ds(block_of(q_me, z, y) * slots, slots)

    def push(n, carry):
        c = lax.div(n, PEERS)
        dz, dy = hop(lax.rem(n, PEERS))
        target = expert_of(lax.rem(q_me + c, NX), lax.rem(z + dz, NZ), lax.rem(y + dy, NY))
        fill(target)
        pltpu.make_async_remote_copy(
            src_ref=send.at[target], dst_ref=recv.at[:, my_rows],
            send_sem=f_send, recv_sem=f_recv.at[c],
            device_id={"expert": target}, device_id_type=MESH,
        ).start()
        return carry

    lax.fori_loop(1, N, push, 0)
    fill(me)
    pltpu.make_async_copy(send.at[me], recv.at[:, my_rows], f_recv.at[0]).start()

    own_up.wait()
    own_down.wait()
    up_copy.wait()
    down_copy.wait()

    groups = per_chunk // SUB
    grid_a = lax.broadcasted_iota(jnp.int32, (PEERS, per_chunk), 0)
    grid_b = lax.broadcasted_iota(jnp.int32, (PEERS, per_chunk), 1)
    to_peer = jnp.where(lax.div(grid_b, slots) == grid_a, 1.0, 0.0)
    row_id = lax.broadcasted_iota(jnp.int32, (per_chunk, LANES), 0)
    lane_id = lax.broadcasted_iota(jnp.int32, (per_chunk, LANES), 1)
    to_lane = jnp.where(lax.rem(row_id, slots) == lane_id, 1.0, 0.0)

    def chunk(c, carry):
        q = lax.rem(q_me - c + NX, NX)
        first = pl.multiple_of(q * per_chunk, SUB)
        local_wait(recv.at[:, pl.ds(0, per_chunk)], f_recv.at[c])

        def unpack(g, inner):
            r = pl.ds(pl.multiple_of(first + g * SUB, SUB), SUB)
            both = jnp.concatenate(
                [recv[0, r].reshape(SUB * SUB, LANES), recv[1, r].reshape(SUB * SUB, LANES)], axis=1
            )
            out = bf16(dot(perm[...], both))
            for f in range(SUB):
                part = out[f * SUB : (f + 1) * SUB]
                rows_x[r, f * LANES : (f + 1) * LANES] = part[:, :LANES]
                rows_g[r, f * LANES : (f + 1) * LANES] = part[:, LANES:]
            return inner

        lax.fori_loop(0, groups, unpack, 0)

        here = pl.ds(first, per_chunk)
        gate = jnp.zeros((per_chunk, 1), jnp.float32)
        for t in range(2 * half // 256):
            cols = slice(t * 256, (t + 1) * 256)
            hidden = dot(rows_x[here, :], wu[:, cols])
            upstream = dot(rows_g[here, :], wd[cols, :], ((1,), (1,)))
            s = jax.nn.sigmoid(hidden)
            activation = bf16(hidden * s)
            act[here, cols] = activation
            dhid[here, cols] = bf16(upstream * (s * (1.0 + hidden * (1.0 - s))))
            gate += jnp.sum(activation.astype(jnp.float32) * upstream, axis=1, keepdims=True)

        for t in range(WIDE // 512):
            cols = slice(t * 512, (t + 1) * 512)
            drow[:, cols] = bf16(dot(dhid[here, :], wu[cols, :], ((1,), (1,))))

        for g in range(0, groups, 2):
            pair = [
                jnp.concatenate(
                    [
                        drow[(g + h) * SUB : (g + h + 1) * SUB, f * LANES : (f + 1) * LANES]
                        for f in range(SUB)
                    ],
                    axis=0,
                )
                for h in range(2)
            ]
            out = bf16(dot(perm[...], jnp.concatenate(pair, axis=1)))
            for h in range(2):
                r = pl.ds(pl.multiple_of(first + (g + h) * SUB, SUB), SUB)
                dsend[r] = out[:, h * LANES : (h + 1) * LANES].reshape(SUB, SUB, LANES)

        @pl.when(c == 0)
        def _():
            pltpu.make_async_copy(dsend.at[my_rows], back.at[my_rows], r_recv.at[0]).start()

        def reply(i, inner):
            dz, dy = hop(i)
            zz, yy = lax.rem(z - dz + NZ, NZ), lax.rem(y - dy + NY, NY)
            source = pl.ds(block_of(q, zz, yy) * slots, slots)
            pltpu.make_async_remote_copy(
                src_ref=dsend.at[source], dst_ref=back.at[my_rows],
                send_sem=r_send, recv_sem=r_recv.at[c],
                device_id={"expert": expert_of(q, zz, yy)}, device_id_type=MESH,
            ).start()
            return inner

        lax.fori_loop(jnp.where(c == 0, 1, 0), PEERS, reply, 0)

        spread = lax.dot_general(
            to_peer, gate * to_lane, (((1,), (0,)), ((), ())),
            precision=lax.Precision.HIGHEST, preferred_element_type=jnp.float32,
        )
        gsend[pl.ds(q * PEERS, PEERS)] = spread.reshape(PEERS, 1, LANES)
        return carry

    lax.fori_loop(0, CHUNKS, chunk, 0)

    pltpu.make_async_copy(gsend.at[block_of(q_me, z, y)], gback.at[me], g_recv).start()

    def reply_gate(n, carry):
        c = lax.div(n, PEERS)
        dz, dy = hop(lax.rem(n, PEERS))
        q, zz, yy = lax.rem(q_me - c + NX, NX), lax.rem(z - dz + NZ, NZ), lax.rem(y - dy + NY, NY)
        pltpu.make_async_remote_copy(
            src_ref=gsend.at[block_of(q, zz, yy)], dst_ref=gback.at[me],
            send_sem=g_send, recv_sem=g_recv,
            device_id={"expert": expert_of(q, zz, yy)}, device_id_type=MESH,
        ).start()
        return carry

    lax.fori_loop(1, N, reply_gate, 0)

    tiles = WIDE // 512
    for t in range(tiles):
        cols = slice(t * 512, (t + 1) * 512)
        up_out[cols, :] = dot(rows_x[:, cols], dhid[:, theirs], ((0,), (0,)))
    up_swap = pltpu.make_async_remote_copy(
        src_ref=up_out, dst_ref=up_in, send_sem=d_send.at[0], recv_sem=d_recv.at[0],
        device_id=partner, device_id_type=MESH,
    )
    up_swap.start()
    for t in range(tiles):
        cols = slice(t * 512, (t + 1) * 512)
        down_out[:, cols] = dot(act[:, theirs], rows_g[:, cols], ((0,), (0,)))
    down_swap = pltpu.make_async_remote_copy(
        src_ref=down_out, dst_ref=down_in, send_sem=d_send.at[1], recv_sem=d_recv.at[1],
        device_id=partner, device_id_type=MESH,
    )
    down_swap.start()
    up_swap.wait()
    for t in range(tiles):
        cols = slice(t * 512, (t + 1) * 512)
        both = dot(rows_x[:, cols], dhid[:, mine], ((0,), (0,))) + up_in[cols, :]
        dup_ref[cols, :] = bf16(both)
    down_swap.wait()
    for t in range(tiles):
        cols = slice(t * 512, (t + 1) * 512)
        both = dot(act[:, mine], rows_g[:, cols], ((0,), (0,))) + down_in[:, cols]
        ddown_ref[:, cols] = bf16(both)

    total[...] = jnp.zeros_like(total)

    def combine(c, carry):
        q = lax.rem(q_me + c, NX)
        first = pl.multiple_of(q * per_chunk, SUB)
        local_wait(back.at[pl.ds(0, per_chunk)], r_recv.at[c])
        for g in range(0, groups, 2):
            pair = [
                back[pl.ds(pl.multiple_of(first + (g + h) * SUB, SUB), SUB)].reshape(SUB * SUB, LANES)
                for h in range(2)
            ]
            out = bf16(dot(perm[...], jnp.concatenate(pair, axis=1)))
            for h in range(2):
                for f in range(SUB):
                    drow[(g + h) * SUB : (g + h + 1) * SUB, f * LANES : (f + 1) * LANES] = out[
                        f * SUB : (f + 1) * SUB, h * LANES : (h + 1) * LANES
                    ]
        expert = lax.broadcasted_iota(jnp.int32, (N, per_chunk), 0)
        peer = lax.div(lax.broadcasted_iota(jnp.int32, (N, per_chunk), 1), slots)
        owner = expert_of(q, lax.div(peer, NY), lax.rem(peer, NY))
        owned = jnp.where(expert == owner, 1.0, 0.0)
        slot = lax.rem(lax.broadcasted_iota(jnp.int32, (1, per_chunk), 1), slots)
        picked = jnp.zeros((1, per_chunk), jnp.float32)
        for k in range(slots):
            picked += jnp.where(slot == k, dot(pick_ref[k].astype(jnp.float32), owned), 0.0)
        token = lax.broadcasted_iota(jnp.int32, (total.shape[0], per_chunk), 0)
        chosen = bf16(jnp.where(token.astype(jnp.float32) == picked, 1.0, 0.0))
        for t in range(tiles):
            cols = slice(t * 512, (t + 1) * 512)
            total[:, cols] += dot(chosen, drow[:, cols])
        return carry

    lax.fori_loop(0, CHUNKS, combine, 0)
    dtok_ref[...] = bf16(total[...])

    local_wait(gback, g_recv)
    eye = jnp.where(
        lax.broadcasted_iota(jnp.int32, (8, LANES), 0)
        == lax.broadcasted_iota(jnp.int32, (8, LANES), 1),
        1.0,
        0.0,
    )
    by_slot = lax.dot_general(
        eye, gback[...].reshape(N, LANES), (((1,), (1,)), ((), ())),
        precision=lax.Precision.HIGHEST, preferred_element_type=jnp.float32,
    )
    for k in range(slots):
        c = scale_vec[k : k + 1, :]
        inverse = jnp.where(c > 0.0, 1.0 / jnp.where(c > 0.0, c, 1.0), 0.0)
        dgate_ref[k : k + 1, :] = bf16(by_slot[k : k + 1, :] * inverse)
    local_wait(gsend.at[pl.ds(0, N - 1)], g_send)
    local_wait(send.at[pl.ds(0, N - 1)], f_send)
    local_wait(dsend.at[pl.ds(0, (N - 1) * slots)], r_send)


def lean_kernel(
    idx_ref, pick_hbm, gates_hbm, count_hbm, tok_ref, grad_ref, up_ref, down_ref,
    dtok_ref, dgate_ref, dup_ref, ddown_ref, over_ref,
    pick_ref, gates_ref, count_ref, tok, grad, scale_vec, scale, gback,
    send, recv, wu, wd, rows_x, rows_g, act, dhid, drow, dsend, back, gsend,
    up_out, up_in, up_own, down_out, down_in, down_own, total, perm, above,
    third, r1_in, r1, meta1, live3, o2, r2, meta2, got2, o3, o3_out, r3,
    d3, rr1_in, rr1, ro2, rr2, ro3, ro3_out, d3back, pack_out, pack_in, pack_src, pack_dst, own_pick, flag_ref, flag_in,
    w_sem, s_sem, small_sem, f_send, f_recv, r_send, r_recv, g_send, g_recv, d_send, d_recv,
    t_send, t_recv, m_send, m_recv,
):
    me = lax.axis_index("expert")
    core = lax.axis_index("dp")
    x, y, z = place(me)
    p = lax.rem(me, PLANE)
    q_me = lax.rem(x + y, NX)
    slots = pick_ref.shape[0]
    direct = send.shape[2]
    quarter = PEERS * direct
    per_chunk = recv.shape[1] // PARTS
    half = up_ref.shape[1]
    mine = pl.ds(pl.multiple_of(core * half, LANES), half)
    partner = {"dp": 1 - core}
    my_lanes = pl.ds(pl.multiple_of(p * LANES, LANES), LANES)

    barrier = pltpu.get_barrier_semaphore()
    pl.semaphore_signal(barrier, inc=1, device_id=partner, device_id_type=MESH)

    def greet(step, carry):
        pl.semaphore_signal(
            barrier, inc=1, device_id={"expert": lax.rem(me + step, N)}, device_id_type=MESH
        )
        return carry

    lax.fori_loop(1, N, greet, 0)

    small = [
        pltpu.make_async_copy(src, dst, small_sem.at[i])
        for i, (src, dst) in enumerate(
            ((gates_hbm, gates_ref), (count_hbm, count_ref), (pick_hbm, pick_ref))
        )
    ]
    for copy in small:
        copy.start()
    own_up = pltpu.make_async_copy(up_ref, wu.at[:, mine], w_sem.at[0])
    own_up.start()
    own_down = pltpu.make_async_copy(down_ref, wd.at[mine, :], w_sem.at[1])
    own_down.start()

    a = lax.broadcasted_iota(jnp.int32, (PAIRS, PAIRS), 0)
    b = lax.broadcasted_iota(jnp.int32, (PAIRS, PAIRS), 1)
    swap = (lax.rem(a, SUB) == lax.div(b, SUB)) & (lax.div(a, SUB) == lax.rem(b, SUB))
    perm[...] = bf16(jnp.where(swap, 1.0, 0.0))
    above[...] = bf16(jnp.where(a < b, 1.0, 0.0))

    for copy in small:
        copy.wait()
    scale_vec[...] = jnp.zeros_like(scale_vec)
    for k in range(slots):
        live = jnp.where(count_ref[...] > k, 1.0, 0.0)
        scale_vec[k : k + 1, :] = live * gates_ref[k : k + 1, :].astype(jnp.float32)
        live3[0] = live
    to_scalars = pltpu.make_async_copy(scale_vec, scale, s_sem)
    to_scalars.start()

    few = lax.broadcasted_iota(jnp.int32, (FEW, N), 0).astype(jnp.float32)

    def squeeze(live):
        position = dot(bf16(live), above[:N, :N])
        return bf16(jnp.where((few == position) & (live > 0.5), 1.0, 0.0))

    token = lax.broadcasted_iota(jnp.int32, (tok.shape[0], N), 0)
    last_pick = jnp.where(token == pick_ref[slots - 1], 1.0, 0.0)
    last_scaled = bf16(last_pick * scale_vec[slots - 1 : slots, :])
    squeezed = squeeze(live3[0])
    own_pick[...] = bf16(dot(bf16(last_pick), squeezed, ((1,), (1,))))
    chosen_rows = bf16(dot(squeezed, bf16(last_pick), ((1,), (1,))))
    scaled_rows = bf16(dot(squeezed, last_scaled, ((1,), (1,))))
    for t in range(WIDE // 512):
        cols = slice(t * 512, (t + 1) * 512)
        row_part = bf16(dot(chosen_rows, tok_ref[:, cols]))
        grad_part = bf16(dot(scaled_rows, grad_ref[:, cols]))
        for m in range(512 // LANES):
            lanes = slice(m * LANES, (m + 1) * LANES)
            third[t * 512 // LANES + m, :, :LANES] = row_part[:, lanes]
            third[t * 512 // LANES + m, :, LANES:] = grad_part[:, lanes]

    def by_row(g, carry):
        r = pl.ds(pl.multiple_of(g * SUB, SUB), SUB)
        both = jnp.concatenate(
            [
                jnp.concatenate([ref[r, f * LANES : (f + 1) * LANES] for f in range(SUB)], axis=0)
                for ref in (tok_ref, grad_ref)
            ],
            axis=1,
        )
        out = bf16(dot(perm[...], both))
        tok[r] = out[:, :LANES].reshape(SUB, SUB, LANES)
        grad[r] = out[:, LANES:].reshape(SUB, SUB, LANES)
        return carry

    lax.fori_loop(0, tok.shape[0] // SUB, by_row, 0)
    to_scalars.wait()

    def ship(src, dst, target, send_sem, recv_sem):
        pltpu.make_async_remote_copy(
            src_ref=src, dst_ref=dst, send_sem=send_sem, recv_sem=recv_sem,
            device_id={"expert": target}, device_id_type=MESH,
        ).start()

    def in_plane(src_of, dst, sem):
        def one(k, carry):
            peer = lax.rem(p + k, PLANE)
            ship(src_of(peer), dst, z * PLANE + peer, t_send.at[sem], t_recv.at[sem])
            return carry

        pltpu.make_async_copy(src_of(p), dst, t_recv.at[sem]).start()
        lax.fori_loop(1, PLANE, one, 0)

    def along_z(src, dst, sems):
        def one(k, carry):
            zz = lax.rem(z + k, NZ)
            ship(src.at[zz], dst.at[z], zz * PLANE + p, sems[0], sems[1])
            return carry

        pltpu.make_async_copy(src.at[z], dst.at[z], sems[1]).start()
        lax.fori_loop(1, NZ, one, 0)

    my_peer = (z * NY + y) * direct

    def rows_at(c):
        return pl.ds(c * quarter + my_peer, direct)

    def fill(target):
        for k in range(direct):
            row = idx_ref[k, 0, target]
            send[target, 0, k] = tok[row]
            send[target, 1, k] = bf16(grad[row].astype(jnp.float32) * scale[k, target])

    def target_of(c, i):
        dz, dy = hop(i)
        return expert_of(lax.rem(q_me + c, NX), lax.rem(z + dz, NZ), lax.rem(y + dy, NY))

    def fill_first(i, carry):
        fill(target_of(0, i))
        return carry

    def push_part(c):
        def push(i, carry):
            target = target_of(c, i)
            if c > 0:
                fill(target)
            ship(send.at[target], recv.at[:, rows_at(c)], target, f_send, f_recv.at[c * PARTS // NX])
            return carry

        if c == 0:
            pltpu.make_async_copy(send.at[me], recv.at[:, rows_at(0)], f_recv.at[0]).start()
        lax.fori_loop(1 if c == 0 else 0, PEERS, push, 0)

    lax.fori_loop(0, PEERS, fill_first, 0)
    pl.semaphore_wait(barrier, N)

    push_part(0)

    in_plane(lambda m: third.at[m], r1_in.at[p], 0)

    def tell(k, carry):
        ship(live3.at[0], meta1.at[p], z * PLANE + lax.rem(p + k, PLANE), m_send.at[0], m_recv.at[0])
        return carry

    pltpu.make_async_copy(live3.at[0], meta1.at[p], m_recv.at[0]).start()
    lax.fori_loop(1, PLANE, tell, 0)

    up_copy = pltpu.make_async_remote_copy(
        src_ref=up_ref, dst_ref=wu.at[:, mine], send_sem=w_sem.at[2], recv_sem=w_sem.at[3],
        device_id=partner, device_id_type=MESH,
    )
    up_copy.start()
    down_copy = pltpu.make_async_remote_copy(
        src_ref=down_ref, dst_ref=wd.at[mine, :], send_sem=w_sem.at[4], recv_sem=w_sem.at[5],
        device_id=partner, device_id_type=MESH,
    )
    down_copy.start()

    row_a = lax.broadcasted_iota(jnp.int32, (N, PAIRS), 0)
    col_a = lax.broadcasted_iota(jnp.int32, (N, PAIRS), 1)
    col_p = lax.broadcasted_iota(jnp.int32, (PLANE, PAIRS), 1)
    row_p = lax.broadcasted_iota(jnp.int32, (PLANE, PAIRS), 0)
    rank = lax.broadcasted_iota(jnp.int32, (CAP, PAIRS), 0).astype(jnp.float32)

    def pack(zz, over):
        pick_plane = jnp.where(row_a == zz * PLANE + lax.rem(col_a, PLANE), 1.0, 0.0)
        spread = dot(meta1[...].reshape(PLANE, LANES), pick_plane)
        own = jnp.where(lax.div(col_p, PLANE) == row_p, spread, 0.0)
        live = jnp.sum(own, axis=0, keepdims=True)
        position = dot(bf16(live), above[...])
        chosen = bf16(jnp.where((rank == position) & (live > 0.5), 1.0, 0.0))
        pack_out[zz] = chosen
        meta2[zz, :, :PAIRS] = live
        source = jnp.concatenate(
            [r1[j, pl.ds(pl.multiple_of(zz * PLANE, PLANE), PLANE)] for j in range(PLANE)], axis=0
        )
        o2[zz] = bf16(dot(chosen, source))
        return jnp.maximum(over, jnp.sum(live, axis=1, keepdims=True))

    def send_thirds():
        local_wait(meta1, m_recv.at[0])
        local_wait(r1_in, t_recv.at[0])

        def widen(j, crowd):
            live = meta1[j]
            chosen = squeeze(live)
            pack_src[j] = chosen
            r1[j] = bf16(dot(chosen, r1_in[j], ((0,), (0,))))
            return jnp.maximum(crowd, jnp.sum(live, axis=1, keepdims=True))

        crowd = lax.fori_loop(0, PLANE, widen, jnp.zeros((1, 1), jnp.float32))
        most = lax.fori_loop(0, NZ, pack, jnp.zeros((1, 1), jnp.float32))
        over = jnp.broadcast_to(jnp.where((most > CAP) | (crowd > FEW), 1.0, 0.0), (1, LANES))
        for j in range(NZ):
            meta2[j, :, PAIRS:] = over
        along_z(meta2, got2, (m_send.at[1], m_recv.at[1]))
        along_z(o2, r2, (t_send.at[1], t_recv.at[1]))

    def compute(first, rows):
        here = pl.ds(first, rows)
        gate = jnp.zeros((rows, 1), jnp.float32)
        for t in range(2 * half // 256):
            cols = slice(t * 256, (t + 1) * 256)
            hidden = dot(rows_x[here, :], wu[:, cols])
            upstream = dot(rows_g[here, :], wd[cols, :], ((1,), (1,)))
            s = jax.nn.sigmoid(hidden)
            activation = bf16(hidden * s)
            act[here, cols] = activation
            dhid[here, cols] = bf16(upstream * (s * (1.0 + hidden * (1.0 - s))))
            gate += jnp.sum(activation.astype(jnp.float32) * upstream, axis=1, keepdims=True)
        return gate

    def row_grads(first, rows, out):
        for t in range(WIDE // 512):
            cols = slice(t * 512, (t + 1) * 512)
            out[:rows, cols] = bf16(dot(dhid[pl.ds(first, rows), :], wu[cols, :], ((1,), (1,))))

    def peer_ids(c, sign, shape, axis):
        row = lax.broadcasted_iota(jnp.int32, shape, axis) + c * per_chunk
        turn = lax.div(row, quarter)
        peer = lax.div(lax.rem(row, quarter), direct)
        q = lax.rem(q_me + sign * turn + NX, NX)
        return expert_of(q, lax.div(peer, NY), lax.rem(peer, NY)), lax.rem(row, direct)

    groups = per_chunk // SUB
    gsend[...] = jnp.zeros_like(gsend)

    def chunk(c):
        first = c * per_chunk
        local_wait(recv.at[:, pl.ds(0, per_chunk)], f_recv.at[c])

        def unpack(g, inner):
            r = pl.ds(pl.multiple_of(first + g * SUB, SUB), SUB)
            both = jnp.concatenate(
                [recv[0, r].reshape(PAIRS, LANES), recv[1, r].reshape(PAIRS, LANES)], axis=1
            )
            out = bf16(dot(perm[...], both))
            for f in range(SUB):
                part = out[f * SUB : (f + 1) * SUB]
                rows_x[r, f * LANES : (f + 1) * LANES] = part[:, :LANES]
                rows_g[r, f * LANES : (f + 1) * LANES] = part[:, LANES:]
            return inner

        lax.fori_loop(0, groups, unpack, 0)
        gate = compute(first, per_chunk)
        row_grads(first, per_chunk, drow)

        for g in range(0, groups, 2):
            pair = [
                jnp.concatenate(
                    [
                        drow[(g + h) * SUB : (g + h + 1) * SUB, f * LANES : (f + 1) * LANES]
                        for f in range(SUB)
                    ],
                    axis=0,
                )
                for h in range(2)
            ]
            out = bf16(dot(perm[...], jnp.concatenate(pair, axis=1)))
            for h in range(2):
                r = pl.ds(first + (g + h) * SUB, SUB)
                dsend[r] = out[:, h * LANES : (h + 1) * LANES].reshape(SUB, SUB, LANES)

        if c == 0:
            pltpu.make_async_copy(dsend.at[rows_at(0)], back.at[rows_at(0)], r_recv.at[0]).start()

        def reply(n, inner):
            turn = lax.div(n, PEERS)
            dz, dy = hop(lax.rem(n, PEERS))
            q = lax.rem(q_me - turn + NX, NX)
            zz, yy = lax.rem(z - dz + NZ, NZ), lax.rem(y - dy + NY, NY)
            source = pl.ds(turn * quarter + (zz * NY + yy) * direct, direct)
            ship(
                dsend.at[source], back.at[rows_at(turn)], expert_of(q, zz, yy),
                r_send, r_recv.at[c],
            )
            return inner

        span = N // PARTS
        lax.fori_loop(max(1, c * span), (c + 1) * span, reply, 0)

        owner, slot = peer_ids(c, -1, (1, per_chunk), 1)
        to_source = jnp.where(
            lax.broadcasted_iota(jnp.int32, (N, per_chunk), 0) == owner, 1.0, 0.0
        )
        _, slot = peer_ids(c, -1, (per_chunk, LANES), 0)
        to_lane = lax.broadcasted_iota(jnp.int32, (per_chunk, LANES), 1) == slot
        spread = lax.dot_general(
            to_source, jnp.where(to_lane, gate, 0.0), (((1,), (0,)), ((), ())),
            precision=lax.Precision.HIGHEST, preferred_element_type=jnp.float32,
        )
        gsend[...] += spread.reshape(N, 1, LANES)

    def open_thirds():
        local_wait(got2, m_recv.at[1])
        local_wait(r2, t_recv.at[1])
        flag = jnp.zeros((1, LANES), jnp.float32)
        for j in range(NZ):
            flag = jnp.maximum(flag, got2[j, :, PAIRS:])
        flag_ref[...] = jnp.broadcast_to(flag, flag_ref.shape)

        def one(zz, carry):
            live = got2[zz][:, :PAIRS]
            position = dot(bf16(live), above[...])
            live = dot(bf16(live), perm[...])
            position = dot(bf16(position), perm[...])
            chosen = bf16(jnp.where((rank == position) & (live > 0.5), 1.0, 0.0))
            pack_in[zz] = chosen
            out = bf16(dot(chosen, r2[zz], ((0,), (0,))))
            for j in range(PLANE):
                o3[j, pl.ds(pl.multiple_of(zz * PLANE, PLANE), PLANE)] = out[j * SUB : (j + 1) * SUB]
            return carry

        lax.fori_loop(0, NZ, one, 0)
        flags = got2[...].reshape(NZ, PAIRS + LANES)[:, :PAIRS]
        row_s = lax.broadcasted_iota(jnp.int32, (PAIRS, N), 0)
        col_s = lax.broadcasted_iota(jnp.int32, (PAIRS, N), 1)
        row_z = lax.broadcasted_iota(jnp.int32, (NZ, N), 0)
        col_z = lax.broadcasted_iota(jnp.int32, (NZ, N), 1)

        def narrow(j, carry):
            here = (lax.rem(row_s, PLANE) == j) & (lax.div(row_s, PLANE) == lax.rem(col_s, PLANE))
            spread = dot(flags, jnp.where(here, 1.0, 0.0))
            live = jnp.where(lax.div(col_z, PLANE) == row_z, spread, 0.0)
            chosen = squeeze(jnp.sum(live, axis=0, keepdims=True))
            pack_dst[j] = chosen
            o3_out[j] = bf16(dot(chosen, o3[j]))
            return carry

        lax.fori_loop(0, PLANE, narrow, 0)
        in_plane(lambda m: o3_out.at[m], r3.at[p], 2)

    def run_thirds():
        local_wait(r3, t_recv.at[2])
        first = recv.shape[1]
        for m in range(PLANE):
            lanes = slice(m * LANES, (m + 1) * LANES)
            rows_x[first:, lanes] = r3[m, :, :LANES]
            rows_g[first:, lanes] = r3[m, :, LANES:]
        gate = compute(first, FEW)
        row_grads(first, FEW, d3)
        in_plane(
            lambda m: d3.at[:, pl.ds(pl.multiple_of(m * LANES, LANES), LANES)], rr1_in.at[p], 3
        )
        lane = lax.broadcasted_iota(jnp.int32, (FEW, LANES), 1)
        spread = lax.dot_general(
            pack_dst[p].astype(jnp.float32), jnp.where(lane == slots - 1, gate, 0.0),
            (((0,), (0,)), ((), ())),
            precision=lax.Precision.HIGHEST, preferred_element_type=jnp.float32,
        )
        gsend[...] += spread.reshape(N, 1, LANES)

    def pack_back():
        local_wait(rr1_in, t_recv.at[3])

        def widen(j, carry):
            rr1[j] = bf16(dot(pack_dst[j], rr1_in[j], ((0,), (0,))))
            return carry

        lax.fori_loop(0, PLANE, widen, 0)

        def one(zz, carry):
            source = jnp.concatenate(
                [rr1[j, pl.ds(pl.multiple_of(zz * PLANE, PLANE), PLANE)] for j in range(PLANE)], axis=0
            )
            ro2[zz] = bf16(dot(pack_in[zz], source))
            return carry

        lax.fori_loop(0, NZ, one, 0)
        along_z(ro2, rr2, (t_send.at[4], t_recv.at[4]))

    def open_back():
        local_wait(rr2, t_recv.at[4])

        def one(zz, carry):
            out = bf16(dot(pack_out[zz], rr2[zz], ((0,), (0,))))
            for j in range(PLANE):
                ro3[j, pl.ds(pl.multiple_of(zz * PLANE, PLANE), PLANE)] = out[j * SUB : (j + 1) * SUB]
            return carry

        lax.fori_loop(0, NZ, one, 0)

        def narrow(j, carry):
            ro3_out[j] = bf16(dot(pack_src[j], ro3[j]))
            return carry

        lax.fori_loop(0, PLANE, narrow, 0)
        in_plane(lambda m: ro3_out.at[m], d3back.at[:, my_lanes], 5)

    def weights_here():
        own_up.wait()
        own_down.wait()
        up_copy.wait()
        down_copy.wait()

    tiles = WIDE // 512

    def weight_grads():
        pltpu.make_async_copy(gsend.at[me], gback.at[me], g_recv).start()

        def reply_gate(n, carry):
            target = lax.rem(me + n, N)
            ship(gsend.at[target], gback.at[me], target, g_send, g_recv)
            return carry

        lax.fori_loop(1, N, reply_gate, 0)

        flag_swap = pltpu.make_async_remote_copy(
            src_ref=flag_ref, dst_ref=flag_in, send_sem=d_send.at[2], recv_sem=d_recv.at[2],
            device_id=partner, device_id_type=MESH,
        )
        flag_swap.start()

        first_core = core == 0
        for t in range(tiles):
            cols = slice(t * 512, (t + 1) * 512)
            whole = dot(rows_x[:, cols], dhid[...], ((0,), (0,)))
            left, right = whole[:, :half], whole[:, half:]
            up_out[cols, :] = bf16(jnp.where(first_core, right, left))
            up_own[cols, :] = jnp.where(first_core, left, right)
        up_swap = pltpu.make_async_remote_copy(
            src_ref=up_out, dst_ref=up_in, send_sem=d_send.at[0], recv_sem=d_recv.at[0],
            device_id=partner, device_id_type=MESH,
        )
        up_swap.start()
        for t in range(tiles):
            cols = slice(t * 512, (t + 1) * 512)
            whole = dot(act[...], rows_g[:, cols], ((0,), (0,)))
            left, right = whole[:half], whole[half:]
            down_out[:, cols] = bf16(jnp.where(first_core, right, left))
            down_own[:, cols] = jnp.where(first_core, left, right)
        down_swap = pltpu.make_async_remote_copy(
            src_ref=down_out, dst_ref=down_in, send_sem=d_send.at[1], recv_sem=d_recv.at[1],
            device_id=partner, device_id_type=MESH,
        )
        down_swap.start()
        up_swap.wait()
        for t in range(tiles):
            cols = slice(t * 512, (t + 1) * 512)
            dup_ref[cols, :] = bf16(up_own[cols, :] + up_in[cols, :].astype(jnp.float32))
        down_swap.wait()
        for t in range(tiles):
            cols = slice(t * 512, (t + 1) * 512)
            ddown_ref[:, cols] = bf16(down_own[:, cols] + down_in[:, cols].astype(jnp.float32))
        flag_swap.wait()
        over_ref[0, 0] = jnp.max(jnp.maximum(flag_ref[...], flag_in[...]))

    def finish_rows():
        total[...] = jnp.zeros_like(total)

        def combine(c, carry):
            first = pl.multiple_of(c * per_chunk, SUB)
            local_wait(back.at[pl.ds(0, per_chunk)], r_recv.at[c])
            for g in range(0, groups, 2):
                pair = [
                    back[pl.ds(pl.multiple_of(first + (g + h) * SUB, SUB), SUB)].reshape(PAIRS, LANES)
                    for h in range(2)
                ]
                out = bf16(dot(perm[...], jnp.concatenate(pair, axis=1)))
                for h in range(2):
                    for f in range(SUB):
                        drow[(g + h) * SUB : (g + h + 1) * SUB, f * LANES : (f + 1) * LANES] = out[
                            f * SUB : (f + 1) * SUB, h * LANES : (h + 1) * LANES
                        ]
            owner, slot = peer_ids(c, 1, (1, per_chunk), 1)
            owned = jnp.where(
                lax.broadcasted_iota(jnp.int32, (N, per_chunk), 0) == owner, 1.0, 0.0
            )
            picked = jnp.zeros((1, per_chunk), jnp.float32)
            for k in range(direct):
                picked += jnp.where(slot == k, dot(pick_ref[k].astype(jnp.float32), owned), 0.0)
            rows = lax.broadcasted_iota(jnp.int32, (total.shape[0], per_chunk), 0)
            chosen = bf16(jnp.where(rows.astype(jnp.float32) == picked, 1.0, 0.0))
            for t in range(tiles):
                cols = slice(t * 512, (t + 1) * 512)
                total[:, cols] += dot(chosen, drow[:, cols])
            return carry

        lax.fori_loop(0, PARTS, combine, 0)
        local_wait(d3back, t_recv.at[5])
        for t in range(tiles):
            cols = slice(t * 512, (t + 1) * 512)
            dtok_ref[:, cols] = bf16(total[:, cols] + dot(own_pick[...], d3back[:, cols]))

    push_part(1)
    send_thirds()
    push_part(2)
    push_part(3)
    weights_here()
    chunk(0)
    open_thirds()
    run_thirds()
    chunk(1)
    pack_back()
    weight_grads()
    open_back()
    finish_rows()

    local_wait(gback, g_recv)
    eye = jnp.where(
        lax.broadcasted_iota(jnp.int32, (8, LANES), 0)
        == lax.broadcasted_iota(jnp.int32, (8, LANES), 1),
        1.0,
        0.0,
    )
    by_slot = lax.dot_general(
        eye, gback[...].reshape(N, LANES), (((1,), (1,)), ((), ())),
        precision=lax.Precision.HIGHEST, preferred_element_type=jnp.float32,
    )
    for k in range(slots):
        c = scale_vec[k : k + 1, :]
        inverse = jnp.where(c > 0.0, 1.0 / jnp.where(c > 0.0, c, 1.0), 0.0)
        dgate_ref[k : k + 1, :] = bf16(by_slot[k : k + 1, :] * inverse)

    local_wait(gsend.at[pl.ds(0, N - 1)], g_send)
    local_wait(send.at[pl.ds(0, N - 1)], f_send)
    local_wait(dsend.at[pl.ds(0, (N - 1) * direct)], r_send)
    local_wait(meta1.at[pl.ds(0, PLANE - 1)], m_send.at[0])
    local_wait(meta2.at[pl.ds(0, NZ - 1)], m_send.at[1])
    for i, ref in enumerate((third, o2, o3_out, rr1_in, ro2, ro3_out)):
        local_wait(ref.at[pl.ds(0, ref.shape[0] - 1)], t_send.at[i])


def write_out(*refs):
    count = len(refs) // 2
    copies = [
        pltpu.make_async_copy(refs[i], refs[count + i], refs[-1].at[i]) for i in range(count)
    ]
    for copy in copies:
        copy.start()
    for copy in copies:
        copy.wait()


def per_device(tokens, grad_out, gates, slot_index, slot_count, up_weight, down_weight):
    experts, slots = slot_index.shape[2:]
    held, width = tokens.shape[1:]
    half = up_weight.shape[2]
    total = experts * slots
    picks = jnp.transpose(slot_index[0], (2, 0, 1))

    vmem = pl.BlockSpec(memory_space=pltpu.VMEM)
    smem = pl.BlockSpec(memory_space=pltpu.SMEM)
    anywhere = pl.BlockSpec(memory_space=pl.ANY)
    hbm = pl.BlockSpec(memory_space=pltpu.HBM)
    low, full = jnp.bfloat16, jnp.float32

    def stay(array):
        return pltpu.with_memory_space_constraint(array, pltpu.HBM)

    dma = pltpu.SemaphoreType.DMA
    outs = (((held, width), low), ((slots, experts), low), ((width, half), low), ((half, width), low))
    kept = tuple(pltpu.VMEM(shape, dtype) for shape, dtype in outs)
    operands = (
        picks,
        stay(picks),
        stay(gates[0, 0].T),
        stay(slot_count[0]),
        tokens[0],
        grad_out[0],
        up_weight[0],
        down_weight[0],
    )
    small = [
        pltpu.VMEM((slots, 1, experts), jnp.int32),
        pltpu.VMEM((slots, experts), low),
        pltpu.VMEM((1, experts), jnp.int32),
        pltpu.VMEM((held, SUB, LANES), low),
        pltpu.VMEM((held, SUB, LANES), low),
        pltpu.VMEM((8, experts), full),
        pltpu.SMEM((8, experts), full),
        pltpu.VMEM((experts, 1, LANES), full),
    ]

    def shared(sent, rows, parts, swapped):
        return [
            pltpu.VMEM((experts, 2, sent, SUB, LANES), low),
            pltpu.VMEM((2, sent * experts, SUB, LANES), low),
            pltpu.VMEM((width, 2 * half), low),
            pltpu.VMEM((2 * half, width), low),
            pltpu.VMEM((rows, width), low),
            pltpu.VMEM((rows, width), low),
            pltpu.VMEM((rows, 2 * half), low),
            pltpu.VMEM((rows, 2 * half), low),
            pltpu.VMEM((sent * experts // parts, width), low),
            pltpu.VMEM((sent * experts, SUB, LANES), low),
            pltpu.VMEM((sent * experts, SUB, LANES), low),
            pltpu.VMEM((experts, 1, LANES), full),
            *swapped,
            pltpu.VMEM((held, width), full),
            pltpu.VMEM((PAIRS, PAIRS), low),
        ]

    thirds = [
        pltpu.VMEM((PAIRS, PAIRS), low),
        pltpu.VMEM((PLANE, FEW, 2 * LANES), low),
        pltpu.VMEM((PLANE, FEW, 2 * LANES), low),
        pltpu.VMEM((PLANE, experts, 2 * LANES), low),
        pltpu.VMEM((PLANE, 1, LANES), full),
        pltpu.VMEM((1, 1, LANES), full),
        pltpu.VMEM((NZ, CAP, 2 * LANES), low),
        pltpu.VMEM((NZ, CAP, 2 * LANES), low),
        pltpu.VMEM((NZ, 1, PAIRS + LANES), full),
        pltpu.VMEM((NZ, 1, PAIRS + LANES), full),
        pltpu.VMEM((PLANE, experts, 2 * LANES), low),
        pltpu.VMEM((PLANE, FEW, 2 * LANES), low),
        pltpu.VMEM((PLANE, FEW, 2 * LANES), low),
        pltpu.VMEM((FEW, width), low),
        pltpu.VMEM((PLANE, FEW, LANES), low),
        pltpu.VMEM((PLANE, experts, LANES), low),
        pltpu.VMEM((NZ, CAP, LANES), low),
        pltpu.VMEM((NZ, CAP, LANES), low),
        pltpu.VMEM((PLANE, experts, LANES), low),
        pltpu.VMEM((PLANE, FEW, LANES), low),
        pltpu.VMEM((FEW, width), low),
        pltpu.VMEM((NZ, CAP, PAIRS), low),
        pltpu.VMEM((NZ, CAP, PAIRS), low),
        pltpu.VMEM((PLANE, FEW, experts), low),
        pltpu.VMEM((PLANE, FEW, experts), low),
        pltpu.VMEM((held, FEW), low),
        pltpu.VMEM((8, LANES), full),
        pltpu.VMEM((8, LANES), full),
    ]

    def sems(chunks, swaps):
        return [
            dma((6,)), dma, dma((3,)), dma, dma((chunks,)), dma, dma((chunks,)),
            dma, dma, dma((swaps,)), dma((swaps,)),
        ]

    def call(body, results, scratch, number):
        return pl.pallas_call(
            body,
            out_shape=tuple(results),
            in_specs=[smem, hbm, hbm, hbm, vmem, vmem, hbm, hbm],
            out_specs=(vmem,) * 4 + (smem,) * (len(results) - 4),
            scratch_shapes=scratch,
            compiler_params=pltpu.CompilerParams(
                collective_id=number, has_side_effects=True, vmem_limit_bytes=50 << 20
            ),
        )(*operands)

    def store(*results):
        return pl.pallas_call(
            write_out,
            out_shape=tuple(jax.ShapeDtypeStruct(shape, dtype) for shape, dtype in outs),
            in_specs=[vmem] * 4,
            out_specs=(anywhere,) * 4,
            scratch_shapes=[dma((4,))],
            compiler_params=pltpu.CompilerParams(vmem_limit_bytes=1 << 20),
        )(*(pltpu.with_memory_space_constraint(r, pltpu.VMEM) for r in results))

    *results, flag = call(
        lean_kernel,
        kept + (jax.ShapeDtypeStruct((1, 1), full),),
        small + shared(slots - 1, (slots - 1) * experts + FEW, PARTS, [pltpu.VMEM(shape, kind) for shape in ((width, half), (half, width)) for kind in (low, low, full)]) + thirds + sems(PARTS, 3) + [dma((6,)), dma((6,)), dma((2,)), dma((2,))],
        0,
    )

    def padded(*unused):
        return store(*call(padded_kernel, kept, small + shared(slots, total, CHUNKS, [pltpu.VMEM(shape, full) for shape in ((width, half), (half, width)) for _ in range(2)]) + sems(CHUNKS, 2), 1))

    d_tokens, d_gate, d_up, d_down = lax.cond(flag[0, 0] > 0.5, padded, store, *results)
    return d_tokens[None], d_gate.T[None, None], d_up[None], d_down[None]


def solution(mesh):
    in_specs = (
        P("dp", "expert", None),
        P("dp", "expert", None),
        P("dp", "expert", None, None),
        P("dp", "expert", None, None),
        P("dp", "expert", None),
        P("expert", None, "dp"),
        P("expert", "dp", None),
    )
    out_specs = (
        P("dp", "expert", None),
        P("dp", "expert", None, None),
        P("expert", None, "dp"),
        P("expert", "dp", None),
    )
    return jax.shard_map(
        per_device, mesh=mesh, in_specs=in_specs, out_specs=out_specs, check_vma=False
    )
```

```python
import jax
import jax.numpy as jnp
from jax import lax
from jax.experimental import pallas as pl
from jax.experimental.pallas import tpu as pltpu
from jax.sharding import PartitionSpec as P

MESH = pl.DeviceIdType.MESH
NX, NY, NZ = 4, 4, 8
N = NX * NY * NZ
CHUNKS = NX
PEERS = NY * NZ
LANES = 128
SUB = 16
WIDE = SUB * LANES
PLANE = NX * NY
PAIRS = PLANE * PLANE
CAP = 96
FEW = 64
PARTS = 2


def place(me):
    return me % NX, (me // NX) % NY, me // (NX * NY)


def block_of(q, z, y):
    return q * PEERS + z * NY + y


def expert_of(q, z, y):
    return (z * NY + y) * NX + lax.rem(q - y + NX, NX)


def hop(i):
    return lax.rem(i, NZ), lax.div(i, NZ)


def bf16(v):
    return v.astype(jnp.bfloat16)


def dot(a, b, dims=((1,), (0,))):
    return lax.dot_general(a, b, (dims, ((), ())), preferred_element_type=jnp.float32)


def local_wait(ref, sem):
    pltpu.make_async_copy(ref, ref, sem).wait()


def padded_kernel(
    idx_ref, pick_hbm, gates_hbm, count_hbm, tok_ref, grad_ref, up_ref, down_ref,
    dtok_ref, dgate_ref, dup_ref, ddown_ref,
    pick_ref, gates_ref, count_ref, tok, grad, scale_vec, scale, gback,
    send, recv, wu, wd, rows_x, rows_g, act, dhid, drow, dsend, back, gsend,
    up_out, up_in, down_out, down_in, total, perm,
    w_sem, s_sem, small_sem, f_send, f_recv, r_send, r_recv, g_send, g_recv, d_send, d_recv,
):
    me = lax.axis_index("expert")
    core = lax.axis_index("dp")
    x, y, z = place(me)
    q_me = lax.rem(x + y, NX)
    slots = send.shape[2]
    per_chunk = PEERS * slots
    half = up_ref.shape[1]
    mine = pl.ds(pl.multiple_of(core * half, LANES), half)
    theirs = pl.ds(pl.multiple_of((1 - core) * half, LANES), half)
    partner = {"dp": 1 - core}

    barrier = pltpu.get_barrier_semaphore()
    pl.semaphore_signal(barrier, inc=1, device_id=partner, device_id_type=MESH)

    def greet(step, carry):
        pl.semaphore_signal(
            barrier, inc=1, device_id={"expert": lax.rem(me + step, N)}, device_id_type=MESH
        )
        return carry

    lax.fori_loop(1, N, greet, 0)

    own_up = pltpu.make_async_copy(up_ref, wu.at[:, mine], w_sem.at[0])
    own_up.start()
    own_down = pltpu.make_async_copy(down_ref, wd.at[mine, :], w_sem.at[1])
    own_down.start()

    small = [
        pltpu.make_async_copy(src, dst, small_sem.at[i])
        for i, (src, dst) in enumerate(
            ((gates_hbm, gates_ref), (count_hbm, count_ref), (pick_hbm, pick_ref))
        )
    ]
    for copy in small:
        copy.start()

    a = lax.broadcasted_iota(jnp.int32, (SUB * SUB, SUB * SUB), 0)
    b = lax.broadcasted_iota(jnp.int32, (SUB * SUB, SUB * SUB), 1)
    swap = (lax.rem(a, SUB) == lax.div(b, SUB)) & (lax.div(a, SUB) == lax.rem(b, SUB))
    perm[...] = jnp.where(swap, 1.0, 0.0).astype(jnp.bfloat16)

    for copy in small:
        copy.wait()
    scale_vec[...] = jnp.zeros_like(scale_vec)
    for k in range(slots):
        live = jnp.where(count_ref[...] > k, 1.0, 0.0)
        scale_vec[k : k + 1, :] = live * gates_ref[k : k + 1, :].astype(jnp.float32)
    to_scalars = pltpu.make_async_copy(scale_vec, scale, s_sem)
    to_scalars.start()

    def by_row(g, carry):
        r = pl.ds(pl.multiple_of(g * SUB, SUB), SUB)
        both = jnp.concatenate(
            [
                jnp.concatenate(
                    [ref[r, f * LANES : (f + 1) * LANES] for f in range(SUB)], axis=0
                )
                for ref in (tok_ref, grad_ref)
            ],
            axis=1,
        )
        out = bf16(dot(perm[...], both))
        tok[r] = out[:, :LANES].reshape(SUB, SUB, LANES)
        grad[r] = out[:, LANES:].reshape(SUB, SUB, LANES)
        return carry

    lax.fori_loop(0, tok.shape[0] // SUB, by_row, 0)
    to_scalars.wait()

    def fill(target):
        for k in range(slots):
            row = idx_ref[k, 0, target]
            send[target, 0, k] = tok[row]
            send[target, 1, k] = bf16(grad[row].astype(jnp.float32) * scale[k, target])

    pl.semaphore_wait(barrier, N)

    up_copy = pltpu.make_async_remote_copy(
        src_ref=up_ref, dst_ref=wu.at[:, mine], send_sem=w_sem.at[2], recv_sem=w_sem.at[3],
        device_id=partner, device_id_type=MESH,
    )
    up_copy.start()
    down_copy = pltpu.make_async_remote_copy(
        src_ref=down_ref, dst_ref=wd.at[mine, :], send_sem=w_sem.at[4], recv_sem=w_sem.at[5],
        device_id=partner, device_id_type=MESH,
    )
    down_copy.start()

    my_rows = pl.ds(block_of(q_me, z, y) * slots, slots)

    def push(n, carry):
        c = lax.div(n, PEERS)
        dz, dy = hop(lax.rem(n, PEERS))
        target = expert_of(lax.rem(q_me + c, NX), lax.rem(z + dz, NZ), lax.rem(y + dy, NY))
        fill(target)
        pltpu.make_async_remote_copy(
            src_ref=send.at[target], dst_ref=recv.at[:, my_rows],
            send_sem=f_send, recv_sem=f_recv.at[c],
            device_id={"expert": target}, device_id_type=MESH,
        ).start()
        return carry

    lax.fori_loop(1, N, push, 0)
    fill(me)
    pltpu.make_async_copy(send.at[me], recv.at[:, my_rows], f_recv.at[0]).start()

    own_up.wait()
    own_down.wait()
    up_copy.wait()
    down_copy.wait()

    groups = per_chunk // SUB
    grid_a = lax.broadcasted_iota(jnp.int32, (PEERS, per_chunk), 0)
    grid_b = lax.broadcasted_iota(jnp.int32, (PEERS, per_chunk), 1)
    to_peer = jnp.where(lax.div(grid_b, slots) == grid_a, 1.0, 0.0)
    row_id = lax.broadcasted_iota(jnp.int32, (per_chunk, LANES), 0)
    lane_id = lax.broadcasted_iota(jnp.int32, (per_chunk, LANES), 1)
    to_lane = jnp.where(lax.rem(row_id, slots) == lane_id, 1.0, 0.0)

    def chunk(c, carry):
        q = lax.rem(q_me - c + NX, NX)
        first = pl.multiple_of(q * per_chunk, SUB)
        local_wait(recv.at[:, pl.ds(0, per_chunk)], f_recv.at[c])

        def unpack(g, inner):
            r = pl.ds(pl.multiple_of(first + g * SUB, SUB), SUB)
            both = jnp.concatenate(
                [recv[0, r].reshape(SUB * SUB, LANES), recv[1, r].reshape(SUB * SUB, LANES)], axis=1
            )
            out = bf16(dot(perm[...], both))
            for f in range(SUB):
                part = out[f * SUB : (f + 1) * SUB]
                rows_x[r, f * LANES : (f + 1) * LANES] = part[:, :LANES]
                rows_g[r, f * LANES : (f + 1) * LANES] = part[:, LANES:]
            return inner

        lax.fori_loop(0, groups, unpack, 0)

        here = pl.ds(first, per_chunk)
        gate = jnp.zeros((per_chunk, 1), jnp.float32)
        for t in range(2 * half // 256):
            cols = slice(t * 256, (t + 1) * 256)
            hidden = dot(rows_x[here, :], wu[:, cols])
            upstream = dot(rows_g[here, :], wd[cols, :], ((1,), (1,)))
            s = jax.nn.sigmoid(hidden)
            activation = bf16(hidden * s)
            act[here, cols] = activation
            dhid[here, cols] = bf16(upstream * (s * (1.0 + hidden * (1.0 - s))))
            gate += jnp.sum(activation.astype(jnp.float32) * upstream, axis=1, keepdims=True)

        for t in range(WIDE // 512):
            cols = slice(t * 512, (t + 1) * 512)
            drow[:, cols] = bf16(dot(dhid[here, :], wu[cols, :], ((1,), (1,))))

        for g in range(0, groups, 2):
            pair = [
                jnp.concatenate(
                    [
                        drow[(g + h) * SUB : (g + h + 1) * SUB, f * LANES : (f + 1) * LANES]
                        for f in range(SUB)
                    ],
                    axis=0,
                )
                for h in range(2)
            ]
            out = bf16(dot(perm[...], jnp.concatenate(pair, axis=1)))
            for h in range(2):
                r = pl.ds(pl.multiple_of(first + (g + h) * SUB, SUB), SUB)
                dsend[r] = out[:, h * LANES : (h + 1) * LANES].reshape(SUB, SUB, LANES)

        @pl.when(c == 0)
        def _():
            pltpu.make_async_copy(dsend.at[my_rows], back.at[my_rows], r_recv.at[0]).start()

        def reply(i, inner):
            dz, dy = hop(i)
            zz, yy = lax.rem(z - dz + NZ, NZ), lax.rem(y - dy + NY, NY)
            source = pl.ds(block_of(q, zz, yy) * slots, slots)
            pltpu.make_async_remote_copy(
                src_ref=dsend.at[source], dst_ref=back.at[my_rows],
                send_sem=r_send, recv_sem=r_recv.at[c],
                device_id={"expert": expert_of(q, zz, yy)}, device_id_type=MESH,
            ).start()
            return inner

        lax.fori_loop(jnp.where(c == 0, 1, 0), PEERS, reply, 0)

        spread = lax.dot_general(
            to_peer, gate * to_lane, (((1,), (0,)), ((), ())),
            precision=lax.Precision.HIGHEST, preferred_element_type=jnp.float32,
        )
        gsend[pl.ds(q * PEERS, PEERS)] = spread.reshape(PEERS, 1, LANES)
        return carry

    lax.fori_loop(0, CHUNKS, chunk, 0)

    pltpu.make_async_copy(gsend.at[block_of(q_me, z, y)], gback.at[me], g_recv).start()

    def reply_gate(n, carry):
        c = lax.div(n, PEERS)
        dz, dy = hop(lax.rem(n, PEERS))
        q, zz, yy = lax.rem(q_me - c + NX, NX), lax.rem(z - dz + NZ, NZ), lax.rem(y - dy + NY, NY)
        pltpu.make_async_remote_copy(
            src_ref=gsend.at[block_of(q, zz, yy)], dst_ref=gback.at[me],
            send_sem=g_send, recv_sem=g_recv,
            device_id={"expert": expert_of(q, zz, yy)}, device_id_type=MESH,
        ).start()
        return carry

    lax.fori_loop(1, N, reply_gate, 0)

    tiles = WIDE // 512
    for t in range(tiles):
        cols = slice(t * 512, (t + 1) * 512)
        up_out[cols, :] = dot(rows_x[:, cols], dhid[:, theirs], ((0,), (0,)))
    up_swap = pltpu.make_async_remote_copy(
        src_ref=up_out, dst_ref=up_in, send_sem=d_send.at[0], recv_sem=d_recv.at[0],
        device_id=partner, device_id_type=MESH,
    )
    up_swap.start()
    for t in range(tiles):
        cols = slice(t * 512, (t + 1) * 512)
        down_out[:, cols] = dot(act[:, theirs], rows_g[:, cols], ((0,), (0,)))
    down_swap = pltpu.make_async_remote_copy(
        src_ref=down_out, dst_ref=down_in, send_sem=d_send.at[1], recv_sem=d_recv.at[1],
        device_id=partner, device_id_type=MESH,
    )
    down_swap.start()
    up_swap.wait()
    for t in range(tiles):
        cols = slice(t * 512, (t + 1) * 512)
        both = dot(rows_x[:, cols], dhid[:, mine], ((0,), (0,))) + up_in[cols, :]
        dup_ref[cols, :] = bf16(both)
    down_swap.wait()
    for t in range(tiles):
        cols = slice(t * 512, (t + 1) * 512)
        both = dot(act[:, mine], rows_g[:, cols], ((0,), (0,))) + down_in[:, cols]
        ddown_ref[:, cols] = bf16(both)

    total[...] = jnp.zeros_like(total)

    def combine(c, carry):
        q = lax.rem(q_me + c, NX)
        first = pl.multiple_of(q * per_chunk, SUB)
        local_wait(back.at[pl.ds(0, per_chunk)], r_recv.at[c])
        for g in range(0, groups, 2):
            pair = [
                back[pl.ds(pl.multiple_of(first + (g + h) * SUB, SUB), SUB)].reshape(SUB * SUB, LANES)
                for h in range(2)
            ]
            out = bf16(dot(perm[...], jnp.concatenate(pair, axis=1)))
            for h in range(2):
                for f in range(SUB):
                    drow[(g + h) * SUB : (g + h + 1) * SUB, f * LANES : (f + 1) * LANES] = out[
                        f * SUB : (f + 1) * SUB, h * LANES : (h + 1) * LANES
                    ]
        expert = lax.broadcasted_iota(jnp.int32, (N, per_chunk), 0)
        peer = lax.div(lax.broadcasted_iota(jnp.int32, (N, per_chunk), 1), slots)
        owner = expert_of(q, lax.div(peer, NY), lax.rem(peer, NY))
        owned = jnp.where(expert == owner, 1.0, 0.0)
        slot = lax.rem(lax.broadcasted_iota(jnp.int32, (1, per_chunk), 1), slots)
        picked = jnp.zeros((1, per_chunk), jnp.float32)
        for k in range(slots):
            picked += jnp.where(slot == k, dot(pick_ref[k].astype(jnp.float32), owned), 0.0)
        token = lax.broadcasted_iota(jnp.int32, (total.shape[0], per_chunk), 0)
        chosen = bf16(jnp.where(token.astype(jnp.float32) == picked, 1.0, 0.0))
        for t in range(tiles):
            cols = slice(t * 512, (t + 1) * 512)
            total[:, cols] += dot(chosen, drow[:, cols])
        return carry

    lax.fori_loop(0, CHUNKS, combine, 0)
    dtok_ref[...] = bf16(total[...])

    local_wait(gback, g_recv)
    eye = jnp.where(
        lax.broadcasted_iota(jnp.int32, (8, LANES), 0)
        == lax.broadcasted_iota(jnp.int32, (8, LANES), 1),
        1.0,
        0.0,
    )
    by_slot = lax.dot_general(
        eye, gback[...].reshape(N, LANES), (((1,), (1,)), ((), ())),
        precision=lax.Precision.HIGHEST, preferred_element_type=jnp.float32,
    )
    for k in range(slots):
        c = scale_vec[k : k + 1, :]
        inverse = jnp.where(c > 0.0, 1.0 / jnp.where(c > 0.0, c, 1.0), 0.0)
        dgate_ref[k : k + 1, :] = bf16(by_slot[k : k + 1, :] * inverse)
    local_wait(gsend.at[pl.ds(0, N - 1)], g_send)
    local_wait(send.at[pl.ds(0, N - 1)], f_send)
    local_wait(dsend.at[pl.ds(0, (N - 1) * slots)], r_send)


def lean_kernel(
    idx_ref, pick_hbm, gates_hbm, count_hbm, tok_ref, grad_ref, up_ref, down_ref,
    dtok_ref, dgate_ref, dup_ref, ddown_ref, over_ref,
    pick_ref, gates_ref, count_ref, tok, grad, scale_vec, scale, gback,
    send, recv, wu, wd, rows_x, rows_g, act, dhid, drow, dsend, back, gsend,
    up_out, up_in, up_own, down_out, down_in, down_own, total, perm, above,
    third, r1_in, r1, meta1, live3, o2, r2, meta2, got2, o3, o3_out, r3,
    d3, rr1_in, rr1, ro2, rr2, ro3, ro3_out, d3back, pack_out, pack_in, pack_src, pack_dst, own_pick, flag_ref, flag_in,
    w_sem, s_sem, small_sem, f_send, f_recv, r_send, r_recv, g_send, g_recv, d_send, d_recv,
    t_send, t_recv, m_send, m_recv,
):
    me = lax.axis_index("expert")
    core = lax.axis_index("dp")
    x, y, z = place(me)
    p = lax.rem(me, PLANE)
    q_me = lax.rem(x + y, NX)
    slots = pick_ref.shape[0]
    direct = send.shape[2]
    quarter = PEERS * direct
    per_chunk = recv.shape[1] // PARTS
    half = up_ref.shape[1]
    mine = pl.ds(pl.multiple_of(core * half, LANES), half)
    partner = {"dp": 1 - core}
    my_lanes = pl.ds(pl.multiple_of(p * LANES, LANES), LANES)

    barrier = pltpu.get_barrier_semaphore()
    pl.semaphore_signal(barrier, inc=1, device_id=partner, device_id_type=MESH)

    def greet(step, carry):
        pl.semaphore_signal(
            barrier, inc=1, device_id={"expert": lax.rem(me + step, N)}, device_id_type=MESH
        )
        return carry

    lax.fori_loop(1, N, greet, 0)

    small = [
        pltpu.make_async_copy(src, dst, small_sem.at[i])
        for i, (src, dst) in enumerate(
            ((gates_hbm, gates_ref), (count_hbm, count_ref), (pick_hbm, pick_ref))
        )
    ]
    for copy in small:
        copy.start()
    own_up = pltpu.make_async_copy(up_ref, wu.at[:, mine], w_sem.at[0])
    own_up.start()
    own_down = pltpu.make_async_copy(down_ref, wd.at[mine, :], w_sem.at[1])
    own_down.start()

    a = lax.broadcasted_iota(jnp.int32, (PAIRS, PAIRS), 0)
    b = lax.broadcasted_iota(jnp.int32, (PAIRS, PAIRS), 1)
    swap = (lax.rem(a, SUB) == lax.div(b, SUB)) & (lax.div(a, SUB) == lax.rem(b, SUB))
    perm[...] = bf16(jnp.where(swap, 1.0, 0.0))
    above[...] = bf16(jnp.where(a < b, 1.0, 0.0))

    for copy in small:
        copy.wait()
    scale_vec[...] = jnp.zeros_like(scale_vec)
    for k in range(slots):
        live = jnp.where(count_ref[...] > k, 1.0, 0.0)
        scale_vec[k : k + 1, :] = live * gates_ref[k : k + 1, :].astype(jnp.float32)
        live3[0] = live
    to_scalars = pltpu.make_async_copy(scale_vec, scale, s_sem)
    to_scalars.start()

    few = lax.broadcasted_iota(jnp.int32, (FEW, N), 0).astype(jnp.float32)

    def squeeze(live):
        position = dot(bf16(live), above[:N, :N])
        return bf16(jnp.where((few == position) & (live > 0.5), 1.0, 0.0))

    token = lax.broadcasted_iota(jnp.int32, (tok.shape[0], N), 0)
    last_pick = jnp.where(token == pick_ref[slots - 1], 1.0, 0.0)
    last_scaled = bf16(last_pick * scale_vec[slots - 1 : slots, :])
    squeezed = squeeze(live3[0])
    own_pick[...] = bf16(dot(bf16(last_pick), squeezed, ((1,), (1,))))
    chosen_rows = bf16(dot(squeezed, bf16(last_pick), ((1,), (1,))))
    scaled_rows = bf16(dot(squeezed, last_scaled, ((1,), (1,))))
    for t in range(WIDE // 512):
        cols = slice(t * 512, (t + 1) * 512)
        row_part = bf16(dot(chosen_rows, tok_ref[:, cols]))
        grad_part = bf16(dot(scaled_rows, grad_ref[:, cols]))
        for m in range(512 // LANES):
            lanes = slice(m * LANES, (m + 1) * LANES)
            third[t * 512 // LANES + m, :, :LANES] = row_part[:, lanes]
            third[t * 512 // LANES + m, :, LANES:] = grad_part[:, lanes]

    def by_row(g, carry):
        r = pl.ds(pl.multiple_of(g * SUB, SUB), SUB)
        both = jnp.concatenate(
            [
                jnp.concatenate([ref[r, f * LANES : (f + 1) * LANES] for f in range(SUB)], axis=0)
                for ref in (tok_ref, grad_ref)
            ],
            axis=1,
        )
        out = bf16(dot(perm[...], both))
        tok[r] = out[:, :LANES].reshape(SUB, SUB, LANES)
        grad[r] = out[:, LANES:].reshape(SUB, SUB, LANES)
        return carry

    lax.fori_loop(0, tok.shape[0] // SUB, by_row, 0)
    to_scalars.wait()

    def ship(src, dst, target, send_sem, recv_sem):
        pltpu.make_async_remote_copy(
            src_ref=src, dst_ref=dst, send_sem=send_sem, recv_sem=recv_sem,
            device_id={"expert": target}, device_id_type=MESH,
        ).start()

    def in_plane(src_of, dst, sem):
        def one(k, carry):
            peer = lax.rem(p + k, PLANE)
            ship(src_of(peer), dst, z * PLANE + peer, t_send.at[sem], t_recv.at[sem])
            return carry

        pltpu.make_async_copy(src_of(p), dst, t_recv.at[sem]).start()
        lax.fori_loop(1, PLANE, one, 0)

    def along_z(src, dst, sems):
        def one(k, carry):
            zz = lax.rem(z + k, NZ)
            ship(src.at[zz], dst.at[z], zz * PLANE + p, sems[0], sems[1])
            return carry

        pltpu.make_async_copy(src.at[z], dst.at[z], sems[1]).start()
        lax.fori_loop(1, NZ, one, 0)

    my_peer = (z * NY + y) * direct

    def rows_at(c):
        return pl.ds(c * quarter + my_peer, direct)

    def fill(target):
        for k in range(direct):
            row = idx_ref[k, 0, target]
            send[target, 0, k] = tok[row]
            send[target, 1, k] = bf16(grad[row].astype(jnp.float32) * scale[k, target])

    def target_of(c, i):
        dz, dy = hop(i)
        return expert_of(lax.rem(q_me + c, NX), lax.rem(z + dz, NZ), lax.rem(y + dy, NY))

    def fill_first(i, carry):
        fill(target_of(0, i))
        return carry

    def push_part(c):
        def push(i, carry):
            target = target_of(c, i)
            if c > 0:
                fill(target)
            ship(send.at[target], recv.at[:, rows_at(c)], target, f_send, f_recv.at[c * PARTS // NX])
            return carry

        if c == 0:
            pltpu.make_async_copy(send.at[me], recv.at[:, rows_at(0)], f_recv.at[0]).start()
        lax.fori_loop(1 if c == 0 else 0, PEERS, push, 0)

    lax.fori_loop(0, PEERS, fill_first, 0)
    pl.semaphore_wait(barrier, N)

    push_part(0)

    in_plane(lambda m: third.at[m], r1_in.at[p], 0)

    def tell(k, carry):
        ship(live3.at[0], meta1.at[p], z * PLANE + lax.rem(p + k, PLANE), m_send.at[0], m_recv.at[0])
        return carry

    pltpu.make_async_copy(live3.at[0], meta1.at[p], m_recv.at[0]).start()
    lax.fori_loop(1, PLANE, tell, 0)

    up_copy = pltpu.make_async_remote_copy(
        src_ref=up_ref, dst_ref=wu.at[:, mine], send_sem=w_sem.at[2], recv_sem=w_sem.at[3],
        device_id=partner, device_id_type=MESH,
    )
    up_copy.start()
    down_copy = pltpu.make_async_remote_copy(
        src_ref=down_ref, dst_ref=wd.at[mine, :], send_sem=w_sem.at[4], recv_sem=w_sem.at[5],
        device_id=partner, device_id_type=MESH,
    )
    down_copy.start()

    row_a = lax.broadcasted_iota(jnp.int32, (N, PAIRS), 0)
    col_a = lax.broadcasted_iota(jnp.int32, (N, PAIRS), 1)
    col_p = lax.broadcasted_iota(jnp.int32, (PLANE, PAIRS), 1)
    row_p = lax.broadcasted_iota(jnp.int32, (PLANE, PAIRS), 0)
    rank = lax.broadcasted_iota(jnp.int32, (CAP, PAIRS), 0).astype(jnp.float32)

    def pack(zz, over):
        pick_plane = jnp.where(row_a == zz * PLANE + lax.rem(col_a, PLANE), 1.0, 0.0)
        spread = dot(meta1[...].reshape(PLANE, LANES), pick_plane)
        own = jnp.where(lax.div(col_p, PLANE) == row_p, spread, 0.0)
        live = jnp.sum(own, axis=0, keepdims=True)
        position = dot(bf16(live), above[...])
        chosen = bf16(jnp.where((rank == position) & (live > 0.5), 1.0, 0.0))
        pack_out[zz] = chosen
        meta2[zz, :, :PAIRS] = live
        source = jnp.concatenate(
            [r1[j, pl.ds(pl.multiple_of(zz * PLANE, PLANE), PLANE)] for j in range(PLANE)], axis=0
        )
        o2[zz] = bf16(dot(chosen, source))
        return jnp.maximum(over, jnp.sum(live, axis=1, keepdims=True))

    def send_thirds():
        local_wait(meta1, m_recv.at[0])
        local_wait(r1_in, t_recv.at[0])

        def widen(j, crowd):
            live = meta1[j]
            chosen = squeeze(live)
            pack_src[j] = chosen
            r1[j] = bf16(dot(chosen, r1_in[j], ((0,), (0,))))
            return jnp.maximum(crowd, jnp.sum(live, axis=1, keepdims=True))

        crowd = lax.fori_loop(0, PLANE, widen, jnp.zeros((1, 1), jnp.float32))
        most = lax.fori_loop(0, NZ, pack, jnp.zeros((1, 1), jnp.float32))
        over = jnp.broadcast_to(jnp.where((most > CAP) | (crowd > FEW), 1.0, 0.0), (1, LANES))
        for j in range(NZ):
            meta2[j, :, PAIRS:] = over
        along_z(meta2, got2, (m_send.at[1], m_recv.at[1]))
        along_z(o2, r2, (t_send.at[1], t_recv.at[1]))

    def compute(first, rows):
        here = pl.ds(first, rows)
        gate = jnp.zeros((rows, 1), jnp.float32)
        for t in range(2 * half // 256):
            cols = slice(t * 256, (t + 1) * 256)
            hidden = dot(rows_x[here, :], wu[:, cols])
            upstream = dot(rows_g[here, :], wd[cols, :], ((1,), (1,)))
            s = jax.nn.sigmoid(hidden)
            activation = bf16(hidden * s)
            act[here, cols] = activation
            dhid[here, cols] = bf16(upstream * (s * (1.0 + hidden * (1.0 - s))))
            gate += jnp.sum(activation.astype(jnp.float32) * upstream, axis=1, keepdims=True)
        return gate

    def row_grads(first, rows, out):
        for t in range(WIDE // 512):
            cols = slice(t * 512, (t + 1) * 512)
            out[:rows, cols] = bf16(dot(dhid[pl.ds(first, rows), :], wu[cols, :], ((1,), (1,))))

    def peer_ids(c, sign, shape, axis):
        row = lax.broadcasted_iota(jnp.int32, shape, axis) + c * per_chunk
        turn = lax.div(row, quarter)
        peer = lax.div(lax.rem(row, quarter), direct)
        q = lax.rem(q_me + sign * turn + NX, NX)
        return expert_of(q, lax.div(peer, NY), lax.rem(peer, NY)), lax.rem(row, direct)

    groups = per_chunk // SUB
    gsend[...] = jnp.zeros_like(gsend)

    def chunk(c):
        first = c * per_chunk
        local_wait(recv.at[:, pl.ds(0, per_chunk)], f_recv.at[c])

        def unpack(g, inner):
            r = pl.ds(pl.multiple_of(first + g * SUB, SUB), SUB)
            both = jnp.concatenate(
                [recv[0, r].reshape(PAIRS, LANES), recv[1, r].reshape(PAIRS, LANES)], axis=1
            )
            out = bf16(dot(perm[...], both))
            for f in range(SUB):
                part = out[f * SUB : (f + 1) * SUB]
                rows_x[r, f * LANES : (f + 1) * LANES] = part[:, :LANES]
                rows_g[r, f * LANES : (f + 1) * LANES] = part[:, LANES:]
            return inner

        lax.fori_loop(0, groups, unpack, 0)
        gate = compute(first, per_chunk)
        row_grads(first, per_chunk, drow)

        for g in range(0, groups, 2):
            pair = [
                jnp.concatenate(
                    [
                        drow[(g + h) * SUB : (g + h + 1) * SUB, f * LANES : (f + 1) * LANES]
                        for f in range(SUB)
                    ],
                    axis=0,
                )
                for h in range(2)
            ]
            out = bf16(dot(perm[...], jnp.concatenate(pair, axis=1)))
            for h in range(2):
                r = pl.ds(first + (g + h) * SUB, SUB)
                dsend[r] = out[:, h * LANES : (h + 1) * LANES].reshape(SUB, SUB, LANES)

        if c == 0:
            pltpu.make_async_copy(dsend.at[rows_at(0)], back.at[rows_at(0)], r_recv.at[0]).start()

        def reply(n, inner):
            turn = lax.div(n, PEERS)
            dz, dy = hop(lax.rem(n, PEERS))
            q = lax.rem(q_me - turn + NX, NX)
            zz, yy = lax.rem(z - dz + NZ, NZ), lax.rem(y - dy + NY, NY)
            source = pl.ds(turn * quarter + (zz * NY + yy) * direct, direct)
            ship(
                dsend.at[source], back.at[rows_at(turn)], expert_of(q, zz, yy),
                r_send, r_recv.at[c],
            )
            return inner

        span = N // PARTS
        lax.fori_loop(max(1, c * span), (c + 1) * span, reply, 0)

        owner, slot = peer_ids(c, -1, (1, per_chunk), 1)
        to_source = jnp.where(
            lax.broadcasted_iota(jnp.int32, (N, per_chunk), 0) == owner, 1.0, 0.0
        )
        _, slot = peer_ids(c, -1, (per_chunk, LANES), 0)
        to_lane = lax.broadcasted_iota(jnp.int32, (per_chunk, LANES), 1) == slot
        spread = lax.dot_general(
            to_source, jnp.where(to_lane, gate, 0.0), (((1,), (0,)), ((), ())),
            precision=lax.Precision.HIGHEST, preferred_element_type=jnp.float32,
        )
        gsend[...] += spread.reshape(N, 1, LANES)

    def open_thirds():
        local_wait(got2, m_recv.at[1])
        local_wait(r2, t_recv.at[1])
        flag = jnp.zeros((1, LANES), jnp.float32)
        for j in range(NZ):
            flag = jnp.maximum(flag, got2[j, :, PAIRS:])
        flag_ref[...] = jnp.broadcast_to(flag, flag_ref.shape)

        def one(zz, carry):
            live = got2[zz][:, :PAIRS]
            position = dot(bf16(live), above[...])
            live = dot(bf16(live), perm[...])
            position = dot(bf16(position), perm[...])
            chosen = bf16(jnp.where((rank == position) & (live > 0.5), 1.0, 0.0))
            pack_in[zz] = chosen
            out = bf16(dot(chosen, r2[zz], ((0,), (0,))))
            for j in range(PLANE):
                o3[j, pl.ds(pl.multiple_of(zz * PLANE, PLANE), PLANE)] = out[j * SUB : (j + 1) * SUB]
            return carry

        lax.fori_loop(0, NZ, one, 0)
        flags = got2[...].reshape(NZ, PAIRS + LANES)[:, :PAIRS]
        row_s = lax.broadcasted_iota(jnp.int32, (PAIRS, N), 0)
        col_s = lax.broadcasted_iota(jnp.int32, (PAIRS, N), 1)
        row_z = lax.broadcasted_iota(jnp.int32, (NZ, N), 0)
        col_z = lax.broadcasted_iota(jnp.int32, (NZ, N), 1)

        def narrow(j, carry):
            here = (lax.rem(row_s, PLANE) == j) & (lax.div(row_s, PLANE) == lax.rem(col_s, PLANE))
            spread = dot(flags, jnp.where(here, 1.0, 0.0))
            live = jnp.where(lax.div(col_z, PLANE) == row_z, spread, 0.0)
            chosen = squeeze(jnp.sum(live, axis=0, keepdims=True))
            pack_dst[j] = chosen
            o3_out[j] = bf16(dot(chosen, o3[j]))
            return carry

        lax.fori_loop(0, PLANE, narrow, 0)
        in_plane(lambda m: o3_out.at[m], r3.at[p], 2)

    def run_thirds():
        local_wait(r3, t_recv.at[2])
        first = recv.shape[1]
        for m in range(PLANE):
            lanes = slice(m * LANES, (m + 1) * LANES)
            rows_x[first:, lanes] = r3[m, :, :LANES]
            rows_g[first:, lanes] = r3[m, :, LANES:]
        gate = compute(first, FEW)
        row_grads(first, FEW, d3)
        in_plane(
            lambda m: d3.at[:, pl.ds(pl.multiple_of(m * LANES, LANES), LANES)], rr1_in.at[p], 3
        )
        lane = lax.broadcasted_iota(jnp.int32, (FEW, LANES), 1)
        spread = lax.dot_general(
            pack_dst[p].astype(jnp.float32), jnp.where(lane == slots - 1, gate, 0.0),
            (((0,), (0,)), ((), ())),
            precision=lax.Precision.HIGHEST, preferred_element_type=jnp.float32,
        )
        gsend[...] += spread.reshape(N, 1, LANES)

    def pack_back():
        local_wait(rr1_in, t_recv.at[3])

        def widen(j, carry):
            rr1[j] = bf16(dot(pack_dst[j], rr1_in[j], ((0,), (0,))))
            return carry

        lax.fori_loop(0, PLANE, widen, 0)

        def one(zz, carry):
            source = jnp.concatenate(
                [rr1[j, pl.ds(pl.multiple_of(zz * PLANE, PLANE), PLANE)] for j in range(PLANE)], axis=0
            )
            ro2[zz] = bf16(dot(pack_in[zz], source))
            return carry

        lax.fori_loop(0, NZ, one, 0)
        along_z(ro2, rr2, (t_send.at[4], t_recv.at[4]))

    def open_back():
        local_wait(rr2, t_recv.at[4])

        def one(zz, carry):
            out = bf16(dot(pack_out[zz], rr2[zz], ((0,), (0,))))
            for j in range(PLANE):
                ro3[j, pl.ds(pl.multiple_of(zz * PLANE, PLANE), PLANE)] = out[j * SUB : (j + 1) * SUB]
            return carry

        lax.fori_loop(0, NZ, one, 0)

        def narrow(j, carry):
            ro3_out[j] = bf16(dot(pack_src[j], ro3[j]))
            return carry

        lax.fori_loop(0, PLANE, narrow, 0)
        in_plane(lambda m: ro3_out.at[m], d3back.at[:, my_lanes], 5)

    def weights_here():
        own_up.wait()
        own_down.wait()
        up_copy.wait()
        down_copy.wait()

    tiles = WIDE // 512

    flag_swap = pltpu.make_async_remote_copy(
        src_ref=flag_ref, dst_ref=flag_in, send_sem=d_send.at[2], recv_sem=d_recv.at[2],
        device_id=partner, device_id_type=MESH,
    )
    up_swap = pltpu.make_async_remote_copy(
        src_ref=up_out, dst_ref=up_in, send_sem=d_send.at[0], recv_sem=d_recv.at[0],
        device_id=partner, device_id_type=MESH,
    )
    down_swap = pltpu.make_async_remote_copy(
        src_ref=down_out, dst_ref=down_in, send_sem=d_send.at[1], recv_sem=d_recv.at[1],
        device_id=partner, device_id_type=MESH,
    )

    def weight_grads():
        pltpu.make_async_copy(gsend.at[me], gback.at[me], g_recv).start()

        def reply_gate(n, carry):
            target = lax.rem(me + n, N)
            ship(gsend.at[target], gback.at[me], target, g_send, g_recv)
            return carry

        lax.fori_loop(1, N, reply_gate, 0)

        flag_swap.start()

        first_core = core == 0
        for t in range(tiles):
            cols = slice(t * 512, (t + 1) * 512)
            whole = dot(rows_x[:, cols], dhid[...], ((0,), (0,)))
            left, right = whole[:, :half], whole[:, half:]
            up_out[cols, :] = bf16(jnp.where(first_core, right, left))
            up_own[cols, :] = jnp.where(first_core, left, right)
        up_swap.start()
        for t in range(tiles):
            cols = slice(t * 512, (t + 1) * 512)
            whole = dot(act[...], rows_g[:, cols], ((0,), (0,)))
            left, right = whole[:half], whole[half:]
            down_out[:, cols] = bf16(jnp.where(first_core, right, left))
            down_own[:, cols] = jnp.where(first_core, left, right)
        down_swap.start()

    def finish_grads():
        up_swap.wait()
        for t in range(tiles):
            cols = slice(t * 512, (t + 1) * 512)
            dup_ref[cols, :] = bf16(up_own[cols, :] + up_in[cols, :].astype(jnp.float32))
        down_swap.wait()
        for t in range(tiles):
            cols = slice(t * 512, (t + 1) * 512)
            ddown_ref[:, cols] = bf16(down_own[:, cols] + down_in[:, cols].astype(jnp.float32))
        flag_swap.wait()
        over_ref[0, 0] = jnp.max(jnp.maximum(flag_ref[...], flag_in[...]))

    def finish_rows():
        total[...] = jnp.zeros_like(total)

        def combine(c, carry):
            first = pl.multiple_of(c * per_chunk, SUB)
            local_wait(back.at[pl.ds(0, per_chunk)], r_recv.at[c])
            for g in range(0, groups, 2):
                pair = [
                    back[pl.ds(pl.multiple_of(first + (g + h) * SUB, SUB), SUB)].reshape(PAIRS, LANES)
                    for h in range(2)
                ]
                out = bf16(dot(perm[...], jnp.concatenate(pair, axis=1)))
                for h in range(2):
                    for f in range(SUB):
                        drow[(g + h) * SUB : (g + h + 1) * SUB, f * LANES : (f + 1) * LANES] = out[
                            f * SUB : (f + 1) * SUB, h * LANES : (h + 1) * LANES
                        ]
            owner, slot = peer_ids(c, 1, (1, per_chunk), 1)
            owned = jnp.where(
                lax.broadcasted_iota(jnp.int32, (N, per_chunk), 0) == owner, 1.0, 0.0
            )
            picked = jnp.zeros((1, per_chunk), jnp.float32)
            for k in range(direct):
                picked += jnp.where(slot == k, dot(pick_ref[k].astype(jnp.float32), owned), 0.0)
            rows = lax.broadcasted_iota(jnp.int32, (total.shape[0], per_chunk), 0)
            chosen = bf16(jnp.where(rows.astype(jnp.float32) == picked, 1.0, 0.0))
            for t in range(tiles):
                cols = slice(t * 512, (t + 1) * 512)
                total[:, cols] += dot(chosen, drow[:, cols])
            return carry

        lax.fori_loop(0, PARTS, combine, 0)
        local_wait(d3back, t_recv.at[5])
        for t in range(tiles):
            cols = slice(t * 512, (t + 1) * 512)
            dtok_ref[:, cols] = bf16(total[:, cols] + dot(own_pick[...], d3back[:, cols]))

    push_part(1)
    send_thirds()
    push_part(2)
    push_part(3)
    weights_here()
    chunk(0)
    open_thirds()
    run_thirds()
    chunk(1)
    pack_back()
    weight_grads()
    open_back()
    finish_grads()
    finish_rows()

    local_wait(gback, g_recv)
    eye = jnp.where(
        lax.broadcasted_iota(jnp.int32, (8, LANES), 0)
        == lax.broadcasted_iota(jnp.int32, (8, LANES), 1),
        1.0,
        0.0,
    )
    by_slot = lax.dot_general(
        eye, gback[...].reshape(N, LANES), (((1,), (1,)), ((), ())),
        precision=lax.Precision.HIGHEST, preferred_element_type=jnp.float32,
    )
    for k in range(slots):
        c = scale_vec[k : k + 1, :]
        inverse = jnp.where(c > 0.0, 1.0 / jnp.where(c > 0.0, c, 1.0), 0.0)
        dgate_ref[k : k + 1, :] = bf16(by_slot[k : k + 1, :] * inverse)

    local_wait(gsend.at[pl.ds(0, N - 1)], g_send)
    local_wait(send.at[pl.ds(0, N - 1)], f_send)
    local_wait(dsend.at[pl.ds(0, (N - 1) * direct)], r_send)
    local_wait(meta1.at[pl.ds(0, PLANE - 1)], m_send.at[0])
    local_wait(meta2.at[pl.ds(0, NZ - 1)], m_send.at[1])
    for i, ref in enumerate((third, o2, o3_out, rr1_in, ro2, ro3_out)):
        local_wait(ref.at[pl.ds(0, ref.shape[0] - 1)], t_send.at[i])


def write_out(*refs):
    count = len(refs) // 2
    copies = [
        pltpu.make_async_copy(refs[i], refs[count + i], refs[-1].at[i]) for i in range(count)
    ]
    for copy in copies:
        copy.start()
    for copy in copies:
        copy.wait()


def per_device(tokens, grad_out, gates, slot_index, slot_count, up_weight, down_weight):
    experts, slots = slot_index.shape[2:]
    held, width = tokens.shape[1:]
    half = up_weight.shape[2]
    total = experts * slots
    picks = jnp.transpose(slot_index[0], (2, 0, 1))

    vmem = pl.BlockSpec(memory_space=pltpu.VMEM)
    smem = pl.BlockSpec(memory_space=pltpu.SMEM)
    anywhere = pl.BlockSpec(memory_space=pl.ANY)
    hbm = pl.BlockSpec(memory_space=pltpu.HBM)
    low, full = jnp.bfloat16, jnp.float32

    def stay(array):
        return pltpu.with_memory_space_constraint(array, pltpu.HBM)

    dma = pltpu.SemaphoreType.DMA
    outs = (((held, width), low), ((slots, experts), low), ((width, half), low), ((half, width), low))
    kept = tuple(pltpu.VMEM(shape, dtype) for shape, dtype in outs)
    operands = (
        picks,
        stay(picks),
        stay(gates[0, 0].T),
        stay(slot_count[0]),
        tokens[0],
        grad_out[0],
        up_weight[0],
        down_weight[0],
    )
    small = [
        pltpu.VMEM((slots, 1, experts), jnp.int32),
        pltpu.VMEM((slots, experts), low),
        pltpu.VMEM((1, experts), jnp.int32),
        pltpu.VMEM((held, SUB, LANES), low),
        pltpu.VMEM((held, SUB, LANES), low),
        pltpu.VMEM((8, experts), full),
        pltpu.SMEM((8, experts), full),
        pltpu.VMEM((experts, 1, LANES), full),
    ]

    def shared(sent, rows, parts, swapped):
        return [
            pltpu.VMEM((experts, 2, sent, SUB, LANES), low),
            pltpu.VMEM((2, sent * experts, SUB, LANES), low),
            pltpu.VMEM((width, 2 * half), low),
            pltpu.VMEM((2 * half, width), low),
            pltpu.VMEM((rows, width), low),
            pltpu.VMEM((rows, width), low),
            pltpu.VMEM((rows, 2 * half), low),
            pltpu.VMEM((rows, 2 * half), low),
            pltpu.VMEM((sent * experts // parts, width), low),
            pltpu.VMEM((sent * experts, SUB, LANES), low),
            pltpu.VMEM((sent * experts, SUB, LANES), low),
            pltpu.VMEM((experts, 1, LANES), full),
            *swapped,
            pltpu.VMEM((held, width), full),
            pltpu.VMEM((PAIRS, PAIRS), low),
        ]

    thirds = [
        pltpu.VMEM((PAIRS, PAIRS), low),
        pltpu.VMEM((PLANE, FEW, 2 * LANES), low),
        pltpu.VMEM((PLANE, FEW, 2 * LANES), low),
        pltpu.VMEM((PLANE, experts, 2 * LANES), low),
        pltpu.VMEM((PLANE, 1, LANES), full),
        pltpu.VMEM((1, 1, LANES), full),
        pltpu.VMEM((NZ, CAP, 2 * LANES), low),
        pltpu.VMEM((NZ, CAP, 2 * LANES), low),
        pltpu.VMEM((NZ, 1, PAIRS + LANES), full),
        pltpu.VMEM((NZ, 1, PAIRS + LANES), full),
        pltpu.VMEM((PLANE, experts, 2 * LANES), low),
        pltpu.VMEM((PLANE, FEW, 2 * LANES), low),
        pltpu.VMEM((PLANE, FEW, 2 * LANES), low),
        pltpu.VMEM((FEW, width), low),
        pltpu.VMEM((PLANE, FEW, LANES), low),
        pltpu.VMEM((PLANE, experts, LANES), low),
        pltpu.VMEM((NZ, CAP, LANES), low),
        pltpu.VMEM((NZ, CAP, LANES), low),
        pltpu.VMEM((PLANE, experts, LANES), low),
        pltpu.VMEM((PLANE, FEW, LANES), low),
        pltpu.VMEM((FEW, width), low),
        pltpu.VMEM((NZ, CAP, PAIRS), low),
        pltpu.VMEM((NZ, CAP, PAIRS), low),
        pltpu.VMEM((PLANE, FEW, experts), low),
        pltpu.VMEM((PLANE, FEW, experts), low),
        pltpu.VMEM((held, FEW), low),
        pltpu.VMEM((8, LANES), full),
        pltpu.VMEM((8, LANES), full),
    ]

    def sems(chunks, swaps):
        return [
            dma((6,)), dma, dma((3,)), dma, dma((chunks,)), dma, dma((chunks,)),
            dma, dma, dma((swaps,)), dma((swaps,)),
        ]

    def call(body, results, scratch, number):
        return pl.pallas_call(
            body,
            out_shape=tuple(results),
            in_specs=[smem, hbm, hbm, hbm, vmem, vmem, hbm, hbm],
            out_specs=(vmem,) * 4 + (smem,) * (len(results) - 4),
            scratch_shapes=scratch,
            compiler_params=pltpu.CompilerParams(
                collective_id=number, has_side_effects=True, vmem_limit_bytes=50 << 20
            ),
        )(*operands)

    def store(*results):
        return pl.pallas_call(
            write_out,
            out_shape=tuple(jax.ShapeDtypeStruct(shape, dtype) for shape, dtype in outs),
            in_specs=[vmem] * 4,
            out_specs=(anywhere,) * 4,
            scratch_shapes=[dma((4,))],
            compiler_params=pltpu.CompilerParams(vmem_limit_bytes=1 << 20),
        )(*(pltpu.with_memory_space_constraint(r, pltpu.VMEM) for r in results))

    *results, flag = call(
        lean_kernel,
        kept + (jax.ShapeDtypeStruct((1, 1), full),),
        small + shared(slots - 1, (slots - 1) * experts + FEW, PARTS, [pltpu.VMEM(shape, kind) for shape in ((width, half), (half, width)) for kind in (low, low, full)]) + thirds + sems(PARTS, 3) + [dma((6,)), dma((6,)), dma((2,)), dma((2,))],
        0,
    )

    def padded(*unused):
        return store(*call(padded_kernel, kept, small + shared(slots, total, CHUNKS, [pltpu.VMEM(shape, full) for shape in ((width, half), (half, width)) for _ in range(2)]) + sems(CHUNKS, 2), 1))

    d_tokens, d_gate, d_up, d_down = lax.cond(flag[0, 0] > 0.5, padded, store, *results)
    return d_tokens[None], d_gate.T[None, None], d_up[None], d_down[None]


def solution(mesh):
    in_specs = (
        P("dp", "expert", None),
        P("dp", "expert", None),
        P("dp", "expert", None, None),
        P("dp", "expert", None, None),
        P("dp", "expert", None),
        P("expert", None, "dp"),
        P("expert", "dp", None),
    )
    out_specs = (
        P("dp", "expert", None),
        P("dp", "expert", None, None),
        P("expert", None, "dp"),
        P("expert", "dp", None),
    )
    return jax.shard_map(
        per_device, mesh=mesh, in_specs=in_specs, out_specs=out_specs, check_vma=False
    )
```
